256 devices in a mesh: ctx: 128 (over x_hi, z, y, core), tp: 2 (over x_lo).
Axes of the slice: x: 4 (x_hi: 2, x_lo: 2; x = x_hi * 2 + x_lo), y: 4, z: 8, core: 2. Of those that a mesh axis runs over, the one named last changes fastest.
Arguments:
- query: bfloat16 [32768, 2048], P('ctx', 'tp'), may hold values from -6 to 6
- key_in: bfloat16 [32768, 2048], P('ctx', 'tp'), may hold values from -6 to 6
- value: bfloat16 [32768, 2048], P('ctx', 'tp'), may hold values from -6 to 6
- grad_out: bfloat16 [32768, 2048], P('ctx', 'tp'), may hold values from -6 to 6
- residue: float32 [16, 2048], P(None, 'tp'), may hold values from -0.125 to 0.125
- rate: float32 [16, 2048], P(None, 'tp'), may hold values from 0.5 to 1024
Outputs:
- grad_query: bfloat16 [32768, 2048], P('ctx', 'tp')
- grad_key: bfloat16 [32768, 2048], P('ctx', 'tp')
- grad_value: bfloat16 [32768, 2048], P('ctx', 'tp')
- grad_residue: float32 [16, 2048], P(None, 'tp')
- grad_rate: float32 [16, 2048], P(None, 'tp')
The draws below stay inside these ranges and needn't reach their ends.
All inputs are finite; a program needn't handle non-finite values.
Results may differ from the reference program's by a relative error of at most 0.0058.
Values may be sent and summed in bfloat16 or wider, within the bound.
A program may use at most 320 MiB of HBM per device.

```python
import math
import jax
import jax.numpy as jnp
from jax import lax

D = 2048
ORDER = 16
SEQ = 32768


def block_scale(stream_key, shape, cuts, low, top_value):
    loudness, own = 1.0, jax.random.fold_in(stream_key, 6)
    for position, shards_of in cuts:
        steps = jnp.exp(jax.random.uniform(jax.random.fold_in(own, position), (shards_of,), jnp.float32, low / len(cuts), top_value / len(cuts)))
        loudness = loudness * jnp.repeat(steps, shape[position] // shards_of).reshape([-1 if axis == position else 1 for axis in range(len(shape))])
    return loudness


def normal_values(rng, shape, deviation, bound, shards=(), held_as=jnp.bfloat16):
    drawn = jax.random.normal(rng, shape, jnp.float32) * deviation
    if len(shards) > 0:
        drawn = block_scale(rng, shape, shards, -0.22, 0.18) * drawn
    return jnp.clip(drawn, min=-bound, max=bound).astype(held_as)


def setup_inputs(seed: int = 0) -> dict:
    arg_keys = jax.random.split(jax.random.key(seed), 7)
    query = normal_values(arg_keys[0], (SEQ, D), 1.0, 6.0, ((0, 128), (1, 2)))
    key_in = normal_values(arg_keys[1], (SEQ, D), 1.0, 6.0, ((0, 128), (1, 2)))
    value = normal_values(arg_keys[2], (SEQ, D), 1.0, 6.0, ((0, 128), (1, 2)))
    grad_out = normal_values(arg_keys[3], (SEQ, D), 1.0, 6.0, ((0, 128), (1, 2)))
    residue = normal_values(arg_keys[4], (ORDER, D), 0.02, 0.125, ((1, 2),), jnp.float32)
    rate = jnp.clip(jnp.exp(math.log(1024.0) - 7.624619 * jax.random.uniform(arg_keys[5], (ORDER, D), jnp.float32) ** block_scale(arg_keys[5], (ORDER, D), ((1, 2),), -0.2, 0.2)), 0.5, 1024.0)
    return dict(query=query, key_in=key_in, value=value, grad_out=grad_out, residue=residue, rate=rate)


def channel_block(items):
    gated, grad_conv, res_b, rate_b = items
    length = gated.shape[0]
    size = 2 * length
    steps = jnp.arange(length, dtype=jnp.float32)[:, None]
    filt = jnp.zeros(gated.shape, jnp.float32)
    for mode in range(res_b.shape[0]):
        filt = filt + res_b[mode][None, :] * jnp.exp(-rate_b[mode][None, :] * steps / SEQ)
    gated_f = gated.astype(jnp.float32)
    grad_f = grad_conv.astype(jnp.float32)
    spec_u = jnp.fft.rfft(gated_f, n=size, axis=0)
    spec_g = jnp.fft.rfft(grad_f, n=size, axis=0)
    spec_h = jnp.fft.rfft(filt, n=size, axis=0)
    conv = jnp.fft.irfft(spec_h * spec_u, n=size, axis=0)[:length]
    grad_gated = jnp.fft.irfft(jnp.conj(spec_h) * spec_g, n=size, axis=0)[:length]
    grad_filter = jnp.fft.irfft(jnp.conj(spec_u) * spec_g, n=size, axis=0)[:length]
    res_rows = []
    rate_rows = []
    for mode in range(res_b.shape[0]):
        weight = jnp.exp(-rate_b[mode][None, :] * steps / SEQ)
        res_rows.append(jnp.sum(grad_filter * weight, axis=0))
        rate_rows.append(-res_b[mode] * jnp.sum(grad_filter * weight * steps / SEQ, axis=0))
    scale = SEQ ** -0.5
    return (conv.astype(jnp.bfloat16), grad_gated.astype(jnp.bfloat16),
            scale * jnp.stack(res_rows), scale * jnp.stack(rate_rows))


def reference(query, key_in, value, grad_out, residue, rate):
    gated = (key_in.astype(jnp.float32) * value.astype(jnp.float32)).astype(jnp.bfloat16)
    grad_conv = (grad_out.astype(jnp.float32) * query.astype(jnp.float32)).astype(jnp.bfloat16)
    width = min(128, D)
    count = D // width
    modes = residue.shape[0]

    def split(arr, rows):
        return arr.reshape(rows, count, width).transpose(1, 0, 2)

    def join(arr, rows):
        return arr.transpose(1, 0, 2).reshape(rows, D)

    conv, grad_gated, grad_residue, grad_rate = lax.map(
        channel_block, (split(gated, SEQ), split(grad_conv, SEQ), split(residue, modes), split(rate, modes)))
    conv = join(conv, SEQ).astype(jnp.float32)
    grad_gated = join(grad_gated, SEQ).astype(jnp.float32)
    grad_query = (grad_out.astype(jnp.float32) * conv).astype(jnp.bfloat16)
    grad_key = (grad_gated * value.astype(jnp.float32)).astype(jnp.bfloat16)
    grad_value = (grad_gated * key_in.astype(jnp.float32)).astype(jnp.bfloat16)
    return grad_query, grad_key, grad_value, join(grad_residue, modes), join(grad_rate, modes)
```

```python
import jax
import jax.numpy as jnp
from jax import lax
from jax.experimental import pallas as pl
from jax.experimental.pallas import tpu as pltpu
from jax.sharding import PartitionSpec as P

SEQ = 32768
MODES = 16
ROWS = 256
SUB = 16
NSUB = ROWS // SUB
LANES = 128
TILE = 256
INNER = 8
OUTER = 16
F32 = jnp.float32
BF16 = jnp.bfloat16


def rows_iota(shape, dim):
    return lax.broadcasted_iota(jnp.int32, shape, dim)


def dot(a, b):
    return jnp.dot(a, b, preferred_element_type=F32)


def gate(a_ref, b_ref):
    return (a_ref[...].astype(F32) * b_ref[...].astype(F32)).astype(BF16)


def state_kernel(q_ref, k_ref, v_ref, go_ref, rate_ref, sub_s_ref, sub_b_ref, send_ref, ptab, btab, uf, gf):
    u = gate(k_ref, v_ref)
    g = gate(go_ref, q_ref)
    for half in range(TILE // LANES):
        cols = slice(half * LANES, (half + 1) * LANES)
        uf[half] = u[:, cols].astype(F32)
        gf[half] = g[:, cols].astype(F32)
    lam = rate_ref[...] * (1.0 / SEQ)
    pos = rows_iota((SUB, TILE), 0).astype(F32)
    for m in range(MODES):
        row = lam[m : m + 1, :]
        ptab[m] = jnp.exp(-row * (SUB - 1.0 - pos)).astype(BF16)
        btab[m] = jnp.exp(-row * (pos + 1.0)).astype(BF16)
    out_row = rows_iota((2 * MODES, MODES * SUB), 0)
    in_row = rows_iota((2 * MODES, MODES * SUB), 1)
    hit = (in_row // SUB) == (out_row % MODES)
    off = (in_row % SUB).astype(F32)
    first = out_row < MODES
    sel_s = jnp.where(hit, jnp.where(first, 1.0, SUB - 1.0 - off), 0.0).astype(BF16)
    sel_b = jnp.where(hit, jnp.where(first, 1.0, off + 1.0), 0.0).astype(BF16)
    step = jnp.exp(-lam * SUB)
    zero = jnp.zeros((MODES, TILE), F32)
    s, q, bn, tn, gr, gw = zero, zero, zero, zero, zero, zero
    decay = jnp.ones((MODES, TILE), F32)
    for k in range(NSUB):
        uk = u[k * SUB : (k + 1) * SUB, :]
        gk = g[k * SUB : (k + 1) * SUB, :]
        su = dot(sel_s, (ptab[...] * uk[None]).reshape(MODES * SUB, TILE))
        sg = dot(sel_b, (btab[...] * gk[None]).reshape(MODES * SUB, TILE))
        s_k, m_k = su[:MODES], su[MODES:]
        b_k, t_k = sg[:MODES], sg[MODES:]
        sub_s_ref[k] = s_k.astype(BF16)
        sub_b_ref[k] = b_k.astype(BF16)
        gr = gr + b_k * s
        gw = gw + t_k * s + b_k * q
        q = step * (q + float(SUB) * s) + m_k
        s = step * s + s_k
        db = decay * b_k
        bn = bn + db
        tn = tn + decay * t_k + float(k * SUB) * db
        decay = decay * step
    halves = []
    for half in range(TILE // LANES):
        acc = [jnp.zeros((8, LANES), F32) for _ in range(SUB)]
        for octet in range(NSUB // 8):
            us = [uf[half, pl.ds(octet * 8 * SUB + b, 8, stride=SUB), :] for b in range(SUB)]
            for b in range(SUB):
                gb = gf[half, pl.ds(octet * 8 * SUB + b, 8, stride=SUB), :]
                for lag in range(b + 1):
                    acc[lag] = acc[lag] + gb * us[b - lag]
        halves.append([jnp.sum(a, axis=0, keepdims=True) for a in acc])
    unit = jnp.exp(-lam)
    power = jnp.ones((MODES, TILE), F32)
    for lag in range(SUB):
        row = jnp.concatenate([h[lag] for h in halves], axis=1)
        term = row * power
        gr = gr + term
        gw = gw + float(lag) * term
        power = power * unit
    for half in range(TILE // LANES):
        cols = slice(half * LANES, (half + 1) * LANES)
        for n, part in enumerate((s, q, bn, tn, gr, gw)):
            send_ref[half, n * MODES : (n + 1) * MODES, :] = part[:, cols].astype(BF16)


def exchange_kernel(
    send_a, rate_ref, out_ref,
    recv_a, send_b, recv_b, send_d, recv_d, send_c, recv_c, pre_s, pre_b,
    sa, ra, sb, rb, sd, rd, sc, rc,
):
    me = lax.axis_index("ctx")
    grp = me // INNER
    idx = me % INNER
    inner = [(idx + d) % INNER for d in range(1, INNER)]
    outer = [(grp + d) % OUTER for d in range(1, OUTER)]

    def to_inner(j):
        return {"ctx": grp * INNER + j}

    def to_outer(p):
        return {"ctx": p * INNER + idx}

    barrier = pltpu.get_barrier_semaphore()
    for j in inner:
        pl.semaphore_signal(barrier, inc=1, device_id=to_inner(j), device_id_type=pl.DeviceIdType.MESH)
    for p in outer:
        pl.semaphore_signal(barrier, inc=1, device_id=to_outer(p), device_id_type=pl.DeviceIdType.MESH)
    pl.semaphore_wait(barrier, INNER + OUTER - 2)

    def trade(src, dst, ssem, rsem, own, others, target):
        for j in others:
            pltpu.make_async_remote_copy(
                src_ref=src.at[j], dst_ref=dst.at[own], send_sem=ssem.at[j], recv_sem=rsem.at[own],
                device_id=target(j), device_id_type=pl.DeviceIdType.MESH,
            ).start()
        dst[own] = src[own]
        for j in others:
            cp = pltpu.make_async_remote_copy(
                src_ref=src.at[j], dst_ref=dst.at[j], send_sem=ssem.at[j], recv_sem=rsem.at[j],
                device_id=target(j), device_id_type=pl.DeviceIdType.MESH,
            )
            cp.wait_recv()

    def drain(src, dst, ssem, rsem, others, target):
        for j in others:
            pltpu.make_async_remote_copy(
                src_ref=src.at[j], dst_ref=dst.at[j], send_sem=ssem.at[j], recv_sem=rsem.at[j],
                device_id=target(j), device_id_type=pl.DeviceIdType.MESH,
            ).wait_send()

    trade(send_a, recv_a, sa, ra, idx, inner, to_inner)
    cols = pl.ds(pl.multiple_of(idx * LANES, LANES), LANES)
    lam = rate_ref[:, cols] * (1.0 / SEQ)
    dec = jnp.exp(-lam * float(ROWS))
    zero = jnp.zeros((MODES, LANES), F32)
    s, q, gr, gw, bn, tn = zero, zero, zero, zero, zero, zero
    front = jnp.ones((MODES, LANES), F32)
    nears = []
    for j in range(INNER):
        part = [recv_a[j, n * MODES : (n + 1) * MODES, :].astype(F32) for n in range(6)]
        s_j, m_j, b_j, t_j, gr_j, gw_j = part
        pre_s[j] = s
        nears.append(b_j)
        gr = gr + gr_j + b_j * s
        gw = gw + gw_j + t_j * s + b_j * q
        q = dec * (q + float(ROWS) * s) + m_j
        s = dec * s + s_j
        db = front * b_j
        bn = bn + db
        tn = tn + front * t_j + float(ROWS * j) * db
        front = front * dec
    back = zero
    for j in reversed(range(INNER)):
        pre_b[j] = back
        back = dec * back + nears[j]
    for n, part in enumerate((s, q, bn, tn, gr, gw)):
        send_b[:, n, :] = part

    trade(send_b, recv_b, sb, rb, grp, outer, to_outer)
    mine = rows_iota((MODES, LANES), 0) == grp
    lam_row = jnp.sum(jnp.where(mine, lam, 0.0), axis=0, keepdims=True)
    span = float(ROWS * INNER)
    dec_g = jnp.exp(-lam_row * span)
    zrow = jnp.zeros((1, LANES), F32)
    s, q, gr, gw, back = zrow, zrow, zrow, zrow, zrow
    for p in range(OUTER):
        s_p, m_p, b_p, t_p, gr_p, gw_p = [recv_b[p, n : n + 1, :] for n in range(6)]
        send_d[p, 0:1, :] = s
        gr = gr + gr_p + b_p * s
        gw = gw + gw_p + t_p * s + b_p * q
        q = dec_g * (q + span * s) + m_p
        s = dec_g * s + s_p
    for p in reversed(range(OUTER)):
        send_d[p, 1:2, :] = back
        send_d[p, 2:3, :] = gr
        send_d[p, 3:4, :] = gw
        back = dec_g * back + recv_b[p, 2:3, :]

    trade(send_d, recv_d, sd, rd, grp, outer, to_outer)
    state, back, gr, gw = [recv_d[:, n, :] for n in range(4)]
    decs = [jnp.ones((MODES, LANES), F32)]
    for j in range(1, INNER):
        decs.append(decs[-1] * dec)
    for j in range(INNER):
        parts = (pre_s[j] + decs[j] * state, pre_b[j] + decs[INNER - 1 - j] * back, gr, gw)
        for n, part in enumerate(parts):
            send_c[j, n * MODES : (n + 1) * MODES, :] = part.astype(BF16)

    trade(send_c, recv_c, sc, rc, idx, inner, to_inner)
    out_ref[...] = recv_c[...]
    drain(send_a, recv_a, sa, ra, inner, to_inner)
    drain(send_b, recv_b, sb, rb, outer, to_outer)
    drain(send_d, recv_d, sd, rd, outer, to_outer)
    drain(send_c, recv_c, sc, rc, inner, to_inner)


def finish_kernel(
    q_ref, k_ref, v_ref, go_ref, res_ref, rate_ref, sub_s_ref, sub_b_ref, in_ref,
    gq_ref, gk_ref, gv_ref, gres_ref, grate_ref, wtab, vtab, htab,
):
    u = gate(k_ref, v_ref)
    g = gate(go_ref, q_ref)
    lam = rate_ref[...] * (1.0 / SEQ)
    res = res_ref[...]

    def incoming(n):
        return jnp.concatenate(
            [in_ref[h, n * MODES : (n + 1) * MODES, :].astype(F32) for h in range(TILE // LANES)], axis=1
        )

    scale = SEQ ** -0.5
    gres_ref[...] = scale * incoming(2)
    grate_ref[...] = (-scale / SEQ) * res * incoming(3)
    unit = jnp.exp(-lam)
    power = res
    for b in range(SUB):
        htab[b] = jnp.broadcast_to(jnp.sum(power, axis=0, keepdims=True), (SUB, TILE)).astype(BF16)
        vtab[SUB - 1 - b] = power.astype(BF16)
        power = power * unit
        wtab[b] = power.astype(BF16)
    step = jnp.exp(-lam * SUB)
    state = incoming(0)
    states = []
    for k in range(NSUB):
        states.append(state.astype(BF16))
        state = step * state + sub_s_ref[k].astype(F32)
    back = incoming(1)
    backs = [None] * NSUB
    for k in reversed(range(NSUB)):
        backs[k] = back.astype(BF16)
        back = step * back + sub_b_ref[k].astype(F32)
    out_row = rows_iota((SUB, SUB * SUB), 0)
    in_row = rows_iota((SUB, SUB * SUB), 1)
    major, minor = in_row // SUB, in_row % SUB
    pick = (major == out_row).astype(F32).astype(BF16)
    down = (major + minor == out_row).astype(F32).astype(BF16)
    up = (minor - major == out_row).astype(F32).astype(BF16)
    for k in range(NSUB):
        rows = slice(k * SUB, (k + 1) * SUB)

        def spread(tab, val):
            return (tab[...] * val[None]).reshape(SUB * SUB, TILE)

        conv = dot(pick, spread(wtab, states[k])) + dot(down, spread(htab, u[rows]))
        grad = dot(pick, spread(vtab, backs[k])) + dot(up, spread(htab, g[rows]))
        gq_ref[rows, :] = (go_ref[rows, :].astype(F32) * conv).astype(BF16)
        gk_ref[rows, :] = (v_ref[rows, :].astype(F32) * grad).astype(BF16)
        gv_ref[rows, :] = (k_ref[rows, :].astype(F32) * grad).astype(BF16)


def local(query, key_in, value, grad_out, residue, rate):
    rows, chans = query.shape
    tiles = chans // TILE
    per = TILE // LANES
    big = pl.BlockSpec((ROWS, TILE), lambda i: (0, i))
    small = pl.BlockSpec((MODES, TILE), lambda i: (0, i))
    subs = pl.BlockSpec((NSUB, MODES, TILE), lambda i: (0, 0, i))
    vmem = pl.BlockSpec(memory_space=pltpu.VMEM)
    sub_s, sub_b, summary = pl.pallas_call(
        state_kernel,
        grid=(tiles,),
        out_shape=(
            jax.ShapeDtypeStruct((NSUB, MODES, chans), BF16),
            jax.ShapeDtypeStruct((NSUB, MODES, chans), BF16),
            jax.ShapeDtypeStruct((INNER, 6 * MODES, LANES), BF16),
        ),
        in_specs=[big, big, big, big, small],
        out_specs=[subs, subs, pl.BlockSpec((per, 6 * MODES, LANES), lambda i: (i, 0, 0))],
        scratch_shapes=[
            pltpu.VMEM((MODES, SUB, TILE), BF16),
            pltpu.VMEM((MODES, SUB, TILE), BF16),
            pltpu.VMEM((per, ROWS, LANES), F32),
            pltpu.VMEM((per, ROWS, LANES), F32),
        ],
        compiler_params=pltpu.CompilerParams(vmem_limit_bytes=32 * 2**20),
        name="states",
    )(query, key_in, value, grad_out, rate)

    dma = pltpu.SemaphoreType.DMA
    incoming = pl.pallas_call(
        exchange_kernel,
        out_shape=jax.ShapeDtypeStruct((INNER, 4 * MODES, LANES), BF16),
        in_specs=[vmem, vmem],
        out_specs=vmem,
        scratch_shapes=[
            pltpu.VMEM((INNER, 6 * MODES, LANES), BF16),
            pltpu.VMEM((OUTER, 8, LANES), F32),
            pltpu.VMEM((OUTER, 8, LANES), F32),
            pltpu.VMEM((OUTER, 8, LANES), F32),
            pltpu.VMEM((OUTER, 8, LANES), F32),
            pltpu.VMEM((INNER, 4 * MODES, LANES), BF16),
            pltpu.VMEM((INNER, 4 * MODES, LANES), BF16),
            pltpu.VMEM((INNER, MODES, LANES), F32),
            pltpu.VMEM((INNER, MODES, LANES), F32),
            dma((INNER,)), dma((INNER,)), dma((OUTER,)), dma((OUTER,)),
            dma((OUTER,)), dma((OUTER,)), dma((INNER,)), dma((INNER,)),
        ],
        compiler_params=pltpu.CompilerParams(collective_id=0, has_side_effects=True, vmem_limit_bytes=16 * 2**20),
        name="exchange",
    )(summary, rate)

    return pl.pallas_call(
        finish_kernel,
        grid=(tiles,),
        out_shape=(
            jax.ShapeDtypeStruct((rows, chans), BF16),
            jax.ShapeDtypeStruct((rows, chans), BF16),
            jax.ShapeDtypeStruct((rows, chans), BF16),
            jax.ShapeDtypeStruct((MODES, chans), F32),
            jax.ShapeDtypeStruct((MODES, chans), F32),
        ),
        in_specs=[big, big, big, big, small, small, subs, subs,
                  pl.BlockSpec((per, 4 * MODES, LANES), lambda i: (i, 0, 0))],
        out_specs=[big, big, big, small, small],
        scratch_shapes=[
            pltpu.VMEM((SUB, MODES, TILE), BF16),
            pltpu.VMEM((SUB, MODES, TILE), BF16),
            pltpu.VMEM((SUB, SUB, TILE), BF16),
        ],
        compiler_params=pltpu.CompilerParams(vmem_limit_bytes=32 * 2**20),
        name="finish",
    )(query, key_in, value, grad_out, residue, rate, sub_s, sub_b, incoming)


def solution(mesh):
    big, small = P("ctx", "tp"), P(None, "tp")
    return jax.shard_map(
        local, mesh=mesh, in_specs=(big, big, big, big, small, small),
        out_specs=(big, big, big, small, small), check_vma=False,
    )
```

```python
import jax
import jax.numpy as jnp
from jax import lax
from jax.experimental import pallas as pl
from jax.experimental.pallas import tpu as pltpu
from jax.sharding import PartitionSpec as P

SEQ = 32768
MODES = 16
ROWS = 256
CHANS = 1024
SUB = 16
NSUB = ROWS // SUB
MID = 8
LANES = 128
TILE = 256
TILES = CHANS // TILE
HALVES = TILE // LANES
INNER = 8
OUTER = 16
VMEM_LIMIT = 63 * 2**20
F32 = jnp.float32
BF16 = jnp.bfloat16
MESH = pl.DeviceIdType.MESH


def iota(shape, dim):
    return lax.broadcasted_iota(jnp.int32, shape, dim)


def dot(a, b):
    return jnp.dot(a, b, preferred_element_type=F32)


def columns(t):
    return pl.ds(pl.multiple_of(t * TILE, TILE), TILE)


def spread(tab, val):
    return (tab * val[None]).reshape(tab.shape[0] * tab.shape[1], TILE)


def state_tables(t, rate, ptab, btab):
    cols = columns(t)
    pos = iota((SUB, TILE), 0).astype(F32)
    lam = rate[:, cols] * (1.0 / SEQ)
    for m in range(MODES):
        row = lam[m : m + 1, :]
        ptab[m, :, cols] = jnp.exp(-row * (SUB - 1.0 - pos)).astype(BF16)
        btab[m, :, cols] = jnp.exp(-row * (pos + 1.0)).astype(BF16)


def states(t, rate, u_ref, g_ref, ptab, btab, uf, gf, sub_s, sub_b, send_a):
    cols = columns(t)
    lam = rate[:, cols] * (1.0 / SEQ)
    out_row = iota((2 * MODES, MODES * SUB), 0)
    in_row = iota((2 * MODES, MODES * SUB), 1)
    hit = (in_row // SUB) == (out_row % MODES)
    off = (in_row % SUB).astype(F32)
    first = out_row < MODES
    sel_s = jnp.where(hit, jnp.where(first, 1.0, SUB - 1.0 - off), 0.0).astype(BF16)
    sel_b = jnp.where(hit, jnp.where(first, 1.0, off + 1.0), 0.0).astype(BF16)
    step = jnp.exp(-lam * SUB)
    zero = jnp.zeros((MODES, TILE), F32)
    s, q, bn, tn, gr, gw = zero, zero, zero, zero, zero, zero
    decay = jnp.ones((MODES, TILE), F32)
    for k in range(NSUB):
        rows = slice(k * SUB, (k + 1) * SUB)
        su = dot(sel_s, spread(ptab[:, :, cols], u_ref[rows, cols]))
        sg = dot(sel_b, spread(btab[:, :, cols], g_ref[rows, cols]))
        s_k, m_k = su[:MODES], su[MODES:]
        b_k, t_k = sg[:MODES], sg[MODES:]
        sub_s[k, :, cols] = s_k
        sub_b[k, :, cols] = b_k
        gr = gr + b_k * s
        gw = gw + t_k * s + b_k * q
        q = step * (q + float(SUB) * s) + m_k
        s = step * s + s_k
        db = decay * b_k
        bn = bn + db
        tn = tn + decay * t_k + float(k * SUB) * db
        decay = decay * step
    halves = []
    for half in range(HALVES):
        acc = [jnp.zeros((8, LANES), F32) for _ in range(SUB)]
        for octet in range(NSUB // 8):
            us = [uf[half, pl.ds(octet * 8 * SUB + b, 8, stride=SUB), :] for b in range(SUB)]
            for b in range(SUB):
                gb = gf[half, pl.ds(octet * 8 * SUB + b, 8, stride=SUB), :]
                for lag in range(b + 1):
                    acc[lag] = acc[lag] + gb * us[b - lag]
        halves.append([jnp.sum(a, axis=0, keepdims=True) for a in acc])
    unit = jnp.exp(-lam)
    power = jnp.ones((MODES, TILE), F32)
    for lag in range(SUB):
        term = jnp.concatenate([h[lag] for h in halves], axis=1) * power
        gr = gr + term
        gw = gw + float(lag) * term
        power = power * unit
    for half in range(HALVES):
        part_cols = slice(half * LANES, (half + 1) * LANES)
        for n, part in enumerate((s, q, bn, tn, gr, gw)):
            send_a[t * HALVES + half, n * MODES : (n + 1) * MODES, :] = part[:, part_cols].astype(BF16)


def near_part(t, rate, res, u_ref, g_ref, wtab, vtab, htab, near_c, near_g):
    cols = columns(t)
    lam = rate[:, cols] * (1.0 / SEQ)
    unit = jnp.exp(-lam)
    power = res[:, cols]
    mid = power * jnp.exp(-lam * float(MID))
    for b in range(SUB):
        htab[b] = jnp.broadcast_to(jnp.sum(power, axis=0, keepdims=True), (SUB, TILE)).astype(BF16)
        vtab[SUB - 1 - b, :, cols] = (power - mid).astype(BF16)
        power = power * unit
        wtab[b, :, cols] = (power - mid).astype(BF16)
    out_row = iota((SUB, SUB * SUB), 0)
    in_row = iota((SUB, SUB * SUB), 1)
    lag, pos = in_row // SUB, in_row % SUB
    down = jnp.where(pos + lag == out_row, 1.0, 0.0).astype(BF16)
    up = jnp.where(pos - lag == out_row, 1.0, 0.0).astype(BF16)
    for k in range(NSUB):
        rows = slice(k * SUB, (k + 1) * SUB)
        near_c[rows, cols] = dot(down, spread(htab[...], u_ref[rows, cols]))
        near_g[rows, cols] = dot(up, spread(htab[...], g_ref[rows, cols]))


def far_part(t, rate, res, k_in, v_in, go_in, wtab, vtab, sub_s, sub_b, near_c, near_g, recv_c, gq, gk, gv):
    cols = columns(t)
    lam = rate[:, cols] * (1.0 / SEQ)
    step = jnp.exp(-lam * SUB)
    mid = res[:, cols] * jnp.exp(-lam * float(MID))

    def incoming(n):
        parts = [recv_c[t * HALVES + h, n * MODES : (n + 1) * MODES, :] for h in range(HALVES)]
        return jnp.concatenate(parts, axis=1)

    out_row = iota((SUB, SUB * MODES), 0)
    in_row = iota((SUB, SUB * MODES), 1)
    pick = jnp.where(in_row // MODES == out_row, 1.0, 0.0).astype(BF16)

    def reach(tab, x):
        base = jnp.sum(mid * x, axis=0, keepdims=True)
        return dot(pick, spread(tab[:, :, cols], x.astype(BF16))) + base

    x = incoming(0)
    for k in range(NSUB):
        rows = slice(k * SUB, (k + 1) * SUB)
        conv = near_c[rows, cols] + reach(wtab, x)
        gq[rows, cols] = (go_in[rows, cols].astype(F32) * conv).astype(BF16)
        x = step * x + sub_s[k, :, cols]
    x = incoming(1)
    for k in reversed(range(NSUB)):
        rows = slice(k * SUB, (k + 1) * SUB)
        grad = near_g[rows, cols] + reach(vtab, x)
        gk[rows, cols] = (v_in[rows, cols].astype(F32) * grad).astype(BF16)
        gv[rows, cols] = (k_in[rows, cols].astype(F32) * grad).astype(BF16)
        x = step * x + sub_b[k, :, cols]


def main_kernel(
    q_hbm, k_hbm, v_hbm, go_hbm, res_hbm, rate_hbm,
    gq_hbm, gk_hbm, gv_hbm, gres_hbm, grate_hbm,
    gq, gk, gv, gres, grate, q_in, k_in, v_in, go_in, res, rate, u_ref, g_ref, uf, gf, ptab, btab, wtab, vtab, htab,
    sub_s, sub_b, near_c, near_g,
    send_a, recv_a, pre_s, pre_b, send_b, recv_b, send_m, recv_m, send_d, recv_d, send_c, recv_c, send_e, recv_e,
    in_sem, par_sem, out_sem, sa, ra, sb, rb, sm, rm, sd, rd, sc, rc, se, re,
):
    me = lax.axis_index("ctx")
    grp = me // INNER
    idx = me % INNER
    inner = [(idx + d) % INNER for d in (4, 5, 3, 2, 6, 7, 1)]
    outer = [(grp + d) % OUTER for d in (12, 4, 11, 13, 5, 3, 10, 6, 14, 2, 9, 7, 8, 15, 1)]

    def to_inner(j):
        return {"ctx": grp * INNER + j}

    def to_outer(p):
        return {"ctx": p * INNER + idx}

    pairs = ((q_hbm, q_in), (k_hbm, k_in), (v_hbm, v_in), (go_hbm, go_in))

    def load(t, n):
        src, dst = pairs[n]
        return pltpu.make_async_copy(src.at[:, columns(t)], dst.at[:, columns(t)], in_sem.at[t, n])

    params = (
        pltpu.make_async_copy(rate_hbm, rate, par_sem.at[0]),
        pltpu.make_async_copy(res_hbm, res, par_sem.at[1]),
    )
    for cp in params:
        cp.start()
    for t in range(TILES):
        for n in range(4):
            load(t, n).start()

    barrier = pltpu.get_barrier_semaphore()
    for j in inner:
        pl.semaphore_signal(barrier, inc=1, device_id=to_inner(j), device_id_type=MESH)
    for p in outer:
        pl.semaphore_signal(barrier, inc=1, device_id=to_outer(p), device_id_type=MESH)

    def remote(src, dst, ssem, rsem, target):
        return pltpu.make_async_remote_copy(
            src_ref=src, dst_ref=dst, send_sem=ssem, recv_sem=rsem, device_id=target, device_id_type=MESH
        )

    for cp in params:
        cp.wait()

    @pl.loop(0, TILES)
    def _(t):
        state_tables(t, rate, ptab, btab)

    @pl.loop(0, TILES)
    def _(t):
        cols = columns(t)
        for n in range(4):
            load(t, n).wait()
        u = (k_in[:, cols].astype(F32) * v_in[:, cols].astype(F32)).astype(BF16)
        g = (go_in[:, cols].astype(F32) * q_in[:, cols].astype(F32)).astype(BF16)
        u_ref[:, cols] = u
        g_ref[:, cols] = g
        for half in range(HALVES):
            part = slice(half * LANES, (half + 1) * LANES)
            uf[half] = u[:, part].astype(F32)
            gf[half] = g[:, part].astype(F32)
        states(t, rate, u_ref, g_ref, ptab, btab, uf, gf, sub_s, sub_b, send_a)

    pl.semaphore_wait(barrier, INNER + OUTER - 2)

    for j in inner:
        remote(send_a.at[j], recv_a.at[idx], sa.at[j], ra.at[idx], to_inner(j)).start()
    recv_a[idx] = send_a[idx]

    @pl.loop(0, TILES)
    def _(t):
        near_part(t, rate, res, u_ref, g_ref, wtab, vtab, htab, near_c, near_g)

    block = pl.ds(pl.multiple_of(idx * LANES, LANES), LANES)
    lam = rate[:, block] * (1.0 / SEQ)
    dec = jnp.exp(-lam * float(ROWS))
    span = float(ROWS * INNER)
    dec_g = jnp.exp(-lam * span)
    for j in inner:
        remote(send_a.at[j], recv_a.at[j], sa.at[j], ra.at[j], to_inner(j)).wait_recv()
    zero = jnp.zeros((MODES, LANES), F32)
    s, q, gr, gw, bn, tn = zero, zero, zero, zero, zero, zero
    front = jnp.ones((MODES, LANES), F32)
    nears = []
    for j in range(INNER):
        part = [recv_a[j, n * MODES : (n + 1) * MODES, :].astype(F32) for n in range(6)]
        s_j, m_j, b_j, t_j, gr_j, gw_j = part
        pre_s[j] = s
        nears.append(b_j)
        gr = gr + gr_j + b_j * s
        gw = gw + gw_j + t_j * s + b_j * q
        q = dec * (q + float(ROWS) * s) + m_j
        s = dec * s + s_j
        db = front * b_j
        bn = bn + db
        tn = tn + front * t_j + float(ROWS * j) * db
        front = front * dec
    for n, part in enumerate((s, q, bn, tn, gr, gw)):
        send_b[:, n, :] = part
    send_m[0] = bn
    send_m[1] = s

    for p in outer:
        remote(send_b.at[p], recv_b.at[grp], sb.at[p], rb.at[grp], to_outer(p)).start()
    for p in outer:
        pick = (p > grp).astype(jnp.int32)
        remote(send_m.at[pick], recv_m.at[grp], sm.at[p], rm.at[grp], to_outer(p)).start()
    recv_b[grp] = send_b[grp]
    recv_m[grp] = zero
    back = zero
    for j in reversed(range(INNER)):
        pre_b[j] = back
        back = dec * back + nears[j]
    decs = [jnp.ones((MODES, LANES), F32)]
    for j in range(1, INNER):
        decs.append(decs[-1] * dec)
    mine = iota((MODES, LANES), 0) == grp
    lam_row = jnp.sum(jnp.where(mine, lam, 0.0), axis=0, keepdims=True)
    dec_row = jnp.exp(-lam_row * span)

    for p in outer:
        remote(send_b.at[p], recv_b.at[p], sb.at[p], rb.at[p], to_outer(p)).wait_recv()
    zrow = jnp.zeros((1, LANES), F32)
    s, q, gr, gw = zrow, zrow, zrow, zrow
    for p in range(OUTER):
        s_p, m_p, b_p, t_p, gr_p, gw_p = [recv_b[p, n : n + 1, :] for n in range(6)]
        gr = gr + gr_p + b_p * s
        gw = gw + gw_p + t_p * s + b_p * q
        q = dec_row * (q + span * s) + m_p
        s = dec_row * s + s_p
    send_d[0:1, :] = gr
    send_d[1:2, :] = gw
    for p in outer:
        remote(send_d, recv_d.at[grp], sd.at[p], rd.at[grp], to_outer(p)).start()
    recv_d[grp] = send_d[...]

    for p in outer:
        remote(send_m.at[0], recv_m.at[p], sm.at[p], rm.at[p], to_outer(p)).wait_recv()
    state, back = zero, zero
    for p in range(OUTER):
        state = jnp.where(p < grp, dec_g * state + recv_m[p], state)
    for p in reversed(range(OUTER)):
        back = jnp.where(p > grp, dec_g * back + recv_m[p], back)

    for j in range(INNER):
        send_c[j, 0:MODES, :] = pre_s[j] + decs[j] * state
        send_c[j, MODES : 2 * MODES, :] = pre_b[j] + decs[INNER - 1 - j] * back
    for j in inner:
        remote(send_c.at[j], recv_c.at[idx], sc.at[j], rc.at[idx], to_inner(j)).start()
    recv_c[idx] = send_c[idx]

    for p in outer:
        remote(send_d, recv_d.at[p], sd.at[p], rd.at[p], to_outer(p)).wait_recv()
    send_e[0:MODES, :] = recv_d[:, 0, :].astype(BF16)
    send_e[MODES : 2 * MODES, :] = recv_d[:, 1, :].astype(BF16)
    for j in inner:
        remote(send_e, recv_e.at[idx], se.at[j], re.at[idx], to_inner(j)).start()
    recv_e[idx] = send_e[...]

    for j in inner:
        remote(send_c.at[j], recv_c.at[j], sc.at[j], rc.at[j], to_inner(j)).wait_recv()

    results = ((gq, gq_hbm), (gk, gk_hbm), (gv, gv_hbm))

    def store(t, n):
        src, dst = results[n]
        return pltpu.make_async_copy(src.at[:, columns(t)], dst.at[:, columns(t)], out_sem.at[t, n])

    @pl.loop(0, TILES)
    def _(t):
        far_part(t, rate, res, k_in, v_in, go_in, wtab, vtab, sub_s, sub_b, near_c, near_g, recv_c, gq, gk, gv)
        for n in range(3):
            store(t, n).start()

    for j in inner:
        remote(send_e, recv_e.at[j], se.at[j], re.at[j], to_inner(j)).wait_recv()
    scale = SEQ ** -0.5
    for j in range(INNER):
        cols = slice(j * LANES, (j + 1) * LANES)
        gres[:, cols] = scale * recv_e[j, 0:MODES, :].astype(F32)
        grate[:, cols] = (-scale / SEQ) * res[:, cols] * recv_e[j, MODES : 2 * MODES, :].astype(F32)

    sums = (
        pltpu.make_async_copy(gres, gres_hbm, par_sem.at[0]),
        pltpu.make_async_copy(grate, grate_hbm, par_sem.at[1]),
    )
    for cp in sums:
        cp.start()
    for j in inner:
        remote(send_a.at[j], recv_a.at[j], sa.at[j], ra.at[j], to_inner(j)).wait_send()
        remote(send_c.at[j], recv_c.at[j], sc.at[j], rc.at[j], to_inner(j)).wait_send()
        remote(send_e, recv_e.at[j], se.at[j], re.at[j], to_inner(j)).wait_send()
    for p in outer:
        remote(send_b.at[p], recv_b.at[p], sb.at[p], rb.at[p], to_outer(p)).wait_send()
        remote(send_m.at[0], recv_m.at[p], sm.at[p], rm.at[p], to_outer(p)).wait_send()
        remote(send_d, recv_d.at[p], sd.at[p], rd.at[p], to_outer(p)).wait_send()
    for t in range(TILES):
        for n in range(3):
            store(t, n).wait()
    for cp in sums:
        cp.wait()


def store_kernel(*refs):
    srcs, dsts, sem = refs[:5], refs[5:10], refs[10]
    copies = [pltpu.make_async_copy(s, d, sem.at[n]) for n, (s, d) in enumerate(zip(srcs, dsts))]
    for cp in copies:
        cp.start()
    for cp in copies:
        cp.wait()


def local(query, key_in, value, grad_out, residue, rate):
    hbm = pl.BlockSpec(memory_space=pltpu.HBM)
    big = jax.ShapeDtypeStruct((ROWS, CHANS), BF16)
    small = jax.ShapeDtypeStruct((MODES, CHANS), F32)
    dma = pltpu.SemaphoreType.DMA

    def buf(*shape, dtype=F32):
        return pltpu.VMEM(shape, dtype)

    results = pl.pallas_call(
        main_kernel,
        out_shape=(big, big, big, small, small),
        in_specs=[hbm] * 6,
        out_specs=[hbm] * 5,
        scratch_shapes=[
            *[buf(ROWS, CHANS, dtype=BF16)] * 3,
            *[buf(MODES, CHANS)] * 2,
            *[buf(ROWS, CHANS, dtype=BF16)] * 4,
            *[buf(MODES, CHANS)] * 2,
            *[buf(ROWS, CHANS, dtype=BF16)] * 2,
            *[buf(HALVES, ROWS, LANES)] * 2,
            *[buf(MODES, SUB, CHANS, dtype=BF16)] * 2,
            *[buf(SUB, MODES, CHANS, dtype=BF16)] * 2,
            buf(SUB, SUB, TILE, dtype=BF16),
            *[buf(NSUB, MODES, CHANS)] * 2,
            *[buf(ROWS, CHANS)] * 2,
            *[buf(INNER, 6 * MODES, LANES, dtype=BF16)] * 2,
            *[buf(INNER, MODES, LANES)] * 2,
            *[buf(OUTER, 8, LANES)] * 2,
            buf(2, MODES, LANES), buf(OUTER, MODES, LANES),
            buf(8, LANES), buf(OUTER, 8, LANES),
            *[buf(INNER, 2 * MODES, LANES)] * 2,
            buf(2 * MODES, LANES, dtype=BF16), buf(INNER, 2 * MODES, LANES, dtype=BF16),
            dma((TILES, 4)), dma((2,)), dma((TILES, 3)),
            dma((INNER,)), dma((INNER,)), dma((OUTER,)), dma((OUTER,)), dma((OUTER,)), dma((OUTER,)),
            dma((OUTER,)), dma((OUTER,)), dma((INNER,)), dma((INNER,)), dma((INNER,)), dma((INNER,)),
        ],
        compiler_params=pltpu.CompilerParams(collective_id=0, has_side_effects=True, vmem_limit_bytes=VMEM_LIMIT),
        name="hyena",
    )(query, key_in, value, grad_out, residue, rate)

    return pl.pallas_call(
        store_kernel,
        out_shape=(big, big, big, small, small),
        in_specs=[hbm] * 5,
        out_specs=[hbm] * 5,
        scratch_shapes=[dma((5,))],
        compiler_params=pltpu.CompilerParams(vmem_limit_bytes=VMEM_LIMIT),
        name="store",
    )(*results)


def solution(mesh):
    big, small = P("ctx", "tp"), P(None, "tp")
    return jax.shard_map(
        local, mesh=mesh, in_specs=(big, big, big, big, small, small),
        out_specs=(big, big, big, small, small), check_vma=False,
    )
```

```python
import jax
import jax.numpy as jnp
from jax import lax
from jax.experimental import pallas as pl
from jax.experimental.pallas import tpu as pltpu
from jax.sharding import PartitionSpec as P

SEQ = 32768
MODES = 16
ROWS = 256
CHANS = 1024
SUB = 16
NSUB = ROWS // SUB
MID = 8
LANES = 128
TILE = 256
TILES = CHANS // TILE
HALVES = TILE // LANES
INNER = 8
OUTER = 16
VMEM_LIMIT = 63 * 2**20
F32 = jnp.float32
BF16 = jnp.bfloat16
MESH = pl.DeviceIdType.MESH


def iota(shape, dim):
    return lax.broadcasted_iota(jnp.int32, shape, dim)


def dot(a, b):
    return jnp.dot(a, b, preferred_element_type=F32)


def columns(t):
    return pl.ds(pl.multiple_of(t * TILE, TILE), TILE)


def spread(tab, val):
    return (tab * val[None]).reshape(tab.shape[0] * tab.shape[1], TILE)


def state_tables(t, rate, ptab, btab):
    cols = columns(t)
    pos = iota((SUB, TILE), 0).astype(F32)
    lam = rate[:, cols] * (1.0 / SEQ)
    for m in range(MODES):
        row = lam[m : m + 1, :]
        ptab[m, :, cols] = jnp.exp(-row * (SUB - 1.0 - pos)).astype(BF16)
        btab[m, :, cols] = jnp.exp(-row * (pos + 1.0)).astype(BF16)


def states(t, rate, u_ref, g_ref, ptab, btab, uf, gf, sub_s, sub_b, send_a):
    cols = columns(t)
    lam = rate[:, cols] * (1.0 / SEQ)
    out_row = iota((2 * MODES, MODES * SUB), 0)
    in_row = iota((2 * MODES, MODES * SUB), 1)
    hit = (in_row // SUB) == (out_row % MODES)
    off = (in_row % SUB).astype(F32)
    first = out_row < MODES
    sel_s = jnp.where(hit, jnp.where(first, 1.0, SUB - 1.0 - off), 0.0).astype(BF16)
    sel_b = jnp.where(hit, jnp.where(first, 1.0, off + 1.0), 0.0).astype(BF16)
    step = jnp.exp(-lam * SUB)
    zero = jnp.zeros((MODES, TILE), F32)
    s, q, bn, tn, gr, gw = zero, zero, zero, zero, zero, zero
    decay = jnp.ones((MODES, TILE), F32)
    for k in range(NSUB):
        rows = slice(k * SUB, (k + 1) * SUB)
        su = dot(sel_s, spread(ptab[:, :, cols], u_ref[rows, cols]))
        sg = dot(sel_b, spread(btab[:, :, cols], g_ref[rows, cols]))
        s_k, m_k = su[:MODES], su[MODES:]
        b_k, t_k = sg[:MODES], sg[MODES:]
        sub_s[k, :, cols] = s_k
        sub_b[k, :, cols] = b_k
        gr = gr + b_k * s
        gw = gw + t_k * s + b_k * q
        q = step * (q + float(SUB) * s) + m_k
        s = step * s + s_k
        db = decay * b_k
        bn = bn + db
        tn = tn + decay * t_k + float(k * SUB) * db
        decay = decay * step
    halves = []
    for half in range(HALVES):
        acc = [jnp.zeros((8, LANES), F32) for _ in range(SUB)]
        for octet in range(NSUB // 8):
            us = [uf[half, pl.ds(octet * 8 * SUB + b, 8, stride=SUB), :] for b in range(SUB)]
            for b in range(SUB):
                gb = gf[half, pl.ds(octet * 8 * SUB + b, 8, stride=SUB), :]
                for lag in range(b + 1):
                    acc[lag] = acc[lag] + gb * us[b - lag]
        halves.append([jnp.sum(a, axis=0, keepdims=True) for a in acc])
    unit = jnp.exp(-lam)
    power = jnp.ones((MODES, TILE), F32)
    for lag in range(SUB):
        term = jnp.concatenate([h[lag] for h in halves], axis=1) * power
        gr = gr + term
        gw = gw + float(lag) * term
        power = power * unit
    for half in range(HALVES):
        part_cols = slice(half * LANES, (half + 1) * LANES)
        for n, part in enumerate((s, q, bn, tn, gr, gw)):
            send_a[t * HALVES + half, n * MODES : (n + 1) * MODES, :] = part[:, part_cols].astype(BF16)


def near_part(t, rate, res, u_ref, g_ref, wtab, vtab, htab, near_c, near_g):
    cols = columns(t)
    lam = rate[:, cols] * (1.0 / SEQ)
    unit = jnp.exp(-lam)
    power = res[:, cols]
    mid = power * jnp.exp(-lam * float(MID))
    for b in range(SUB):
        htab[b] = jnp.broadcast_to(jnp.sum(power, axis=0, keepdims=True), (SUB, TILE)).astype(BF16)
        vtab[SUB - 1 - b, :, cols] = (power - mid).astype(BF16)
        power = power * unit
        wtab[b, :, cols] = (power - mid).astype(BF16)
    out_row = iota((SUB, SUB * SUB), 0)
    in_row = iota((SUB, SUB * SUB), 1)
    lag, pos = in_row // SUB, in_row % SUB
    down = jnp.where(pos + lag == out_row, 1.0, 0.0).astype(BF16)
    up = jnp.where(pos - lag == out_row, 1.0, 0.0).astype(BF16)
    for k in range(NSUB):
        rows = slice(k * SUB, (k + 1) * SUB)
        near_c[rows, cols] = dot(down, spread(htab[...], u_ref[rows, cols]))
        near_g[rows, cols] = dot(up, spread(htab[...], g_ref[rows, cols]))


def far_part(t, rate, res, k_in, v_in, go_in, wtab, vtab, sub_s, sub_b, near_c, near_g, recv_c, gq, gk, gv):
    cols = columns(t)
    lam = rate[:, cols] * (1.0 / SEQ)
    step = jnp.exp(-lam * SUB)
    mid = res[:, cols] * jnp.exp(-lam * float(MID))

    def incoming(n):
        parts = [recv_c[t * HALVES + h, n * MODES : (n + 1) * MODES, :] for h in range(HALVES)]
        return jnp.concatenate(parts, axis=1)

    out_row = iota((SUB, SUB * MODES), 0)
    in_row = iota((SUB, SUB * MODES), 1)
    pick = jnp.where(in_row // MODES == out_row, 1.0, 0.0).astype(BF16)

    def reach(tab, x):
        base = jnp.sum(mid * x, axis=0, keepdims=True)
        return dot(pick, spread(tab[:, :, cols], x.astype(BF16))) + base

    x = incoming(0)
    for k in range(NSUB):
        rows = slice(k * SUB, (k + 1) * SUB)
        conv = near_c[rows, cols] + reach(wtab, x)
        gq[rows, cols] = (go_in[rows, cols].astype(F32) * conv).astype(BF16)
        x = step * x + sub_s[k, :, cols]
    x = incoming(1)
    for k in reversed(range(NSUB)):
        rows = slice(k * SUB, (k + 1) * SUB)
        grad = near_g[rows, cols] + reach(vtab, x)
        gk[rows, cols] = (v_in[rows, cols].astype(F32) * grad).astype(BF16)
        gv[rows, cols] = (k_in[rows, cols].astype(F32) * grad).astype(BF16)
        x = step * x + sub_b[k, :, cols]


def main_kernel(
    q_hbm, k_hbm, v_hbm, go_hbm, res_hbm, rate_hbm,
    gq_hbm, gk_hbm, gv_hbm, gres_hbm, grate_hbm,
    gq, gk, gv, gres, grate, q_in, k_in, v_in, go_in, res, rate, u_ref, g_ref, uf, gf, ptab, btab, wtab, vtab, htab,
    sub_s, sub_b, near_c, near_g,
    send_a, recv_a, pre_s, pre_b, send_b, recv_b, send_m, recv_m, send_d, recv_d, send_c, recv_c, send_e, recv_e,
    in_sem, par_sem, out_sem, sa, ra, sb, rb, sm, rm, sd, rd, sc, rc, se, re,
):
    me = lax.axis_index("ctx")
    grp = me // INNER
    idx = me % INNER
    inner = [(idx + d) % INNER for d in (4, 5, 3, 2, 6, 7, 1)]
    outer = [(grp + d) % OUTER for d in (12, 4, 11, 13, 5, 3, 10, 6, 14, 2, 9, 7, 8, 15, 1)]

    def to_inner(j):
        return {"ctx": grp * INNER + j}

    def to_outer(p):
        return {"ctx": p * INNER + idx}

    pairs = ((q_hbm, q_in), (k_hbm, k_in), (v_hbm, v_in), (go_hbm, go_in))

    def load(t, n):
        src, dst = pairs[n]
        return pltpu.make_async_copy(src.at[:, columns(t)], dst.at[:, columns(t)], in_sem.at[t, n])

    params = (
        pltpu.make_async_copy(rate_hbm, rate, par_sem.at[0]),
        pltpu.make_async_copy(res_hbm, res, par_sem.at[1]),
    )
    for cp in params:
        cp.start()
    for t in range(TILES):
        for n in range(4):
            load(t, n).start()

    barrier = pltpu.get_barrier_semaphore()
    for j in inner:
        pl.semaphore_signal(barrier, inc=1, device_id=to_inner(j), device_id_type=MESH)
    for p in outer:
        pl.semaphore_signal(barrier, inc=1, device_id=to_outer(p), device_id_type=MESH)

    def remote(src, dst, ssem, rsem, target):
        return pltpu.make_async_remote_copy(
            src_ref=src, dst_ref=dst, send_sem=ssem, recv_sem=rsem, device_id=target, device_id_type=MESH
        )

    for cp in params:
        cp.wait()

    @pl.loop(0, TILES)
    def _(t):
        state_tables(t, rate, ptab, btab)

    @pl.loop(0, TILES)
    def _(t):
        cols = columns(t)
        for n in range(4):
            load(t, n).wait()
        u = (k_in[:, cols].astype(F32) * v_in[:, cols].astype(F32)).astype(BF16)
        g = (go_in[:, cols].astype(F32) * q_in[:, cols].astype(F32)).astype(BF16)
        u_ref[:, cols] = u
        g_ref[:, cols] = g
        for half in range(HALVES):
            part = slice(half * LANES, (half + 1) * LANES)
            uf[half] = u[:, part].astype(F32)
            gf[half] = g[:, part].astype(F32)
        states(t, rate, u_ref, g_ref, ptab, btab, uf, gf, sub_s, sub_b, send_a)

    pl.semaphore_wait(barrier, INNER + OUTER - 2)

    for j in inner:
        remote(send_a.at[j], recv_a.at[idx], sa.at[j], ra.at[idx], to_inner(j)).start()
    recv_a[idx] = send_a[idx]

    @pl.loop(0, TILES)
    def _(t):
        near_part(t, rate, res, u_ref, g_ref, wtab, vtab, htab, near_c, near_g)

    block = pl.ds(pl.multiple_of(idx * LANES, LANES), LANES)
    lam = rate[:, block] * (1.0 / SEQ)
    dec = jnp.exp(-lam * float(ROWS))
    span = float(ROWS * INNER)
    dec_g = jnp.exp(-lam * span)
    for j in inner:
        remote(send_a.at[j], recv_a.at[j], sa.at[j], ra.at[j], to_inner(j)).wait_recv()
    zero = jnp.zeros((MODES, LANES), F32)
    s, q, gr, gw, bn, tn = zero, zero, zero, zero, zero, zero
    front = jnp.ones((MODES, LANES), F32)
    nears = []
    for j in range(INNER):
        part = [recv_a[j, n * MODES : (n + 1) * MODES, :].astype(F32) for n in range(6)]
        s_j, m_j, b_j, t_j, gr_j, gw_j = part
        pre_s[j] = s
        nears.append(b_j)
        gr = gr + gr_j + b_j * s
        gw = gw + gw_j + t_j * s + b_j * q
        q = dec * (q + float(ROWS) * s) + m_j
        s = dec * s + s_j
        db = front * b_j
        bn = bn + db
        tn = tn + front * t_j + float(ROWS * j) * db
        front = front * dec
    for n, part in enumerate((s, q, bn, tn, gr, gw)):
        send_b[:, n, :] = part
    send_m[0] = bn
    send_m[1] = s

    for p in outer:
        remote(send_b.at[p], recv_b.at[grp], sb.at[p], rb.at[grp], to_outer(p)).start()
    for p in outer:
        pick = (p > grp).astype(jnp.int32)
        remote(send_m.at[pick], recv_m.at[grp], sm.at[p], rm.at[grp], to_outer(p)).start()
    recv_b[grp] = send_b[grp]
    recv_m[grp] = zero
    back = zero
    for j in reversed(range(INNER)):
        pre_b[j] = back
        back = dec * back + nears[j]
    decs = [jnp.ones((MODES, LANES), F32)]
    for j in range(1, INNER):
        decs.append(decs[-1] * dec)
    mine = iota((MODES, LANES), 0) == grp
    lam_row = jnp.sum(jnp.where(mine, lam, 0.0), axis=0, keepdims=True)
    dec_row = jnp.exp(-lam_row * span)

    for p in outer:
        remote(send_b.at[p], recv_b.at[p], sb.at[p], rb.at[p], to_outer(p)).wait_recv()
    zrow = jnp.zeros((1, LANES), F32)
    s, q, gr, gw = zrow, zrow, zrow, zrow
    for p in range(OUTER):
        s_p, m_p, b_p, t_p, gr_p, gw_p = [recv_b[p, n : n + 1, :] for n in range(6)]
        gr = gr + gr_p + b_p * s
        gw = gw + gw_p + t_p * s + b_p * q
        q = dec_row * (q + span * s) + m_p
        s = dec_row * s + s_p
    send_d[0:1, :] = gr
    send_d[1:2, :] = gw
    for p in outer:
        remote(send_d, recv_d.at[grp], sd.at[p], rd.at[grp], to_outer(p)).start()
    recv_d[grp] = send_d[...]

    for p in outer:
        remote(send_m.at[0], recv_m.at[p], sm.at[p], rm.at[p], to_outer(p)).wait_recv()
    state, back = zero, zero
    for p in range(OUTER):
        state = jnp.where(p < grp, dec_g * state + recv_m[p], state)
    for p in reversed(range(OUTER)):
        back = jnp.where(p > grp, dec_g * back + recv_m[p], back)

    for j in range(INNER):
        send_c[j, 0:MODES, :] = pre_s[j] + decs[j] * state
        send_c[j, MODES : 2 * MODES, :] = pre_b[j] + decs[INNER - 1 - j] * back
    for j in inner:
        remote(send_c.at[j], recv_c.at[idx], sc.at[j], rc.at[idx], to_inner(j)).start()
    recv_c[idx] = send_c[idx]

    for p in outer:
        remote(send_d, recv_d.at[p], sd.at[p], rd.at[p], to_outer(p)).wait_recv()
    send_e[0:MODES, :] = recv_d[:, 0, :].astype(BF16)
    send_e[MODES : 2 * MODES, :] = recv_d[:, 1, :].astype(BF16)
    for j in inner:
        remote(send_e, recv_e.at[idx], se.at[j], re.at[idx], to_inner(j)).start()
    recv_e[idx] = send_e[...]

    for j in inner:
        remote(send_c.at[j], recv_c.at[j], sc.at[j], rc.at[j], to_inner(j)).wait_recv()

    results = ((gq, gq_hbm), (gk, gk_hbm), (gv, gv_hbm))

    def store(t, n):
        src, dst = results[n]
        return pltpu.make_async_copy(src.at[:, columns(t)], dst.at[:, columns(t)], out_sem.at[t, n])

    @pl.loop(0, TILES)
    def _(t):
        far_part(t, rate, res, k_in, v_in, go_in, wtab, vtab, sub_s, sub_b, near_c, near_g, recv_c, gq, gk, gv)
        for n in range(3):
            store(t, n).start()

    for j in inner:
        remote(send_e, recv_e.at[j], se.at[j], re.at[j], to_inner(j)).wait_recv()
    scale = SEQ ** -0.5
    for j in range(INNER):
        cols = slice(j * LANES, (j + 1) * LANES)
        gres[:, cols] = scale * recv_e[j, 0:MODES, :].astype(F32)
        grate[:, cols] = (-scale / SEQ) * res[:, cols] * recv_e[j, MODES : 2 * MODES, :].astype(F32)

    sums = (
        pltpu.make_async_copy(gres, gres_hbm, par_sem.at[0]),
        pltpu.make_async_copy(grate, grate_hbm, par_sem.at[1]),
    )
    for cp in sums:
        cp.start()
    for j in inner:
        remote(send_a.at[j], recv_a.at[j], sa.at[j], ra.at[j], to_inner(j)).wait_send()
        remote(send_c.at[j], recv_c.at[j], sc.at[j], rc.at[j], to_inner(j)).wait_send()
        remote(send_e, recv_e.at[j], se.at[j], re.at[j], to_inner(j)).wait_send()
    for p in outer:
        remote(send_b.at[p], recv_b.at[p], sb.at[p], rb.at[p], to_outer(p)).wait_send()
        remote(send_m.at[0], recv_m.at[p], sm.at[p], rm.at[p], to_outer(p)).wait_send()
        remote(send_d, recv_d.at[p], sd.at[p], rd.at[p], to_outer(p)).wait_send()
    for t in range(TILES):
        for n in range(3):
            store(t, n).wait()
    for cp in sums:
        cp.wait()


def store_kernel(*refs):
    srcs, dsts, held, sem_in, sem_out = refs[:5], refs[5:10], refs[10:15], refs[15], refs[16]
    loads = [pltpu.make_async_copy(s, h, sem_in.at[n]) for n, (s, h) in enumerate(zip(srcs, held))]
    stores = [pltpu.make_async_copy(h, d, sem_out.at[n]) for n, (h, d) in enumerate(zip(held, dsts))]
    for cp in loads:
        cp.start()
    for load, store in zip(loads, stores):
        load.wait()
        store.start()
    for cp in stores:
        cp.wait()


def local(query, key_in, value, grad_out, residue, rate):
    hbm = pl.BlockSpec(memory_space=pltpu.HBM)
    big = jax.ShapeDtypeStruct((ROWS, CHANS), BF16)
    small = jax.ShapeDtypeStruct((MODES, CHANS), F32)
    dma = pltpu.SemaphoreType.DMA

    def buf(*shape, dtype=F32):
        return pltpu.VMEM(shape, dtype)

    results = pl.pallas_call(
        main_kernel,
        out_shape=(big, big, big, small, small),
        in_specs=[hbm] * 6,
        out_specs=[hbm] * 5,
        scratch_shapes=[
            *[buf(ROWS, CHANS, dtype=BF16)] * 3,
            *[buf(MODES, CHANS)] * 2,
            *[buf(ROWS, CHANS, dtype=BF16)] * 4,
            *[buf(MODES, CHANS)] * 2,
            *[buf(ROWS, CHANS, dtype=BF16)] * 2,
            *[buf(HALVES, ROWS, LANES)] * 2,
            *[buf(MODES, SUB, CHANS, dtype=BF16)] * 2,
            *[buf(SUB, MODES, CHANS, dtype=BF16)] * 2,
            buf(SUB, SUB, TILE, dtype=BF16),
            *[buf(NSUB, MODES, CHANS)] * 2,
            *[buf(ROWS, CHANS)] * 2,
            *[buf(INNER, 6 * MODES, LANES, dtype=BF16)] * 2,
            *[buf(INNER, MODES, LANES)] * 2,
            *[buf(OUTER, 8, LANES)] * 2,
            buf(2, MODES, LANES), buf(OUTER, MODES, LANES),
            buf(8, LANES), buf(OUTER, 8, LANES),
            *[buf(INNER, 2 * MODES, LANES)] * 2,
            buf(2 * MODES, LANES, dtype=BF16), buf(INNER, 2 * MODES, LANES, dtype=BF16),
            dma((TILES, 4)), dma((2,)), dma((TILES, 3)),
            dma((INNER,)), dma((INNER,)), dma((OUTER,)), dma((OUTER,)), dma((OUTER,)), dma((OUTER,)),
            dma((OUTER,)), dma((OUTER,)), dma((INNER,)), dma((INNER,)), dma((INNER,)), dma((INNER,)),
        ],
        compiler_params=pltpu.CompilerParams(collective_id=0, has_side_effects=True, vmem_limit_bytes=VMEM_LIMIT),
        name="hyena",
    )(query, key_in, value, grad_out, residue, rate)

    return pl.pallas_call(
        store_kernel,
        out_shape=(big, big, big, small, small),
        in_specs=[hbm] * 5,
        out_specs=[hbm] * 5,
        scratch_shapes=[
            *[buf(ROWS, CHANS, dtype=BF16)] * 3,
            *[buf(MODES, CHANS)] * 2,
            dma((5,)),
            dma((5,)),
        ],
        compiler_params=pltpu.CompilerParams(vmem_limit_bytes=VMEM_LIMIT),
        name="store",
    )(*results)


def solution(mesh):
    big, small = P("ctx", "tp"), P(None, "tp")
    return jax.shard_map(
        local, mesh=mesh, in_specs=(big, big, big, big, small, small),
        out_specs=(big, big, big, small, small), check_vma=False,
    )
```

```python
import jax
import jax.numpy as jnp
from jax import lax
from jax.experimental import pallas as pl
from jax.experimental.pallas import tpu as pltpu
from jax.sharding import PartitionSpec as P

SEQ = 32768
MODES = 16
ROWS = 256
CHANS = 1024
SUB = 16
NSUB = ROWS // SUB
MID = 8
LANES = 128
TILE = 256
TILES = CHANS // TILE
HALVES = TILE // LANES
RUN = 8
SEGS = 2
DEPTH = 8
GROUP = SEGS * RUN
HALF = MODES // SEGS
VMEM_LIMIT = 63 * 2**20
F32 = jnp.float32
BF16 = jnp.bfloat16
MESH = pl.DeviceIdType.MESH


def iota(shape, dim):
    return lax.broadcasted_iota(jnp.int32, shape, dim)


def dot(a, b):
    return jnp.dot(a, b, preferred_element_type=F32)


def columns(t):
    return pl.ds(pl.multiple_of(t * TILE, TILE), TILE)


def spread(tab, val):
    return (tab * val[None]).reshape(tab.shape[0] * tab.shape[1], TILE)


def state_tables(t, rate, ptab, btab):
    cols = columns(t)
    pos = iota((SUB, TILE), 0).astype(F32)
    lam = rate[:, cols] * (1.0 / SEQ)
    for m in range(MODES):
        row = lam[m : m + 1, :]
        ptab[m, :, cols] = jnp.exp(-row * (SUB - 1.0 - pos)).astype(BF16)
        btab[m, :, cols] = jnp.exp(-row * (pos + 1.0)).astype(BF16)


def states(t, rate, u_ref, g_ref, ptab, btab, uf, gf, sub_s, sub_b, send_a):
    cols = columns(t)
    lam = rate[:, cols] * (1.0 / SEQ)
    out_row = iota((2 * MODES, MODES * SUB), 0)
    in_row = iota((2 * MODES, MODES * SUB), 1)
    hit = (in_row // SUB) == (out_row % MODES)
    off = (in_row % SUB).astype(F32)
    first = out_row < MODES
    sel_s = jnp.where(hit, jnp.where(first, 1.0, SUB - 1.0 - off), 0.0).astype(BF16)
    sel_b = jnp.where(hit, jnp.where(first, 1.0, off + 1.0), 0.0).astype(BF16)
    step = jnp.exp(-lam * SUB)
    zero = jnp.zeros((MODES, TILE), F32)
    s, q, bn, tn, gr, gw = zero, zero, zero, zero, zero, zero
    decay = jnp.ones((MODES, TILE), F32)
    for k in range(NSUB):
        rows = slice(k * SUB, (k + 1) * SUB)
        su = dot(sel_s, spread(ptab[:, :, cols], u_ref[rows, cols]))
        sg = dot(sel_b, spread(btab[:, :, cols], g_ref[rows, cols]))
        s_k, m_k = su[:MODES], su[MODES:]
        b_k, t_k = sg[:MODES], sg[MODES:]
        sub_s[k, :, cols] = s_k
        sub_b[k, :, cols] = b_k
        gr = gr + b_k * s
        gw = gw + t_k * s + b_k * q
        q = step * (q + float(SUB) * s) + m_k
        s = step * s + s_k
        db = decay * b_k
        bn = bn + db
        tn = tn + decay * t_k + float(k * SUB) * db
        decay = decay * step
    halves = []
    for half in range(HALVES):
        acc = [jnp.zeros((8, LANES), F32) for _ in range(SUB)]
        for octet in range(NSUB // 8):
            us = [uf[half, pl.ds(octet * 8 * SUB + b, 8, stride=SUB), :] for b in range(SUB)]
            for b in range(SUB):
                gb = gf[half, pl.ds(octet * 8 * SUB + b, 8, stride=SUB), :]
                for lag in range(b + 1):
                    acc[lag] = acc[lag] + gb * us[b - lag]
        halves.append([jnp.sum(a, axis=0, keepdims=True) for a in acc])
    unit = jnp.exp(-lam)
    power = jnp.ones((MODES, TILE), F32)
    for lag in range(SUB):
        term = jnp.concatenate([h[lag] for h in halves], axis=1) * power
        gr = gr + term
        gw = gw + float(lag) * term
        power = power * unit
    for half in range(HALVES):
        part_cols = slice(half * LANES, (half + 1) * LANES)
        for x in range(SEGS):
            modes = slice(x * HALF, (x + 1) * HALF)
            parts = [part[modes, part_cols] for part in (s, q, bn, tn, gr, gw)]
            send_a[x * RUN + t * HALVES + half] = jnp.concatenate(parts, axis=0).astype(BF16)


def near_part(t, rate, res, u_ref, g_ref, wtab, vtab, htab, near_c, near_g):
    cols = columns(t)
    lam = rate[:, cols] * (1.0 / SEQ)
    unit = jnp.exp(-lam)
    power = res[:, cols]
    mid = power * jnp.exp(-lam * float(MID))
    powers = []
    for b in range(SUB):
        htab[b] = jnp.broadcast_to(jnp.sum(power, axis=0, keepdims=True), (SUB, TILE)).astype(BF16)
        powers.append(power - mid)
        power = power * unit
    powers.append(power - mid)
    for i in range(SUB // 2):
        for h in range(2):
            modes = slice(h * HALF, (h + 1) * HALF)
            pair = (powers[2 * i + 1][modes], powers[2 * i + 2][modes])
            wtab[h, i, :, cols] = jnp.concatenate(pair, axis=0).astype(BF16)
            pair = (powers[SUB - 1 - 2 * i][modes], powers[SUB - 2 - 2 * i][modes])
            vtab[h, i, :, cols] = jnp.concatenate(pair, axis=0).astype(BF16)
    out_row = iota((SUB, SUB * SUB), 0)
    in_row = iota((SUB, SUB * SUB), 1)
    lag, pos = in_row // SUB, in_row % SUB
    down = jnp.where(pos + lag == out_row, 1.0, 0.0).astype(BF16)
    up = jnp.where(pos - lag == out_row, 1.0, 0.0).astype(BF16)
    for k in range(NSUB):
        rows = slice(k * SUB, (k + 1) * SUB)
        near_c[rows, cols] = dot(down, spread(htab[...], u_ref[rows, cols]))
        near_g[rows, cols] = dot(up, spread(htab[...], g_ref[rows, cols]))


def far_part(t, rate, res, k_in, v_in, go_in, wtab, vtab, sub_s, sub_b, near_c, near_g, recv_c, gq, gk, gv):
    cols = columns(t)
    lam = rate[:, cols] * (1.0 / SEQ)
    step = jnp.exp(-lam * SUB)
    mid = res[:, cols] * jnp.exp(-lam * float(MID))

    def incoming(n):
        rows = slice(n * HALF, (n + 1) * HALF)
        parts = [
            jnp.concatenate([recv_c[x * RUN + t * HALVES + h, rows, :] for x in range(SEGS)], axis=0)
            for h in range(HALVES)
        ]
        return jnp.concatenate(parts, axis=1)

    out_row = iota((2 * SUB, SUB * MODES), 0)
    in_row = iota((2 * SUB, SUB * MODES), 1)
    pick = jnp.where(in_row // HALF == out_row, 1.0, 0.0).astype(BF16)

    def reach(tab, xs):
        sums = []
        bases = []
        for x in xs:
            bases.append(jnp.broadcast_to(jnp.sum(mid * x, axis=0, keepdims=True), (SUB, TILE)))
            low = jnp.concatenate([x[:HALF], x[:HALF]], axis=0).astype(BF16)
            high = jnp.concatenate([x[HALF:], x[HALF:]], axis=0).astype(BF16)
            sums.append((tab[0, :, :, cols] * low[None] + tab[1, :, :, cols] * high[None]).reshape(SUB * HALF, TILE))
        return dot(pick, jnp.concatenate(sums, axis=0)) + jnp.concatenate(bases, axis=0)

    x = incoming(0)
    for k in range(0, NSUB, 2):
        rows = slice(k * SUB, (k + 2) * SUB)
        after = step * x + sub_s[k, :, cols]
        conv = near_c[rows, cols] + reach(wtab, (x, after))
        gq[rows, cols] = (go_in[rows, cols].astype(F32) * conv).astype(BF16)
        x = step * after + sub_s[k + 1, :, cols]
    x = incoming(1)
    for k in reversed(range(0, NSUB, 2)):
        rows = slice(k * SUB, (k + 2) * SUB)
        before = step * x + sub_b[k + 1, :, cols]
        grad = near_g[rows, cols] + reach(vtab, (before, x))
        gk[rows, cols] = (v_in[rows, cols].astype(F32) * grad).astype(BF16)
        gv[rows, cols] = (k_in[rows, cols].astype(F32) * grad).astype(BF16)
        x = step * before + sub_b[k, :, cols]


def main_kernel(
    q_hbm, k_hbm, v_hbm, go_hbm, res_hbm, rate_hbm,
    gq_hbm, gk_hbm, gv_hbm, gres_hbm, grate_hbm,
    gq, gk, gv, gres, grate, q_in, k_in, v_in, go_in, res, rate, u_ref, g_ref, uf, gf, ptab, btab, wtab, vtab, htab,
    sub_s, sub_b, near_c, near_g,
    send_a, recv_a, pre_s, pre_b, send_m, recv_m, send_x, recv_x, send_c, recv_c, send_e, recv_e,
    in_sem, par_sem, out_sem, sa, ra, sm, rm, sx, rx, sc, rc, se, re,
):
    me = lax.axis_index("ctx")
    seg = me // (DEPTH * RUN)
    z = (me // RUN) % DEPTH
    y = (me % RUN) // 2
    own = seg * RUN + me % RUN
    others = [(own + d) % GROUP for d in (12, 4, 11, 5, 13, 3, 10, 6, 14, 2, 9, 7, 8, 15, 1)]
    layers = [(z + d) % DEPTH for d in (4, 5, 3, 6, 2, 7, 1)]

    def member(j):
        return {"ctx": (j // RUN) * (DEPTH * RUN) + z * RUN + j % RUN}

    def layer(p):
        return {"ctx": seg * (DEPTH * RUN) + p * RUN + me % RUN}

    def gray(n):
        return n + n // 2 - 2 * (n // 3)

    def tile_at(n):
        return (y + gray(n)) % TILES

    pairs = ((q_hbm, q_in), (k_hbm, k_in), (v_hbm, v_in), (go_hbm, go_in))

    def load(t, n):
        src, dst = pairs[n]
        return pltpu.make_async_copy(src.at[:, columns(t)], dst.at[:, columns(t)], in_sem.at[t, n])

    params = (
        pltpu.make_async_copy(rate_hbm, rate, par_sem.at[0]),
        pltpu.make_async_copy(res_hbm, res, par_sem.at[1]),
    )
    for cp in params:
        cp.start()
    for n in reversed(range(TILES)):
        for i in range(4):
            load(tile_at(n), i).start()

    barrier = pltpu.get_barrier_semaphore()
    for j in others:
        pl.semaphore_signal(barrier, inc=1, device_id=member(j), device_id_type=MESH)
    for p in layers:
        pl.semaphore_signal(barrier, inc=1, device_id=layer(p), device_id_type=MESH)

    def remote(src, dst, ssem, rsem, target):
        return pltpu.make_async_remote_copy(
            src_ref=src, dst_ref=dst, send_sem=ssem, recv_sem=rsem, device_id=target, device_id_type=MESH
        )

    for cp in params:
        cp.wait()

    @pl.loop(0, TILES)
    def _(t):
        state_tables(t, rate, ptab, btab)

    def tile_states(t):
        cols = columns(t)
        for n in range(4):
            load(t, n).wait()
        u = (k_in[:, cols].astype(F32) * v_in[:, cols].astype(F32)).astype(BF16)
        g = (go_in[:, cols].astype(F32) * q_in[:, cols].astype(F32)).astype(BF16)
        u_ref[:, cols] = u
        g_ref[:, cols] = g
        for half in range(HALVES):
            part = slice(half * LANES, (half + 1) * LANES)
            uf[half] = u[:, part].astype(F32)
            gf[half] = g[:, part].astype(F32)
        states(t, rate, u_ref, g_ref, ptab, btab, uf, gf, sub_s, sub_b, send_a)

    def tile_owners(t):
        return [x * RUN + t * HALVES + half for x in range(SEGS) for half in range(HALVES)]

    def tile_send(t):
        for j in tile_owners(t):

            @pl.when(j != own)
            def _():
                remote(send_a.at[j], recv_a.at[own], sa.at[j], ra.at[own], member(j)).start()

    @pl.loop(0, 2)
    def _(n):
        tile_states(tile_at(TILES - 1 - n))

    pl.semaphore_wait(barrier, GROUP + DEPTH - 2)
    tile_send(tile_at(3))
    tile_send(tile_at(2))

    @pl.loop(2, TILES)
    def _(n):
        tile_states(tile_at(TILES - 1 - n))
        tile_send(tile_at(TILES - 1 - n))

    recv_a[own] = send_a[own]

    def near(t):
        near_part(t, rate, res, u_ref, g_ref, wtab, vtab, htab, near_c, near_g)

    @pl.loop(0, 2)
    def _(t):
        near(t)

    block = pl.ds(pl.multiple_of((me % RUN) * LANES, LANES), LANES)
    lam8 = rate[pl.ds(pl.multiple_of(seg * HALF, HALF), HALF), block] * (1.0 / SEQ)
    lam = jnp.concatenate([lam8, lam8], axis=0)
    dec = jnp.exp(-lam * float(ROWS))
    span = float(ROWS * RUN)
    dec_g = jnp.exp(-lam * span)
    ahead = jnp.exp(-lam8 * (span * z.astype(F32)))
    behind = jnp.exp(-lam8 * (span * (DEPTH - 1 - z).astype(F32)))
    decs = [jnp.ones((MODES, LANES), F32)]
    for w in range(1, RUN):
        decs.append(decs[-1] * dec)
    zero = jnp.zeros((MODES, LANES), F32)
    for j in others:
        remote(send_a.at[j], recv_a.at[j], sa.at[j], ra.at[j], member(j)).wait_recv()

    def combine(carry, part, decay, length):
        s, q, bn, tn, gr, gw, front, dist = carry
        s_j, m_j, b_j, t_j, gr_j, gw_j = part
        db = front * b_j
        return (
            decay * s + s_j,
            decay * (q + length * s) + m_j,
            bn + db,
            tn + front * t_j + dist * db,
            gr + gr_j + b_j * s,
            gw + gw_j + t_j * s + b_j * q,
            front * decay,
            dist + length,
        )

    ones = jnp.ones((MODES, LANES), F32)
    total = (zero, zero, zero, zero, zero, zero, ones, 0.0)
    nears = []
    for w in range(RUN):
        got = [recv_a[x * RUN + w].astype(F32) for x in range(SEGS)]
        part = [
            jnp.concatenate([rows[n * HALF : (n + 1) * HALF] for rows in got], axis=0) for n in range(6)
        ]
        pre_s[w] = total[0]
        nears.append(part[2])
        total = combine(total, part, dec, float(ROWS))
    s, q, bn, tn, gr, gw = total[:6]
    send_m[0:MODES, :] = s
    send_m[MODES : 2 * MODES, :] = bn
    send_x[...] = jnp.concatenate([q, tn, gr, gw], axis=0).astype(BF16)

    for p in layers:
        remote(send_m, recv_m.at[z], sm.at[p], rm.at[z], layer(p)).start()
    for p in layers:
        remote(send_x, recv_x.at[z], sx.at[p], rx.at[z], layer(p)).start()
    recv_m[z] = send_m[...]
    recv_x[z] = send_x[...]
    back = zero
    for w in reversed(range(RUN)):
        pre_b[w] = back
        back = dec * back + nears[w]

    @pl.loop(2, TILES)
    def _(t):
        near(t)

    for p in layers:
        remote(send_m, recv_m.at[p], sm.at[p], rm.at[p], layer(p)).wait_recv()
    state, whole = zero, zero
    for p in range(DEPTH):
        s_p = recv_m[p, 0:MODES, :]
        state = jnp.where(p < z, dec_g * state + s_p, state)
        whole = dec_g * whole + s_p
    state = jnp.concatenate([state[:HALF], state[HALF:] + ahead * whole[:HALF]], axis=0)
    back, whole = zero, zero
    for p in reversed(range(DEPTH)):
        b_p = recv_m[p, MODES : 2 * MODES, :]
        back = jnp.where(p > z, dec_g * back + b_p, back)
        whole = dec_g * whole + b_p
    back = jnp.concatenate([back[:HALF] + behind * whole[HALF:], back[HALF:]], axis=0)

    for w in range(RUN):
        st = pre_s[w] + decs[w] * state
        bk = pre_b[w] + decs[RUN - 1 - w] * back
        for x in range(SEGS):
            rows = slice(x * HALF, (x + 1) * HALF)
            send_c[x * RUN + w] = jnp.concatenate([st[rows], bk[rows]], axis=0)
    for j in others:
        remote(send_c.at[j], recv_c.at[own], sc.at[j], rc.at[own], member(j)).start()
    recv_c[own] = send_c[own]

    for p in layers:
        remote(send_x, recv_x.at[p], sx.at[p], rx.at[p], layer(p)).wait_recv()
    total = (zero, zero, zero, zero, zero, zero, ones, 0.0)
    for p in range(DEPTH):
        rest = recv_x[p].astype(F32)
        m_p, t_p, gr_p, gw_p = [rest[n * MODES : (n + 1) * MODES] for n in range(4)]
        part = (recv_m[p, 0:MODES, :], m_p, recv_m[p, MODES : 2 * MODES, :], t_p, gr_p, gw_p)
        total = combine(total, part, dec_g, span)
    s, q, bn, tn, gr, gw = total[:6]
    early, late = slice(0, HALF), slice(HALF, MODES)
    gr_all = gr[early] + gr[late] + bn[late] * s[early]
    gw_all = gw[early] + gw[late] + tn[late] * s[early] + bn[late] * q[early]
    send_e[...] = jnp.concatenate([gr_all, gw_all], axis=0).astype(BF16)
    for j in others:
        remote(send_e, recv_e.at[own], se.at[j], re.at[own], member(j)).start()
    recv_e[own] = send_e[...]

    results = ((gq, gq_hbm), (gk, gk_hbm), (gv, gv_hbm))

    def store(t, n):
        src, dst = results[n]
        return pltpu.make_async_copy(src.at[:, columns(t)], dst.at[:, columns(t)], out_sem.at[t, n])

    @pl.loop(0, TILES)
    def _(n):
        t = tile_at(n)
        for j in tile_owners(t):

            @pl.when(j != own)
            def _():
                remote(send_c.at[j], recv_c.at[j], sc.at[j], rc.at[j], member(j)).wait_recv()

        far_part(t, rate, res, k_in, v_in, go_in, wtab, vtab, sub_s, sub_b, near_c, near_g, recv_c, gq, gk, gv)
        for i in range(3):
            store(t, i).start()

    for j in others:
        remote(send_e, recv_e.at[j], se.at[j], re.at[j], member(j)).wait_recv()
    scale = SEQ ** -0.5
    for w in range(RUN):
        cols = slice(w * LANES, (w + 1) * LANES)
        got = [recv_e[x * RUN + w].astype(F32) for x in range(SEGS)]
        gr, gw = [
            jnp.concatenate([rows[n * HALF : (n + 1) * HALF] for rows in got], axis=0) for n in range(2)
        ]
        gres[:, cols] = scale * gr
        grate[:, cols] = (-scale / SEQ) * res[:, cols] * gw
    sums = (
        pltpu.make_async_copy(gres, gres_hbm, par_sem.at[0]),
        pltpu.make_async_copy(grate, grate_hbm, par_sem.at[1]),
    )
    for cp in sums:
        cp.start()
    for j in others:
        remote(send_a.at[j], recv_a.at[j], sa.at[j], ra.at[j], member(j)).wait_send()
        remote(send_c.at[j], recv_c.at[j], sc.at[j], rc.at[j], member(j)).wait_send()
        remote(send_e, recv_e.at[j], se.at[j], re.at[j], member(j)).wait_send()
    for p in layers:
        remote(send_m, recv_m.at[p], sm.at[p], rm.at[p], layer(p)).wait_send()
        remote(send_x, recv_x.at[p], sx.at[p], rx.at[p], layer(p)).wait_send()
    for t in range(TILES):
        for n in range(3):
            store(t, n).wait()
    for cp in sums:
        cp.wait()


def store_kernel(*refs):
    srcs, dsts, held, sem_in, sem_out = refs[:5], refs[5:10], refs[10:15], refs[15], refs[16]
    loads = [pltpu.make_async_copy(s, h, sem_in.at[n]) for n, (s, h) in enumerate(zip(srcs, held))]
    stores = [pltpu.make_async_copy(h, d, sem_out.at[n]) for n, (h, d) in enumerate(zip(held, dsts))]
    for cp in loads:
        cp.start()
    for load, store in zip(loads, stores):
        load.wait()
        store.start()
    for cp in stores:
        cp.wait()


def local(query, key_in, value, grad_out, residue, rate):
    hbm = pl.BlockSpec(memory_space=pltpu.HBM)
    big = jax.ShapeDtypeStruct((ROWS, CHANS), BF16)
    small = jax.ShapeDtypeStruct((MODES, CHANS), F32)
    dma = pltpu.SemaphoreType.DMA

    def buf(*shape, dtype=F32):
        return pltpu.VMEM(shape, dtype)

    results = pl.pallas_call(
        main_kernel,
        out_shape=(big, big, big, small, small),
        in_specs=[hbm] * 6,
        out_specs=[hbm] * 5,
        scratch_shapes=[
            *[buf(ROWS, CHANS, dtype=BF16)] * 3,
            *[buf(MODES, CHANS)] * 2,
            *[buf(ROWS, CHANS, dtype=BF16)] * 4,
            *[buf(MODES, CHANS)] * 2,
            *[buf(ROWS, CHANS, dtype=BF16)] * 2,
            *[buf(HALVES, ROWS, LANES)] * 2,
            *[buf(MODES, SUB, CHANS, dtype=BF16)] * 2,
            *[buf(SEGS, SUB // 2, 2 * HALF, CHANS, dtype=BF16)] * 2,
            buf(SUB, SUB, TILE, dtype=BF16),
            *[buf(NSUB, MODES, CHANS)] * 2,
            *[buf(ROWS, CHANS)] * 2,
            *[buf(GROUP, 6 * HALF, LANES, dtype=BF16)] * 2,
            *[buf(RUN, MODES, LANES)] * 2,
            buf(2 * MODES, LANES), buf(DEPTH, 2 * MODES, LANES),
            buf(4 * MODES, LANES, dtype=BF16), buf(DEPTH, 4 * MODES, LANES, dtype=BF16),
            *[buf(GROUP, 2 * HALF, LANES)] * 2,
            buf(2 * HALF, LANES, dtype=BF16), buf(GROUP, 2 * HALF, LANES, dtype=BF16),
            dma((TILES, 4)), dma((2,)), dma((TILES, 3)),
            dma((GROUP,)), dma((GROUP,)), dma((DEPTH,)), dma((DEPTH,)), dma((DEPTH,)), dma((DEPTH,)),
            dma((GROUP,)), dma((GROUP,)), dma((GROUP,)), dma((GROUP,)),
        ],
        compiler_params=pltpu.CompilerParams(collective_id=0, has_side_effects=True, vmem_limit_bytes=VMEM_LIMIT),
        name="hyena",
    )(query, key_in, value, grad_out, residue, rate)

    return pl.pallas_call(
        store_kernel,
        out_shape=(big, big, big, small, small),
        in_specs=[hbm] * 5,
        out_specs=[hbm] * 5,
        scratch_shapes=[
            *[buf(ROWS, CHANS, dtype=BF16)] * 3,
            *[buf(MODES, CHANS)] * 2,
            dma((5,)),
            dma((5,)),
        ],
        compiler_params=pltpu.CompilerParams(vmem_limit_bytes=VMEM_LIMIT),
        name="store",
    )(*results)


def solution(mesh):
    big, small = P("ctx", "tp"), P(None, "tp")
    return jax.shard_map(
        local, mesh=mesh, in_specs=(big, big, big, big, small, small),
        out_specs=(big, big, big, small, small), check_vma=False,
    )
```

```python
import jax
import jax.numpy as jnp
from jax import lax
from jax.experimental import pallas as pl
from jax.experimental.pallas import tpu as pltpu
from jax.sharding import PartitionSpec as P

SEQ = 32768
MODES = 16
ROWS = 256
CHANS = 1024
SUB = 16
NSUB = ROWS // SUB
MID = 8
LANES = 128
TILE = 256
TILES = CHANS // TILE
HALVES = TILE // LANES
RUN = 8
SEGS = 2
DEPTH = 8
GROUP = SEGS * RUN
HALF = MODES // SEGS
VMEM_LIMIT = 40 * 2**20
F32 = jnp.float32
BF16 = jnp.bfloat16
MESH = pl.DeviceIdType.MESH


def iota(shape, dim):
    return lax.broadcasted_iota(jnp.int32, shape, dim)


def dot(a, b):
    return jnp.dot(a, b, preferred_element_type=F32)


def columns(t):
    return pl.ds(pl.multiple_of(t * TILE, TILE), TILE)


def spread(tab, val):
    return (tab * val[None]).reshape(tab.shape[0] * tab.shape[1], TILE)


def state_tables(t, rate, ptab, btab):
    cols = columns(t)
    pos = iota((SUB, TILE), 0).astype(F32)
    lam = rate[:, cols] * (1.0 / SEQ)
    for m in range(MODES):
        row = lam[m : m + 1, :]
        ptab[m, :, cols] = jnp.exp(-row * (SUB - 1.0 - pos)).astype(BF16)
        btab[m, :, cols] = jnp.exp(-row * (pos + 1.0)).astype(BF16)


def states(t, rate, u_ref, g_ref, ptab, btab, uf, gf, sub_s, sub_b, send_a):
    cols = columns(t)
    lam = rate[:, cols] * (1.0 / SEQ)
    out_row = iota((2 * MODES, MODES * SUB), 0)
    in_row = iota((2 * MODES, MODES * SUB), 1)
    hit = (in_row // SUB) == (out_row % MODES)
    off = (in_row % SUB).astype(F32)
    first = out_row < MODES
    sel_s = jnp.where(hit, jnp.where(first, 1.0, SUB - 1.0 - off), 0.0).astype(BF16)
    sel_b = jnp.where(hit, jnp.where(first, 1.0, off + 1.0), 0.0).astype(BF16)
    step = jnp.exp(-lam * SUB)
    zero = jnp.zeros((MODES, TILE), F32)
    s, q, bn, tn, gr, gw = zero, zero, zero, zero, zero, zero
    decay = jnp.ones((MODES, TILE), F32)
    for k in range(NSUB):
        rows = slice(k * SUB, (k + 1) * SUB)
        su = dot(sel_s, spread(ptab[:, :, cols], u_ref[rows, cols]))
        sg = dot(sel_b, spread(btab[:, :, cols], g_ref[rows, cols]))
        s_k, m_k = su[:MODES], su[MODES:]
        b_k, t_k = sg[:MODES], sg[MODES:]
        sub_s[k, :, cols] = s_k
        sub_b[k, :, cols] = b_k
        gr = gr + b_k * s
        gw = gw + t_k * s + b_k * q
        q = step * (q + float(SUB) * s) + m_k
        s = step * s + s_k
        db = decay * b_k
        bn = bn + db
        tn = tn + decay * t_k + float(k * SUB) * db
        decay = decay * step
    halves = []
    for half in range(HALVES):
        acc = [jnp.zeros((8, LANES), F32) for _ in range(SUB)]
        for octet in range(NSUB // 8):
            us = [uf[half, pl.ds(octet * 8 * SUB + b, 8, stride=SUB), :] for b in range(SUB)]
            for b in range(SUB):
                gb = gf[half, pl.ds(octet * 8 * SUB + b, 8, stride=SUB), :]
                for lag in range(b + 1):
                    acc[lag] = acc[lag] + gb * us[b - lag]
        halves.append([jnp.sum(a, axis=0, keepdims=True) for a in acc])
    unit = jnp.exp(-lam)
    power = jnp.ones((MODES, TILE), F32)
    for lag in range(SUB):
        term = jnp.concatenate([h[lag] for h in halves], axis=1) * power
        gr = gr + term
        gw = gw + float(lag) * term
        power = power * unit
    for half in range(HALVES):
        part_cols = slice(half * LANES, (half + 1) * LANES)
        for x in range(SEGS):
            modes = slice(x * HALF, (x + 1) * HALF)
            parts = [part[modes, part_cols] for part in (s, q, bn, tn, gr, gw)]
            send_a[x * RUN + t * HALVES + half] = jnp.concatenate(parts, axis=0).astype(BF16)


def near_part(t, rate, res, u_ref, g_ref, wtab, vtab, htab, near_c, near_g):
    cols = columns(t)
    lam = rate[:, cols] * (1.0 / SEQ)
    unit = jnp.exp(-lam)
    power = res[:, cols]
    mid = power * jnp.exp(-lam * float(MID))
    powers = []
    for b in range(SUB):
        htab[b] = jnp.broadcast_to(jnp.sum(power, axis=0, keepdims=True), (SUB, TILE)).astype(BF16)
        powers.append(power - mid)
        power = power * unit
    powers.append(power - mid)
    for i in range(SUB // 2):
        for h in range(2):
            modes = slice(h * HALF, (h + 1) * HALF)
            pair = (powers[2 * i + 1][modes], powers[2 * i + 2][modes])
            wtab[h, i, :, cols] = jnp.concatenate(pair, axis=0).astype(BF16)
            pair = (powers[SUB - 1 - 2 * i][modes], powers[SUB - 2 - 2 * i][modes])
            vtab[h, i, :, cols] = jnp.concatenate(pair, axis=0).astype(BF16)
    out_row = iota((SUB, SUB * SUB), 0)
    in_row = iota((SUB, SUB * SUB), 1)
    lag, pos = in_row // SUB, in_row % SUB
    down = jnp.where(pos + lag == out_row, 1.0, 0.0).astype(BF16)
    up = jnp.where(pos - lag == out_row, 1.0, 0.0).astype(BF16)
    for k in range(NSUB):
        rows = slice(k * SUB, (k + 1) * SUB)
        near_c[rows, cols] = dot(down, spread(htab[...], u_ref[rows, cols]))
        near_g[rows, cols] = dot(up, spread(htab[...], g_ref[rows, cols]))


def far_part(t, rate, res, k_in, v_in, go_in, wtab, vtab, sub_s, sub_b, near_c, near_g, recv_c, gq, gk, gv):
    cols = columns(t)
    lam = rate[:, cols] * (1.0 / SEQ)
    step = jnp.exp(-lam * SUB)
    mid = res[:, cols] * jnp.exp(-lam * float(MID))

    def incoming(n):
        rows = slice(n * HALF, (n + 1) * HALF)
        parts = [
            jnp.concatenate([recv_c[x * RUN + t * HALVES + h, rows, :] for x in range(SEGS)], axis=0)
            for h in range(HALVES)
        ]
        return jnp.concatenate(parts, axis=1)

    out_row = iota((2 * SUB, SUB * MODES), 0)
    in_row = iota((2 * SUB, SUB * MODES), 1)
    pick = jnp.where(in_row // HALF == out_row, 1.0, 0.0).astype(BF16)

    def reach(tab, xs):
        sums = []
        bases = []
        for x in xs:
            bases.append(jnp.broadcast_to(jnp.sum(mid * x, axis=0, keepdims=True), (SUB, TILE)))
            low = jnp.concatenate([x[:HALF], x[:HALF]], axis=0).astype(BF16)
            high = jnp.concatenate([x[HALF:], x[HALF:]], axis=0).astype(BF16)
            sums.append((tab[0, :, :, cols] * low[None] + tab[1, :, :, cols] * high[None]).reshape(SUB * HALF, TILE))
        return dot(pick, jnp.concatenate(sums, axis=0)) + jnp.concatenate(bases, axis=0)

    x = incoming(0)
    for k in range(0, NSUB, 2):
        rows = slice(k * SUB, (k + 2) * SUB)
        after = step * x + sub_s[k, :, cols]
        conv = near_c[rows, cols] + reach(wtab, (x, after))
        gq[rows, cols] = (go_in[rows, cols].astype(F32) * conv).astype(BF16)
        x = step * after + sub_s[k + 1, :, cols]
    x = incoming(1)
    for k in reversed(range(0, NSUB, 2)):
        rows = slice(k * SUB, (k + 2) * SUB)
        before = step * x + sub_b[k + 1, :, cols]
        grad = near_g[rows, cols] + reach(vtab, (before, x))
        gk[rows, cols] = (v_in[rows, cols].astype(F32) * grad).astype(BF16)
        gv[rows, cols] = (k_in[rows, cols].astype(F32) * grad).astype(BF16)
        x = step * before + sub_b[k, :, cols]


def main_kernel(
    q_hbm, k_hbm, v_hbm, go_hbm, res_hbm, rate_hbm,
    gq, gk, gv, gres, grate,
    q_in, k_in, v_in, go_in, res, rate, u_ref, g_ref, uf, gf, ptab, btab, wtab, vtab, htab,
    sub_s, sub_b, near_c, near_g,
    send_a, recv_a, pre_s, pre_b, send_m, recv_m, send_x, recv_x, send_c, recv_c, send_e, recv_e,
    in_sem, par_sem, sa, ra, sm, rm, sx, rx, sc, rc, se, re,
):
    me = lax.axis_index("ctx")
    seg = lax.div(me, DEPTH * RUN)
    z = lax.rem(lax.div(me, RUN), DEPTH)
    run = lax.rem(me, RUN)
    y = lax.div(run, 2)
    own = seg * RUN + run
    others = [lax.rem(own + d, GROUP) for d in (12, 4, 11, 5, 13, 3, 10, 6, 14, 2, 9, 7, 8, 15, 1)]
    layers = [lax.rem(z + d, DEPTH) for d in (4, 5, 3, 6, 2, 7, 1)]
    here, column = z * RUN, seg * (DEPTH * RUN) + run

    def member(j):
        return {"ctx": lax.div(j, RUN) * ((DEPTH - 1) * RUN) + here + j}

    def layer(p):
        return {"ctx": column + p * RUN}

    def gray(n):
        return n + lax.div(n, 2) - 2 * lax.div(n, 3)

    def tile_at(n):
        return lax.rem(y + gray(jnp.int32(n)), TILES)

    pairs = ((q_hbm, q_in), (k_hbm, k_in), (v_hbm, v_in), (go_hbm, go_in))

    def load(t, n):
        src, dst = pairs[n]
        return pltpu.make_async_copy(src.at[:, columns(t)], dst.at[:, columns(t)], in_sem.at[t, n])

    params = (
        pltpu.make_async_copy(rate_hbm, rate, par_sem.at[0]),
        pltpu.make_async_copy(res_hbm, res, par_sem.at[1]),
    )
    for cp in params:
        cp.start()
    for n in reversed(range(TILES)):
        for i in range(4):
            load(tile_at(n), i).start()

    barrier = pltpu.get_barrier_semaphore()
    for j in others:
        pl.semaphore_signal(barrier, inc=1, device_id=member(j), device_id_type=MESH)
    for p in layers:
        pl.semaphore_signal(barrier, inc=1, device_id=layer(p), device_id_type=MESH)

    def remote(src, dst, ssem, rsem, target):
        return pltpu.make_async_remote_copy(
            src_ref=src, dst_ref=dst, send_sem=ssem, recv_sem=rsem, device_id=target, device_id_type=MESH
        )

    def arrived(dst, count, rsem):
        part = dst.at[pl.ds(0, count)]
        remote(part, part, sa, rsem, member(others[0])).wait_recv()

    def departed(like, count, ssem):
        part = like.at[pl.ds(0, count)]
        remote(part, part, ssem, ra, member(others[0])).wait_send()

    for cp in params:
        cp.wait()

    @pl.loop(0, TILES)
    def _(t):
        state_tables(t, rate, ptab, btab)

    def tile_states(t):
        cols = columns(t)
        for n in range(4):
            load(t, n).wait()
        u = (k_in[:, cols].astype(F32) * v_in[:, cols].astype(F32)).astype(BF16)
        g = (go_in[:, cols].astype(F32) * q_in[:, cols].astype(F32)).astype(BF16)
        u_ref[:, cols] = u
        g_ref[:, cols] = g
        for half in range(HALVES):
            part = slice(half * LANES, (half + 1) * LANES)
            uf[half] = u[:, part].astype(F32)
            gf[half] = g[:, part].astype(F32)
        states(t, rate, u_ref, g_ref, ptab, btab, uf, gf, sub_s, sub_b, send_a)

    def tile_owners(t):
        return [x * RUN + t * HALVES + half for x in range(SEGS) for half in range(HALVES)]

    def tile_send(t):
        for j in tile_owners(t):

            @pl.when(j != own)
            def _():
                remote(send_a.at[j], recv_a.at[own], sa, ra, member(j)).start()

    @pl.loop(0, 2)
    def _(n):
        tile_states(tile_at(TILES - 1 - n))

    pl.semaphore_wait(barrier, GROUP + DEPTH - 2)
    tile_send(tile_at(3))
    tile_send(tile_at(2))

    @pl.loop(2, TILES)
    def _(n):
        tile_states(tile_at(TILES - 1 - n))
        tile_send(tile_at(TILES - 1 - n))

    recv_a[own] = send_a[own]

    def near(t):
        near_part(t, rate, res, u_ref, g_ref, wtab, vtab, htab, near_c, near_g)

    @pl.loop(0, 2)
    def _(t):
        near(t)

    block = pl.ds(pl.multiple_of(run * LANES, LANES), LANES)
    lam8 = rate[pl.ds(pl.multiple_of(seg * HALF, HALF), HALF), block] * (1.0 / SEQ)
    lam = jnp.concatenate([lam8, lam8], axis=0)
    dec = jnp.exp(-lam * float(ROWS))
    span = float(ROWS * RUN)
    dec_g = jnp.exp(-lam * span)
    ahead = jnp.exp(-lam8 * (span * z.astype(F32)))
    behind = jnp.exp(-lam8 * (span * (DEPTH - 1 - z).astype(F32)))
    decs = [jnp.ones((MODES, LANES), F32)]
    for w in range(1, RUN):
        decs.append(decs[-1] * dec)
    zero = jnp.zeros((MODES, LANES), F32)
    arrived(recv_a, GROUP - 1, ra)

    def combine(carry, part, decay, length):
        s, q, bn, tn, gr, gw, front, dist = carry
        s_j, m_j, b_j, t_j, gr_j, gw_j = part
        db = front * b_j
        return (
            decay * s + s_j,
            decay * (q + length * s) + m_j,
            bn + db,
            tn + front * t_j + dist * db,
            gr + gr_j + b_j * s,
            gw + gw_j + t_j * s + b_j * q,
            front * decay,
            dist + length,
        )

    ones = jnp.ones((MODES, LANES), F32)
    total = (zero, zero, zero, zero, zero, zero, ones, 0.0)
    nears = []
    for w in range(RUN):
        got = [recv_a[x * RUN + w].astype(F32) for x in range(SEGS)]
        part = [
            jnp.concatenate([rows[n * HALF : (n + 1) * HALF] for rows in got], axis=0) for n in range(6)
        ]
        pre_s[w] = total[0]
        nears.append(part[2])
        total = combine(total, part, dec, float(ROWS))
    s, q, bn, tn, gr, gw = total[:6]
    send_m[...] = jnp.concatenate([s, bn], axis=0).astype(BF16)
    early, late = slice(0, HALF), slice(HALF, MODES)
    send_x[...] = jnp.concatenate([q, tn, gr[early] + gr[late], gw[early] + gw[late]], axis=0).astype(BF16)

    for p in layers:
        remote(send_m, recv_m.at[z], sm, rm, layer(p)).start()
    for p in layers:
        remote(send_x, recv_x.at[z], sx, rx, layer(p)).start()
    recv_m[z] = send_m[...]
    recv_x[z] = send_x[...]
    back = zero
    for w in reversed(range(RUN)):
        pre_b[w] = back
        back = dec * back + nears[w]

    @pl.loop(2, TILES)
    def _(t):
        near(t)

    arrived(recv_m, DEPTH - 1, rm)
    state, whole = zero, zero
    for p in range(DEPTH):
        s_p = recv_m[p, 0:MODES, :].astype(F32)
        state = jnp.where(p < z, dec_g * state + s_p, state)
        whole = dec_g * whole + s_p
    state = jnp.concatenate([state[:HALF], state[HALF:] + ahead * whole[:HALF]], axis=0)
    back, whole = zero, zero
    for p in reversed(range(DEPTH)):
        b_p = recv_m[p, MODES : 2 * MODES, :].astype(F32)
        back = jnp.where(p > z, dec_g * back + b_p, back)
        whole = dec_g * whole + b_p
    back = jnp.concatenate([back[:HALF] + behind * whole[HALF:], back[HALF:]], axis=0)

    for w in range(RUN):
        st = pre_s[w] + decs[w] * state
        bk = pre_b[w] + decs[RUN - 1 - w] * back
        for x in range(SEGS):
            rows = slice(x * HALF, (x + 1) * HALF)
            send_c[x * RUN + w] = jnp.concatenate([st[rows], bk[rows]], axis=0)
    for j in others:
        remote(send_c.at[j], recv_c.at[own], sc, rc.at[own], member(j)).start()
    recv_c[own] = send_c[own]

    arrived(recv_x, DEPTH - 1, rx)
    total = (zero, zero, zero, zero, zero, zero, ones, 0.0)
    plain = jnp.zeros((MODES, LANES), F32)
    for p in range(DEPTH):
        states_p = recv_m[p].astype(F32)
        rest = recv_x[p].astype(F32)
        plain = plain + rest[2 * MODES : 3 * MODES]
        part = (states_p[:MODES], rest[:MODES], states_p[MODES:], rest[MODES : 2 * MODES], zero, zero)
        total = combine(total, part, dec_g, span)
    s, q, bn, tn, gr, gw = total[:6]
    gr_all = plain[early] + gr[early] + gr[late] + bn[late] * s[early]
    gw_all = plain[late] + gw[early] + gw[late] + tn[late] * s[early] + bn[late] * q[early]
    send_e[...] = jnp.concatenate([gr_all, gw_all], axis=0).astype(BF16)
    for j in others:
        remote(send_e, recv_e.at[own], se, re, member(j)).start()
    recv_e[own] = send_e[...]

    @pl.loop(0, TILES)
    def _(n):
        t = tile_at(n)
        for j in tile_owners(t):

            @pl.when(j != own)
            def _():
                remote(send_c.at[j], recv_c.at[j], sc, rc.at[j], member(j)).wait_recv()

        far_part(t, rate, res, k_in, v_in, go_in, wtab, vtab, sub_s, sub_b, near_c, near_g, recv_c, gq, gk, gv)

    arrived(recv_e, GROUP - 1, re)
    scale = SEQ ** -0.5
    for w in range(RUN):
        cols = slice(w * LANES, (w + 1) * LANES)
        got = [recv_e[x * RUN + w].astype(F32) for x in range(SEGS)]
        gr, gw = [
            jnp.concatenate([rows[n * HALF : (n + 1) * HALF] for rows in got], axis=0) for n in range(2)
        ]
        gres[:, cols] = scale * gr
        grate[:, cols] = (-scale / SEQ) * res[:, cols] * gw
    departed(recv_a, GROUP - 1, sa)
    departed(recv_m, DEPTH - 1, sm)
    departed(recv_x, DEPTH - 1, sx)
    departed(recv_c, GROUP - 1, sc)
    departed(recv_e, GROUP - 1, se)


def store_kernel(*refs):
    srcs, dsts, sem = refs[:5], refs[5:10], refs[10]
    copies = [pltpu.make_async_copy(s, d, sem.at[n]) for n, (s, d) in enumerate(zip(srcs, dsts))]
    for cp in copies:
        cp.start()
    for cp in copies:
        cp.wait()


def local(query, key_in, value, grad_out, residue, rate):
    hbm = pl.BlockSpec(memory_space=pltpu.HBM)
    vmem = pl.BlockSpec(memory_space=pltpu.VMEM)
    big = jax.ShapeDtypeStruct((ROWS, CHANS), BF16)
    small = jax.ShapeDtypeStruct((MODES, CHANS), F32)
    dma = pltpu.SemaphoreType.DMA

    def buf(*shape, dtype=F32):
        return pltpu.VMEM(shape, dtype)

    held = [pltpu.VMEM((ROWS, CHANS), BF16)] * 3 + [pltpu.VMEM((MODES, CHANS), F32)] * 2
    args = [pltpu.with_memory_space_constraint(x, pltpu.HBM) for x in (query, key_in, value, grad_out, residue, rate)]
    results = pl.pallas_call(
        main_kernel,
        out_shape=held,
        in_specs=[hbm] * 6,
        out_specs=[vmem] * 5,
        scratch_shapes=[
            *[buf(ROWS, CHANS, dtype=BF16)] * 4,
            *[buf(MODES, CHANS)] * 2,
            *[buf(ROWS, CHANS, dtype=BF16)] * 2,
            *[buf(HALVES, ROWS, LANES)] * 2,
            *[buf(MODES, SUB, CHANS, dtype=BF16)] * 2,
            *[buf(SEGS, SUB // 2, 2 * HALF, CHANS, dtype=BF16)] * 2,
            buf(SUB, SUB, TILE, dtype=BF16),
            *[buf(NSUB, MODES, CHANS)] * 2,
            *[buf(ROWS, CHANS)] * 2,
            *[buf(GROUP, 6 * HALF, LANES, dtype=BF16)] * 2,
            *[buf(RUN, MODES, LANES)] * 2,
            buf(2 * MODES, LANES, dtype=BF16), buf(DEPTH, 2 * MODES, LANES, dtype=BF16),
            buf(3 * MODES, LANES, dtype=BF16), buf(DEPTH, 3 * MODES, LANES, dtype=BF16),
            *[buf(GROUP, 2 * HALF, LANES)] * 2,
            buf(2 * HALF, LANES, dtype=BF16), buf(GROUP, 2 * HALF, LANES, dtype=BF16),
            dma((TILES, 4)), dma((2,)),
            dma, dma, dma, dma, dma, dma, dma, dma((GROUP,)), dma, dma,
        ],
        compiler_params=pltpu.CompilerParams(collective_id=0, has_side_effects=True, vmem_limit_bytes=VMEM_LIMIT),
        name="hyena",
    )(*args)

    return pl.pallas_call(
        store_kernel,
        out_shape=(big, big, big, small, small),
        in_specs=[vmem] * 5,
        out_specs=[hbm] * 5,
        scratch_shapes=[dma((5,))],
        compiler_params=pltpu.CompilerParams(vmem_limit_bytes=8 * 2**20),
        name="store",
    )(*[pltpu.with_memory_space_constraint(x, pltpu.VMEM) for x in results])


def solution(mesh):
    big, small = P("ctx", "tp"), P(None, "tp")
    return jax.shard_map(
        local, mesh=mesh, in_specs=(big, big, big, big, small, small),
        out_specs=(big, big, big, small, small), check_vma=False,
    )
```

```python
import jax
import jax.numpy as jnp
from jax import lax
from jax.experimental import pallas as pl
from jax.experimental.pallas import tpu as pltpu
from jax.sharding import PartitionSpec as P

SEQ = 32768
MODES = 16
ROWS = 256
CHANS = 1024
SUB = 16
NSUB = ROWS // SUB
MID = 8
LANES = 128
TILE = 256
TILES = CHANS // TILE
HALVES = TILE // LANES
RUN = 8
SEGS = 2
DEPTH = 8
GROUP = SEGS * RUN
HALF = MODES // SEGS
VMEM_LIMIT = 40 * 2**20
F32 = jnp.float32
BF16 = jnp.bfloat16
MESH = pl.DeviceIdType.MESH


def iota(shape, dim):
    return lax.broadcasted_iota(jnp.int32, shape, dim)


def dot(a, b):
    return jnp.dot(a, b, preferred_element_type=F32)


def columns(t):
    return pl.ds(pl.multiple_of(t * TILE, TILE), TILE)


def spread(tab, val):
    return (tab * val[None]).reshape(tab.shape[0] * tab.shape[1], TILE)


def state_tables(t, rate, ptab, btab):
    cols = columns(t)
    pos = iota((SUB, TILE), 0).astype(F32)
    lam = rate[:, cols] * (1.0 / SEQ)
    for m in range(MODES):
        row = lam[m : m + 1, :]
        ptab[m, :, cols] = jnp.exp(-row * (SUB - 1.0 - pos)).astype(BF16)
        btab[m, :, cols] = jnp.exp(-row * (pos + 1.0)).astype(BF16)


def states(t, rate, u_ref, g_ref, ptab, btab, uf, gf, sub_s, sub_b, send_a):
    cols = columns(t)
    lam = rate[:, cols] * (1.0 / SEQ)
    out_row = iota((2 * MODES, MODES * SUB), 0)
    in_row = iota((2 * MODES, MODES * SUB), 1)
    hit = (in_row // SUB) == (out_row % MODES)
    off = (in_row % SUB).astype(F32)
    first = out_row < MODES
    sel_s = jnp.where(hit, jnp.where(first, 1.0, SUB - 1.0 - off), 0.0).astype(BF16)
    sel_b = jnp.where(hit, jnp.where(first, 1.0, off + 1.0), 0.0).astype(BF16)
    step = jnp.exp(-lam * SUB)
    zero = jnp.zeros((MODES, TILE), F32)
    s, q, bn, tn, gr, gw = zero, zero, zero, zero, zero, zero
    decay = jnp.ones((MODES, TILE), F32)
    for k in range(NSUB):
        rows = slice(k * SUB, (k + 1) * SUB)
        su = dot(sel_s, spread(ptab[:, :, cols], u_ref[rows, cols]))
        sg = dot(sel_b, spread(btab[:, :, cols], g_ref[rows, cols]))
        s_k, m_k = su[:MODES], su[MODES:]
        b_k, t_k = sg[:MODES], sg[MODES:]
        sub_s[k, :, cols] = s_k
        sub_b[k, :, cols] = b_k
        gr = gr + b_k * s
        gw = gw + t_k * s + b_k * q
        q = step * (q + float(SUB) * s) + m_k
        s = step * s + s_k
        db = decay * b_k
        bn = bn + db
        tn = tn + decay * t_k + float(k * SUB) * db
        decay = decay * step
    halves = []
    for half in range(HALVES):
        acc = [jnp.zeros((8, LANES), F32) for _ in range(SUB)]
        for octet in range(NSUB // 8):
            us = [uf[half, pl.ds(octet * 8 * SUB + b, 8, stride=SUB), :] for b in range(SUB)]
            for b in range(SUB):
                gb = gf[half, pl.ds(octet * 8 * SUB + b, 8, stride=SUB), :]
                for lag in range(b + 1):
                    acc[lag] = acc[lag] + gb * us[b - lag]
        halves.append([jnp.sum(a, axis=0, keepdims=True) for a in acc])
    unit = jnp.exp(-lam)
    power = jnp.ones((MODES, TILE), F32)
    for lag in range(SUB):
        term = jnp.concatenate([h[lag] for h in halves], axis=1) * power
        gr = gr + term
        gw = gw + float(lag) * term
        power = power * unit
    for half in range(HALVES):
        part_cols = slice(half * LANES, (half + 1) * LANES)
        for x in range(SEGS):
            modes = slice(x * HALF, (x + 1) * HALF)
            parts = [part[modes, part_cols] for part in (s, q, bn, tn, gr, gw)]
            send_a[x * RUN + t * HALVES + half] = jnp.concatenate(parts, axis=0).astype(BF16)


def near_part(t, rate, res, u_ref, g_ref, wtab, vtab, htab, near_c, near_g):
    cols = columns(t)
    lam = rate[:, cols] * (1.0 / SEQ)
    unit = jnp.exp(-lam)
    power = res[:, cols]
    mid = power * jnp.exp(-lam * float(MID))
    powers = []
    for b in range(SUB):
        htab[b] = jnp.broadcast_to(jnp.sum(power, axis=0, keepdims=True), (SUB, TILE)).astype(BF16)
        powers.append(power - mid)
        power = power * unit
    powers.append(power - mid)
    for i in range(SUB // 2):
        for h in range(2):
            modes = slice(h * HALF, (h + 1) * HALF)
            pair = (powers[2 * i + 1][modes], powers[2 * i + 2][modes])
            wtab[h, i, :, cols] = jnp.concatenate(pair, axis=0).astype(BF16)
            pair = (powers[SUB - 1 - 2 * i][modes], powers[SUB - 2 - 2 * i][modes])
            vtab[h, i, :, cols] = jnp.concatenate(pair, axis=0).astype(BF16)
    out_row = iota((SUB, SUB * SUB), 0)
    in_row = iota((SUB, SUB * SUB), 1)
    lag, pos = in_row // SUB, in_row % SUB
    down = jnp.where(pos + lag == out_row, 1.0, 0.0).astype(BF16)
    up = jnp.where(pos - lag == out_row, 1.0, 0.0).astype(BF16)
    for k in range(NSUB):
        rows = slice(k * SUB, (k + 1) * SUB)
        near_c[rows, cols] = dot(down, spread(htab[...], u_ref[rows, cols]))
        near_g[rows, cols] = dot(up, spread(htab[...], g_ref[rows, cols]))


def far_part(t, rate, res, k_in, v_in, go_in, wtab, vtab, sub_s, sub_b, near_c, near_g, recv_c, gq, gk, gv):
    cols = columns(t)
    lam = rate[:, cols] * (1.0 / SEQ)
    step = jnp.exp(-lam * SUB)
    mid = res[:, cols] * jnp.exp(-lam * float(MID))

    def incoming(n):
        rows = slice(n * HALF, (n + 1) * HALF)
        parts = [
            jnp.concatenate([recv_c[x * RUN + t * HALVES + h].astype(F32)[rows] for x in range(SEGS)], axis=0)
            for h in range(HALVES)
        ]
        return jnp.concatenate(parts, axis=1)

    out_row = iota((2 * SUB, SUB * MODES), 0)
    in_row = iota((2 * SUB, SUB * MODES), 1)
    pick = jnp.where(in_row // HALF == out_row, 1.0, 0.0).astype(BF16)

    def reach(tab, xs):
        sums = []
        bases = []
        for x in xs:
            bases.append(jnp.broadcast_to(jnp.sum(mid * x, axis=0, keepdims=True), (SUB, TILE)))
            low = jnp.concatenate([x[:HALF], x[:HALF]], axis=0).astype(BF16)
            high = jnp.concatenate([x[HALF:], x[HALF:]], axis=0).astype(BF16)
            sums.append((tab[0, :, :, cols] * low[None] + tab[1, :, :, cols] * high[None]).reshape(SUB * HALF, TILE))
        return dot(pick, jnp.concatenate(sums, axis=0)) + jnp.concatenate(bases, axis=0)

    x = incoming(0)
    for k in range(0, NSUB, 2):
        rows = slice(k * SUB, (k + 2) * SUB)
        after = step * x + sub_s[k, :, cols]
        conv = near_c[rows, cols] + reach(wtab, (x, after))
        gq[rows, cols] = (go_in[rows, cols].astype(F32) * conv).astype(BF16)
        x = step * after + sub_s[k + 1, :, cols]
    x = incoming(1)
    for k in reversed(range(0, NSUB, 2)):
        rows = slice(k * SUB, (k + 2) * SUB)
        before = step * x + sub_b[k + 1, :, cols]
        grad = near_g[rows, cols] + reach(vtab, (before, x))
        gk[rows, cols] = (v_in[rows, cols].astype(F32) * grad).astype(BF16)
        gv[rows, cols] = (k_in[rows, cols].astype(F32) * grad).astype(BF16)
        x = step * before + sub_b[k, :, cols]


def main_kernel(
    q_hbm, k_hbm, v_hbm, go_hbm, res_hbm, rate_hbm,
    gq, gk, gv, gres, grate,
    q_in, k_in, v_in, go_in, res, rate, u_ref, g_ref, uf, gf, ptab, btab, wtab, vtab, htab,
    sub_s, sub_b, near_c, near_g,
    send_a, recv_a, pre_s, pre_b, send_m, recv_m, send_x, recv_x, send_c, recv_c, send_e, recv_e,
    in_sem, par_sem, sa, ra, sm, rm, sx, rx, sc, rc, se, re,
):
    me = lax.axis_index("ctx")
    seg = lax.div(me, DEPTH * RUN)
    z = lax.rem(lax.div(me, RUN), DEPTH)
    run = lax.rem(me, RUN)
    y = lax.div(run, 2)
    own = seg * RUN + run
    others = [lax.rem(own + d, GROUP) for d in (12, 4, 11, 5, 13, 3, 10, 6, 14, 2, 9, 7, 8, 15, 1)]
    layers = [lax.rem(z + d, DEPTH) for d in (4, 5, 3, 6, 2, 7, 1)]
    here, column = z * RUN, seg * (DEPTH * RUN) + run

    def member(j):
        return {"ctx": lax.div(j, RUN) * ((DEPTH - 1) * RUN) + here + j}

    def layer(p):
        return {"ctx": column + p * RUN}

    def gray(n):
        return n + lax.div(n, 2) - 2 * lax.div(n, 3)

    def tile_at(n):
        return lax.rem(y + gray(jnp.int32(n)), TILES)

    pairs = ((q_hbm, q_in), (k_hbm, k_in), (v_hbm, v_in), (go_hbm, go_in))

    def load(t, n):
        src, dst = pairs[n]
        return pltpu.make_async_copy(src.at[:, columns(t)], dst.at[:, columns(t)], in_sem.at[t, n])

    params = (
        pltpu.make_async_copy(rate_hbm, rate, par_sem.at[0]),
        pltpu.make_async_copy(res_hbm, res, par_sem.at[1]),
    )
    for cp in params:
        cp.start()
    for n in reversed(range(TILES)):
        for i in range(4):
            load(tile_at(n), i).start()

    barrier = pltpu.get_barrier_semaphore()
    for j in others:
        pl.semaphore_signal(barrier, inc=1, device_id=member(j), device_id_type=MESH)
    for p in layers:
        pl.semaphore_signal(barrier, inc=1, device_id=layer(p), device_id_type=MESH)

    def remote(src, dst, ssem, rsem, target):
        return pltpu.make_async_remote_copy(
            src_ref=src, dst_ref=dst, send_sem=ssem, recv_sem=rsem, device_id=target, device_id_type=MESH
        )

    def arrived(dst, count, rsem):
        part = dst.at[pl.ds(0, count)]
        remote(part, part, sa, rsem, member(others[0])).wait_recv()

    def departed(like, count, ssem):
        part = like.at[pl.ds(0, count)]
        remote(part, part, ssem, ra, member(others[0])).wait_send()

    for cp in params:
        cp.wait()

    @pl.loop(0, TILES)
    def _(t):
        state_tables(t, rate, ptab, btab)

    def tile_states(t):
        cols = columns(t)
        for n in range(4):
            load(t, n).wait()
        u = (k_in[:, cols].astype(F32) * v_in[:, cols].astype(F32)).astype(BF16)
        g = (go_in[:, cols].astype(F32) * q_in[:, cols].astype(F32)).astype(BF16)
        u_ref[:, cols] = u
        g_ref[:, cols] = g
        for half in range(HALVES):
            part = slice(half * LANES, (half + 1) * LANES)
            uf[half] = u[:, part].astype(F32)
            gf[half] = g[:, part].astype(F32)
        states(t, rate, u_ref, g_ref, ptab, btab, uf, gf, sub_s, sub_b, send_a)

    def tile_owners(t):
        return [x * RUN + t * HALVES + half for x in (1 - seg, seg) for half in range(HALVES)]

    def tile_send(t):
        for j in tile_owners(t):

            @pl.when(j != own)
            def _():
                remote(send_a.at[j], recv_a.at[own], sa, ra, member(j)).start()

    @pl.loop(0, 2)
    def _(n):
        tile_states(tile_at(TILES - 1 - n))

    pl.semaphore_wait(barrier, GROUP + DEPTH - 2)
    tile_send(tile_at(3))
    tile_send(tile_at(2))

    @pl.loop(2, TILES)
    def _(n):
        tile_states(tile_at(TILES - 1 - n))
        tile_send(tile_at(TILES - 1 - n))

    recv_a[own] = send_a[own]

    def near(t):
        near_part(t, rate, res, u_ref, g_ref, wtab, vtab, htab, near_c, near_g)

    @pl.loop(0, 2)
    def _(t):
        near(t)

    block = pl.ds(pl.multiple_of(run * LANES, LANES), LANES)
    lam8 = rate[pl.ds(pl.multiple_of(seg * HALF, HALF), HALF), block] * (1.0 / SEQ)
    lam = jnp.concatenate([lam8, lam8], axis=0)
    dec = jnp.exp(-lam * float(ROWS))
    span = float(ROWS * RUN)
    dec_g = jnp.exp(-lam * span)
    ahead = jnp.exp(-lam8 * (span * z.astype(F32)))
    behind = jnp.exp(-lam8 * (span * (DEPTH - 1 - z).astype(F32)))
    decs = [jnp.ones((MODES, LANES), F32)]
    for w in range(1, RUN):
        decs.append(decs[-1] * dec)
    zero = jnp.zeros((MODES, LANES), F32)
    arrived(recv_a, GROUP - 1, ra)

    def combine(carry, part, decay, length):
        s, q, bn, tn, gr, gw, front, dist = carry
        s_j, m_j, b_j, t_j, gr_j, gw_j = part
        db = front * b_j
        return (
            decay * s + s_j,
            decay * (q + length * s) + m_j,
            bn + db,
            tn + front * t_j + dist * db,
            gr + gr_j + b_j * s,
            gw + gw_j + t_j * s + b_j * q,
            front * decay,
            dist + length,
        )

    ones = jnp.ones((MODES, LANES), F32)
    s, bn = zero, zero
    for w in range(RUN):
        pre_s[w] = s
        last = RUN - 1 - w
        pre_b[last] = bn
        s = dec * s + jnp.concatenate([recv_a[x * RUN + w].astype(F32)[0:HALF] for x in range(SEGS)], axis=0)
        near_b = [recv_a[x * RUN + last].astype(F32)[2 * HALF : 3 * HALF] for x in range(SEGS)]
        bn = dec * bn + jnp.concatenate(near_b, axis=0)
    send_m[...] = jnp.concatenate([s, bn], axis=0).astype(BF16)
    for p in layers:
        remote(send_m, recv_m.at[z], sm, rm, layer(p)).start()
    total = (zero, zero, zero, zero, zero, zero, ones, 0.0)
    for w in range(RUN):
        got = [recv_a[x * RUN + w].astype(F32) for x in range(SEGS)]
        part = [
            jnp.concatenate([rows[n * HALF : (n + 1) * HALF] for rows in got], axis=0) for n in range(6)
        ]
        total = combine(total, part, dec, float(ROWS))
    s, q, bn, tn, gr, gw = total[:6]
    early, late = slice(0, HALF), slice(HALF, MODES)
    send_x[...] = jnp.concatenate([q, tn, gr[early] + gr[late], gw[early] + gw[late]], axis=0).astype(BF16)

    for p in layers:
        remote(send_x, recv_x.at[z], sx, rx, layer(p)).start()
    recv_m[z] = send_m[...]
    recv_x[z] = send_x[...]

    @pl.loop(2, TILES)
    def _(t):
        near(t)

    arrived(recv_m, DEPTH - 1, rm)
    state, whole = zero, zero
    for p in range(DEPTH):
        s_p = recv_m[p, 0:MODES, :].astype(F32)
        state = jnp.where(p < z, dec_g * state + s_p, state)
        whole = dec_g * whole + s_p
    state = jnp.concatenate([state[:HALF], state[HALF:] + ahead * whole[:HALF]], axis=0)
    back, whole = zero, zero
    for p in reversed(range(DEPTH)):
        b_p = recv_m[p, MODES : 2 * MODES, :].astype(F32)
        back = jnp.where(p > z, dec_g * back + b_p, back)
        whole = dec_g * whole + b_p
    back = jnp.concatenate([back[:HALF] + behind * whole[HALF:], back[HALF:]], axis=0)

    for w in range(RUN):
        st = pre_s[w] + decs[w] * state
        bk = pre_b[w] + decs[RUN - 1 - w] * back
        for x in range(SEGS):
            rows = slice(x * HALF, (x + 1) * HALF)
            send_c[x * RUN + w] = jnp.concatenate([st[rows], bk[rows]], axis=0).astype(BF16)
    for j in others:
        remote(send_c.at[j], recv_c.at[own], sc, rc.at[own], member(j)).start()
    recv_c[own] = send_c[own]

    arrived(recv_x, DEPTH - 1, rx)
    total = (zero, zero, zero, zero, zero, zero, ones, 0.0)
    plain = jnp.zeros((MODES, LANES), F32)
    for p in range(DEPTH):
        states_p = recv_m[p].astype(F32)
        rest = recv_x[p].astype(F32)
        plain = plain + rest[2 * MODES : 3 * MODES]
        part = (states_p[:MODES], rest[:MODES], states_p[MODES:], rest[MODES : 2 * MODES], zero, zero)
        total = combine(total, part, dec_g, span)
    s, q, bn, tn, gr, gw = total[:6]
    gr_all = plain[early] + gr[early] + gr[late] + bn[late] * s[early]
    gw_all = plain[late] + gw[early] + gw[late] + tn[late] * s[early] + bn[late] * q[early]
    send_e[...] = jnp.concatenate([gr_all, gw_all], axis=0).astype(BF16)
    for j in others:
        remote(send_e, recv_e.at[own], se, re, member(j)).start()
    recv_e[own] = send_e[...]

    @pl.loop(0, TILES)
    def _(n):
        t = tile_at(n)
        for j in tile_owners(t):

            @pl.when(j != own)
            def _():
                remote(send_c.at[j], recv_c.at[j], sc, rc.at[j], member(j)).wait_recv()

        far_part(t, rate, res, k_in, v_in, go_in, wtab, vtab, sub_s, sub_b, near_c, near_g, recv_c, gq, gk, gv)

    arrived(recv_e, GROUP - 1, re)
    scale = SEQ ** -0.5
    for w in range(RUN):
        cols = slice(w * LANES, (w + 1) * LANES)
        got = [recv_e[x * RUN + w].astype(F32) for x in range(SEGS)]
        gr, gw = [
            jnp.concatenate([rows[n * HALF : (n + 1) * HALF] for rows in got], axis=0) for n in range(2)
        ]
        gres[:, cols] = scale * gr
        grate[:, cols] = (-scale / SEQ) * res[:, cols] * gw
    departed(recv_a, GROUP - 1, sa)
    departed(recv_m, DEPTH - 1, sm)
    departed(recv_x, DEPTH - 1, sx)
    departed(recv_c, GROUP - 1, sc)
    departed(recv_e, GROUP - 1, se)


def store_kernel(*refs):
    srcs, dsts, sem = refs[:5], refs[5:10], refs[10]
    copies = [pltpu.make_async_copy(s, d, sem.at[n]) for n, (s, d) in enumerate(zip(srcs, dsts))]
    for cp in copies:
        cp.start()
    for cp in copies:
        cp.wait()


def local(query, key_in, value, grad_out, residue, rate):
    hbm = pl.BlockSpec(memory_space=pltpu.HBM)
    vmem = pl.BlockSpec(memory_space=pltpu.VMEM)
    big = jax.ShapeDtypeStruct((ROWS, CHANS), BF16)
    small = jax.ShapeDtypeStruct((MODES, CHANS), F32)
    dma = pltpu.SemaphoreType.DMA

    def buf(*shape, dtype=F32):
        return pltpu.VMEM(shape, dtype)

    held = [pltpu.VMEM((ROWS, CHANS), BF16)] * 3 + [pltpu.VMEM((MODES, CHANS), F32)] * 2
    args = [pltpu.with_memory_space_constraint(x, pltpu.HBM) for x in (query, key_in, value, grad_out, residue, rate)]
    results = pl.pallas_call(
        main_kernel,
        out_shape=held,
        in_specs=[hbm] * 6,
        out_specs=[vmem] * 5,
        scratch_shapes=[
            *[buf(ROWS, CHANS, dtype=BF16)] * 4,
            *[buf(MODES, CHANS)] * 2,
            *[buf(ROWS, CHANS, dtype=BF16)] * 2,
            *[buf(HALVES, ROWS, LANES)] * 2,
            *[buf(MODES, SUB, CHANS, dtype=BF16)] * 2,
            *[buf(SEGS, SUB // 2, 2 * HALF, CHANS, dtype=BF16)] * 2,
            buf(SUB, SUB, TILE, dtype=BF16),
            *[buf(NSUB, MODES, CHANS)] * 2,
            *[buf(ROWS, CHANS)] * 2,
            *[buf(GROUP, 6 * HALF, LANES, dtype=BF16)] * 2,
            *[buf(RUN, MODES, LANES)] * 2,
            buf(2 * MODES, LANES, dtype=BF16), buf(DEPTH, 2 * MODES, LANES, dtype=BF16),
            buf(3 * MODES, LANES, dtype=BF16), buf(DEPTH, 3 * MODES, LANES, dtype=BF16),
            *[buf(GROUP, 2 * HALF, LANES, dtype=BF16)] * 2,
            buf(2 * HALF, LANES, dtype=BF16), buf(GROUP, 2 * HALF, LANES, dtype=BF16),
            dma((TILES, 4)), dma((2,)),
            dma, dma, dma, dma, dma, dma, dma, dma((GROUP,)), dma, dma,
        ],
        compiler_params=pltpu.CompilerParams(collective_id=0, has_side_effects=True, vmem_limit_bytes=VMEM_LIMIT),
        name="hyena",
    )(*args)

    return pl.pallas_call(
        store_kernel,
        out_shape=(big, big, big, small, small),
        in_specs=[vmem] * 5,
        out_specs=[hbm] * 5,
        scratch_shapes=[dma((5,))],
        compiler_params=pltpu.CompilerParams(vmem_limit_bytes=8 * 2**20),
        name="store",
    )(*[pltpu.with_memory_space_constraint(x, pltpu.VMEM) for x in results])


def solution(mesh):
    big, small = P("ctx", "tp"), P(None, "tp")
    return jax.shard_map(
        local, mesh=mesh, in_specs=(big, big, big, big, small, small),
        out_specs=(big, big, big, small, small), check_vma=False,
    )
```

```python
import jax
import jax.numpy as jnp
from jax import lax
from jax.experimental import pallas as pl
from jax.experimental.pallas import tpu as pltpu
from jax.sharding import PartitionSpec as P

SEQ = 32768
MODES = 16
ROWS = 256
CHANS = 1024
SUB = 16
NSUB = ROWS // SUB
MID = 8
LANES = 128
TILE = 256
TILES = CHANS // TILE
HALVES = TILE // LANES
RUN = 8
SEGS = 2
DEPTH = 8
GROUP = SEGS * RUN
HALF = MODES // SEGS
VMEM_LIMIT = 40 * 2**20
F32 = jnp.float32
BF16 = jnp.bfloat16
MESH = pl.DeviceIdType.MESH


def iota(shape, dim):
    return lax.broadcasted_iota(jnp.int32, shape, dim)


def dot(a, b):
    return jnp.dot(a, b, preferred_element_type=F32)


def columns(t):
    return pl.ds(pl.multiple_of(t * TILE, TILE), TILE)


def spread(tab, val):
    return (tab * val[None]).reshape(tab.shape[0] * tab.shape[1], TILE)


def state_tables(t, rate, ptab, btab):
    cols = columns(t)
    pos = iota((SUB, TILE), 0).astype(F32)
    lam = rate[:, cols] * (1.0 / SEQ)
    for m in range(MODES):
        row = lam[m : m + 1, :]
        ptab[m, :, cols] = jnp.exp(-row * (SUB - 1.0 - pos)).astype(BF16)
        btab[m, :, cols] = jnp.exp(-row * (pos + 1.0)).astype(BF16)


def states(t, rate, u_ref, g_ref, ptab, btab, uf, gf, sub_s, sub_b, send_a):
    cols = columns(t)
    lam = rate[:, cols] * (1.0 / SEQ)
    out_row = iota((2 * MODES, MODES * SUB), 0)
    in_row = iota((2 * MODES, MODES * SUB), 1)
    hit = (in_row // SUB) == (out_row % MODES)
    off = (in_row % SUB).astype(F32)
    first = out_row < MODES
    sel_s = jnp.where(hit, jnp.where(first, 1.0, SUB - 1.0 - off), 0.0).astype(BF16)
    sel_b = jnp.where(hit, jnp.where(first, 1.0, off + 1.0), 0.0).astype(BF16)
    step = jnp.exp(-lam * SUB)
    zero = jnp.zeros((MODES, TILE), F32)
    s, q, bn, tn, gr, gw = zero, zero, zero, zero, zero, zero
    decay = jnp.ones((MODES, TILE), F32)
    for k in range(NSUB):
        rows = slice(k * SUB, (k + 1) * SUB)
        su = dot(sel_s, spread(ptab[:, :, cols], u_ref[rows, cols]))
        sg = dot(sel_b, spread(btab[:, :, cols], g_ref[rows, cols]))
        s_k, m_k = su[:MODES], su[MODES:]
        b_k, t_k = sg[:MODES], sg[MODES:]
        sub_s[k, :, cols] = s_k
        sub_b[k, :, cols] = b_k
        gr = gr + b_k * s
        gw = gw + t_k * s + b_k * q
        q = step * (q + float(SUB) * s) + m_k
        s = step * s + s_k
        db = decay * b_k
        bn = bn + db
        tn = tn + decay * t_k + float(k * SUB) * db
        decay = decay * step
    halves = []
    for half in range(HALVES):
        acc = [jnp.zeros((8, LANES), F32) for _ in range(SUB)]
        for octet in range(NSUB // 8):
            us = [uf[half, pl.ds(octet * 8 * SUB + b, 8, stride=SUB), :] for b in range(SUB)]
            for b in range(SUB):
                gb = gf[half, pl.ds(octet * 8 * SUB + b, 8, stride=SUB), :]
                for lag in range(b + 1):
                    acc[lag] = acc[lag] + gb * us[b - lag]
        halves.append([jnp.sum(a, axis=0, keepdims=True) for a in acc])
    unit = jnp.exp(-lam)
    power = jnp.ones((MODES, TILE), F32)
    for lag in range(SUB):
        term = jnp.concatenate([h[lag] for h in halves], axis=1) * power
        gr = gr + term
        gw = gw + float(lag) * term
        power = power * unit
    for half in range(HALVES):
        part_cols = slice(half * LANES, (half + 1) * LANES)
        for x in range(SEGS):
            modes = slice(x * HALF, (x + 1) * HALF)
            parts = [part[modes, part_cols] for part in (s, q, bn, tn, gr, gw)]
            send_a[x * RUN + t * HALVES + half] = jnp.concatenate(parts, axis=0).astype(BF16)


def near_part(t, rate, res, u_ref, g_ref, wtab, vtab, htab, near_c, near_g):
    cols = columns(t)
    lam = rate[:, cols] * (1.0 / SEQ)
    unit = jnp.exp(-lam)
    power = res[:, cols]
    mid = power * jnp.exp(-lam * float(MID))
    powers = []
    for b in range(SUB):
        htab[b] = jnp.broadcast_to(jnp.sum(power, axis=0, keepdims=True), (SUB, TILE)).astype(BF16)
        powers.append(power - mid)
        power = power * unit
    powers.append(power - mid)
    for i in range(SUB // 2):
        for h in range(2):
            modes = slice(h * HALF, (h + 1) * HALF)
            pair = (powers[2 * i + 1][modes], powers[2 * i + 2][modes])
            wtab[h, i, :, cols] = jnp.concatenate(pair, axis=0).astype(BF16)
            pair = (powers[SUB - 1 - 2 * i][modes], powers[SUB - 2 - 2 * i][modes])
            vtab[h, i, :, cols] = jnp.concatenate(pair, axis=0).astype(BF16)
    out_row = iota((SUB, SUB * SUB), 0)
    in_row = iota((SUB, SUB * SUB), 1)
    lag, pos = in_row // SUB, in_row % SUB
    down = jnp.where(pos + lag == out_row, 1.0, 0.0).astype(BF16)
    up = jnp.where(pos - lag == out_row, 1.0, 0.0).astype(BF16)
    for k in range(NSUB):
        rows = slice(k * SUB, (k + 1) * SUB)
        near_c[rows, cols] = dot(down, spread(htab[...], u_ref[rows, cols]))
        near_g[rows, cols] = dot(up, spread(htab[...], g_ref[rows, cols]))


def far_part(t, rate, res, k_in, v_in, go_in, wtab, vtab, sub_s, sub_b, near_c, near_g, recv_c, gq, gk, gv):
    cols = columns(t)
    lam = rate[:, cols] * (1.0 / SEQ)
    step = jnp.exp(-lam * SUB)
    mid = res[:, cols] * jnp.exp(-lam * float(MID))

    def incoming(n):
        rows = slice(n * HALF, (n + 1) * HALF)
        parts = [
            jnp.concatenate([recv_c[x * RUN + t * HALVES + h].astype(F32)[rows] for x in range(SEGS)], axis=0)
            for h in range(HALVES)
        ]
        return jnp.concatenate(parts, axis=1)

    out_row = iota((2 * SUB, SUB * MODES), 0)
    in_row = iota((2 * SUB, SUB * MODES), 1)
    pick = jnp.where(in_row // HALF == out_row, 1.0, 0.0).astype(BF16)

    def reach(tab, xs):
        sums = []
        bases = []
        for x in xs:
            bases.append(jnp.broadcast_to(jnp.sum(mid * x, axis=0, keepdims=True), (SUB, TILE)))
            low = jnp.concatenate([x[:HALF], x[:HALF]], axis=0).astype(BF16)
            high = jnp.concatenate([x[HALF:], x[HALF:]], axis=0).astype(BF16)
            sums.append((tab[0, :, :, cols] * low[None] + tab[1, :, :, cols] * high[None]).reshape(SUB * HALF, TILE))
        return dot(pick, jnp.concatenate(sums, axis=0)) + jnp.concatenate(bases, axis=0)

    x = incoming(0)
    for k in range(0, NSUB, 2):
        rows = slice(k * SUB, (k + 2) * SUB)
        after = step * x + sub_s[k, :, cols]
        conv = near_c[rows, cols] + reach(wtab, (x, after))
        gq[rows, cols] = (go_in[rows, cols].astype(F32) * conv).astype(BF16)
        x = step * after + sub_s[k + 1, :, cols]
    x = incoming(1)
    for k in reversed(range(0, NSUB, 2)):
        rows = slice(k * SUB, (k + 2) * SUB)
        before = step * x + sub_b[k + 1, :, cols]
        grad = near_g[rows, cols] + reach(vtab, (before, x))
        gk[rows, cols] = (v_in[rows, cols].astype(F32) * grad).astype(BF16)
        gv[rows, cols] = (k_in[rows, cols].astype(F32) * grad).astype(BF16)
        x = step * before + sub_b[k, :, cols]


def main_kernel(
    q_hbm, k_hbm, v_hbm, go_hbm, res_hbm, rate_hbm,
    gq, gk, gv, gres, grate,
    q_in, k_in, v_in, go_in, res, rate, u_ref, g_ref, uf, gf, ptab, btab, wtab, vtab, htab,
    sub_s, sub_b, near_c, near_g,
    send_a, recv_a, pre_s, pre_b, send_m, recv_m, send_x, recv_x, send_c, recv_c, send_e, recv_e,
    in_sem, par_sem, sa, ra, sm, rm, sx, rx, sc, rc, se, re,
):
    me = lax.axis_index("ctx")
    seg = lax.div(me, DEPTH * RUN)
    z = lax.rem(lax.div(me, RUN), DEPTH)
    run = lax.rem(me, RUN)
    y = lax.div(run, 2)
    own = seg * RUN + run
    others = [lax.rem(own + d, GROUP) for d in (12, 4, 11, 5, 13, 3, 10, 6, 14, 2, 9, 7, 8, 15, 1)]
    layers = [lax.rem(z + d, DEPTH) for d in (4, 5, 3, 6, 2, 7, 1)]
    here, column = z * RUN, seg * (DEPTH * RUN) + run

    def member(j):
        return {"ctx": lax.div(j, RUN) * ((DEPTH - 1) * RUN) + here + j}

    def layer(p):
        return {"ctx": column + p * RUN}

    def gray(n):
        return n + lax.div(n, 2) - 2 * lax.div(n, 3)

    def tile_at(n):
        return lax.rem(y + gray(jnp.int32(n)), TILES)

    pairs = ((q_hbm, q_in), (k_hbm, k_in), (v_hbm, v_in), (go_hbm, go_in))

    def load(t, n):
        src, dst = pairs[n]
        return pltpu.make_async_copy(src.at[:, columns(t)], dst.at[:, columns(t)], in_sem.at[t, n])

    params = (
        pltpu.make_async_copy(rate_hbm, rate, par_sem.at[0]),
        pltpu.make_async_copy(res_hbm, res, par_sem.at[1]),
    )
    for cp in params:
        cp.start()
    barrier = pltpu.get_barrier_semaphore()
    for p in layers:
        pl.semaphore_signal(barrier, inc=1, device_id=layer(p), device_id_type=MESH)
    for j in others:
        pl.semaphore_signal(barrier, inc=1, device_id=member(j), device_id_type=MESH)

    for n in reversed(range(TILES)):
        for i in range(4):
            load(tile_at(n), i).start()

    def remote(src, dst, ssem, rsem, target):
        return pltpu.make_async_remote_copy(
            src_ref=src, dst_ref=dst, send_sem=ssem, recv_sem=rsem, device_id=target, device_id_type=MESH
        )

    def arrived(dst, count, rsem):
        part = dst.at[pl.ds(0, count)]
        remote(part, part, sa, rsem, member(others[0])).wait_recv()

    def departed(like, count, ssem):
        part = like.at[pl.ds(0, count)]
        remote(part, part, ssem, ra, member(others[0])).wait_send()

    for cp in params:
        cp.wait()

    @pl.loop(0, TILES)
    def _(t):
        state_tables(t, rate, ptab, btab)

    def tile_states(t):
        cols = columns(t)
        for n in range(4):
            load(t, n).wait()
        u = (k_in[:, cols].astype(F32) * v_in[:, cols].astype(F32)).astype(BF16)
        g = (go_in[:, cols].astype(F32) * q_in[:, cols].astype(F32)).astype(BF16)
        u_ref[:, cols] = u
        g_ref[:, cols] = g
        for half in range(HALVES):
            part = slice(half * LANES, (half + 1) * LANES)
            uf[half] = u[:, part].astype(F32)
            gf[half] = g[:, part].astype(F32)
        states(t, rate, u_ref, g_ref, ptab, btab, uf, gf, sub_s, sub_b, send_a)

    def tile_owners(t):
        return [x * RUN + t * HALVES + half for x in (1 - seg, seg) for half in range(HALVES)]

    def tile_send(t):
        for j in tile_owners(t):

            @pl.when(j != own)
            def _():
                remote(send_a.at[j], recv_a.at[own], sa, ra, member(j)).start()

    @pl.loop(0, 2)
    def _(n):
        tile_states(tile_at(TILES - 1 - n))

    pl.semaphore_wait(barrier, GROUP + DEPTH - 2)
    tile_send(tile_at(3))
    tile_send(tile_at(2))

    @pl.loop(2, TILES)
    def _(n):
        tile_states(tile_at(TILES - 1 - n))
        tile_send(tile_at(TILES - 1 - n))

    recv_a[own] = send_a[own]

    def near(t):
        near_part(t, rate, res, u_ref, g_ref, wtab, vtab, htab, near_c, near_g)

    @pl.loop(0, 2)
    def _(t):
        near(t)

    block = pl.ds(pl.multiple_of(run * LANES, LANES), LANES)
    lam8 = rate[pl.ds(pl.multiple_of(seg * HALF, HALF), HALF), block] * (1.0 / SEQ)
    lam = jnp.concatenate([lam8, lam8], axis=0)
    dec = jnp.exp(-lam * float(ROWS))
    span = float(ROWS * RUN)
    dec_g = jnp.exp(-lam * span)
    ahead = jnp.exp(-lam8 * (span * z.astype(F32)))
    behind = jnp.exp(-lam8 * (span * (DEPTH - 1 - z).astype(F32)))
    decs = [jnp.ones((MODES, LANES), F32)]
    for w in range(1, RUN):
        decs.append(decs[-1] * dec)
    zero = jnp.zeros((MODES, LANES), F32)
    arrived(recv_a, GROUP - 1, ra)

    def combine(carry, part, decay, length):
        s, q, bn, tn, gr, gw, front, dist = carry
        s_j, m_j, b_j, t_j, gr_j, gw_j = part
        db = front * b_j
        return (
            decay * s + s_j,
            decay * (q + length * s) + m_j,
            bn + db,
            tn + front * t_j + dist * db,
            gr + gr_j + b_j * s,
            gw + gw_j + t_j * s + b_j * q,
            front * decay,
            dist + length,
        )

    ones = jnp.ones((MODES, LANES), F32)
    s, bn = zero, zero
    for w in range(RUN):
        pre_s[w] = s
        last = RUN - 1 - w
        pre_b[last] = bn
        s = dec * s + jnp.concatenate([recv_a[x * RUN + w].astype(F32)[0:HALF] for x in range(SEGS)], axis=0)
        near_b = [recv_a[x * RUN + last].astype(F32)[2 * HALF : 3 * HALF] for x in range(SEGS)]
        bn = dec * bn + jnp.concatenate(near_b, axis=0)
    send_m[...] = jnp.concatenate([s, bn], axis=0).astype(BF16)
    for p in layers:
        remote(send_m, recv_m.at[z], sm, rm, layer(p)).start()
    total = (zero, zero, zero, zero, zero, zero, ones, 0.0)
    for w in range(RUN):
        got = [recv_a[x * RUN + w].astype(F32) for x in range(SEGS)]
        part = [
            jnp.concatenate([rows[n * HALF : (n + 1) * HALF] for rows in got], axis=0) for n in range(6)
        ]
        total = combine(total, part, dec, float(ROWS))
    s, q, bn, tn, gr, gw = total[:6]
    early, late = slice(0, HALF), slice(HALF, MODES)
    send_x[...] = jnp.concatenate([q, tn, gr[early] + gr[late], gw[early] + gw[late]], axis=0).astype(BF16)

    for p in layers:
        remote(send_x, recv_x.at[z], sx, rx, layer(p)).start()
    recv_m[z] = send_m[...]
    recv_x[z] = send_x[...]

    @pl.loop(2, TILES)
    def _(t):
        near(t)

    arrived(recv_m, DEPTH - 1, rm)
    state, whole = zero, zero
    for p in range(DEPTH):
        s_p = recv_m[p, 0:MODES, :].astype(F32)
        state = jnp.where(p < z, dec_g * state + s_p, state)
        whole = dec_g * whole + s_p
    state = jnp.concatenate([state[:HALF], state[HALF:] + ahead * whole[:HALF]], axis=0)
    back, whole = zero, zero
    for p in reversed(range(DEPTH)):
        b_p = recv_m[p, MODES : 2 * MODES, :].astype(F32)
        back = jnp.where(p > z, dec_g * back + b_p, back)
        whole = dec_g * whole + b_p
    back = jnp.concatenate([back[:HALF] + behind * whole[HALF:], back[HALF:]], axis=0)

    for w in range(RUN):
        st = pre_s[w] + decs[w] * state
        bk = pre_b[w] + decs[RUN - 1 - w] * back
        for x in range(SEGS):
            rows = slice(x * HALF, (x + 1) * HALF)
            send_c[x * RUN + w] = jnp.concatenate([st[rows], bk[rows]], axis=0).astype(BF16)
    for j in others:
        remote(send_c.at[j], recv_c.at[own], sc, rc.at[own], member(j)).start()
    recv_c[own] = send_c[own]

    arrived(recv_x, DEPTH - 1, rx)
    total = (zero, zero, zero, zero, zero, zero, ones, 0.0)
    plain = jnp.zeros((MODES, LANES), F32)
    for p in range(DEPTH):
        states_p = recv_m[p].astype(F32)
        rest = recv_x[p].astype(F32)
        plain = plain + rest[2 * MODES : 3 * MODES]
        part = (states_p[:MODES], rest[:MODES], states_p[MODES:], rest[MODES : 2 * MODES], zero, zero)
        total = combine(total, part, dec_g, span)
    s, q, bn, tn, gr, gw = total[:6]
    gr_all = plain[early] + gr[early] + gr[late] + bn[late] * s[early]
    gw_all = plain[late] + gw[early] + gw[late] + tn[late] * s[early] + bn[late] * q[early]
    send_e[...] = jnp.concatenate([gr_all, gw_all], axis=0).astype(BF16)
    for j in others:
        remote(send_e, recv_e.at[own], se, re, member(j)).start()
    recv_e[own] = send_e[...]

    @pl.loop(0, TILES)
    def _(n):
        t = tile_at(n)
        for j in tile_owners(t):

            @pl.when(j != own)
            def _():
                remote(send_c.at[j], recv_c.at[j], sc, rc.at[j], member(j)).wait_recv()

        far_part(t, rate, res, k_in, v_in, go_in, wtab, vtab, sub_s, sub_b, near_c, near_g, recv_c, gq, gk, gv)

    arrived(recv_e, GROUP - 1, re)
    scale = SEQ ** -0.5
    for w in range(RUN):
        cols = slice(w * LANES, (w + 1) * LANES)
        got = [recv_e[x * RUN + w].astype(F32) for x in range(SEGS)]
        gr, gw = [
            jnp.concatenate([rows[n * HALF : (n + 1) * HALF] for rows in got], axis=0) for n in range(2)
        ]
        gres[:, cols] = scale * gr
        grate[:, cols] = (-scale / SEQ) * res[:, cols] * gw
    departed(recv_a, GROUP - 1, sa)
    departed(recv_m, DEPTH - 1, sm)
    departed(recv_x, DEPTH - 1, sx)
    departed(recv_c, GROUP - 1, sc)
    departed(recv_e, GROUP - 1, se)


def store_kernel(*refs):
    srcs, dsts, sem = refs[:5], refs[5:10], refs[10]
    copies = [pltpu.make_async_copy(s, d, sem.at[n]) for n, (s, d) in enumerate(zip(srcs, dsts))]
    for cp in copies:
        cp.start()
    for cp in copies:
        cp.wait()


def local(query, key_in, value, grad_out, residue, rate):
    hbm = pl.BlockSpec(memory_space=pltpu.HBM)
    vmem = pl.BlockSpec(memory_space=pltpu.VMEM)
    big = jax.ShapeDtypeStruct((ROWS, CHANS), BF16)
    small = jax.ShapeDtypeStruct((MODES, CHANS), F32)
    dma = pltpu.SemaphoreType.DMA

    def buf(*shape, dtype=F32):
        return pltpu.VMEM(shape, dtype)

    held = [pltpu.VMEM((ROWS, CHANS), BF16)] * 3 + [pltpu.VMEM((MODES, CHANS), F32)] * 2
    args = [pltpu.with_memory_space_constraint(x, pltpu.HBM) for x in (query, key_in, value, grad_out, residue, rate)]
    results = pl.pallas_call(
        main_kernel,
        out_shape=held,
        in_specs=[hbm] * 6,
        out_specs=[vmem] * 5,
        scratch_shapes=[
            *[buf(ROWS, CHANS, dtype=BF16)] * 4,
            *[buf(MODES, CHANS)] * 2,
            *[buf(ROWS, CHANS, dtype=BF16)] * 2,
            *[buf(HALVES, ROWS, LANES)] * 2,
            *[buf(MODES, SUB, CHANS, dtype=BF16)] * 2,
            *[buf(SEGS, SUB // 2, 2 * HALF, CHANS, dtype=BF16)] * 2,
            buf(SUB, SUB, TILE, dtype=BF16),
            *[buf(NSUB, MODES, CHANS)] * 2,
            *[buf(ROWS, CHANS)] * 2,
            *[buf(GROUP, 6 * HALF, LANES, dtype=BF16)] * 2,
            *[buf(RUN, MODES, LANES)] * 2,
            buf(2 * MODES, LANES, dtype=BF16), buf(DEPTH, 2 * MODES, LANES, dtype=BF16),
            buf(3 * MODES, LANES, dtype=BF16), buf(DEPTH, 3 * MODES, LANES, dtype=BF16),
            *[buf(GROUP, 2 * HALF, LANES, dtype=BF16)] * 2,
            buf(2 * HALF, LANES, dtype=BF16), buf(GROUP, 2 * HALF, LANES, dtype=BF16),
            dma((TILES, 4)), dma((2,)),
            dma, dma, dma, dma, dma, dma, dma, dma((GROUP,)), dma, dma,
        ],
        compiler_params=pltpu.CompilerParams(collective_id=0, has_side_effects=True, vmem_limit_bytes=VMEM_LIMIT),
        name="hyena",
    )(*args)

    return pl.pallas_call(
        store_kernel,
        out_shape=(big, big, big, small, small),
        in_specs=[vmem] * 5,
        out_specs=[hbm] * 5,
        scratch_shapes=[dma((5,))],
        compiler_params=pltpu.CompilerParams(vmem_limit_bytes=8 * 2**20),
        name="store",
    )(*[pltpu.with_memory_space_constraint(x, pltpu.VMEM) for x in results])


def solution(mesh):
    big, small = P("ctx", "tp"), P(None, "tp")
    return jax.shard_map(
        local, mesh=mesh, in_specs=(big, big, big, big, small, small),
        out_specs=(big, big, big, small, small), check_vma=False,
    )
```

```python
import jax
import jax.numpy as jnp
from jax import lax
from jax.experimental import pallas as pl
from jax.experimental.pallas import tpu as pltpu
from jax.sharding import PartitionSpec as P

SEQ = 32768
MODES = 16
ROWS = 256
CHANS = 1024
SUB = 16
NSUB = ROWS // SUB
MID = 8
LANES = 128
TILE = 256
TILES = CHANS // TILE
HALVES = TILE // LANES
RUN = 8
SEGS = 2
DEPTH = 8
GROUP = SEGS * RUN
HALF = MODES // SEGS
VMEM_LIMIT = 40 * 2**20
F32 = jnp.float32
BF16 = jnp.bfloat16
MESH = pl.DeviceIdType.MESH


def iota(shape, dim):
    return lax.broadcasted_iota(jnp.int32, shape, dim)


def dot(a, b):
    return jnp.dot(a, b, preferred_element_type=F32)


def columns(t):
    return pl.ds(pl.multiple_of(t * TILE, TILE), TILE)


def spread(tab, val):
    return (tab * val[None]).reshape(tab.shape[0] * tab.shape[1], TILE)


def state_tables(t, rate, ptab, btab):
    cols = columns(t)
    pos = iota((SUB, TILE), 0).astype(F32)
    lam = rate[:, cols] * (1.0 / SEQ)
    for m in range(MODES):
        row = lam[m : m + 1, :]
        ptab[m, :, cols] = jnp.exp(-row * (SUB - 1.0 - pos)).astype(BF16)
        btab[m, :, cols] = jnp.exp(-row * (pos + 1.0)).astype(BF16)


def selectors(sel_s, sel_b, pick):
    out_row = iota((2 * MODES, MODES * SUB), 0)
    in_row = iota((2 * MODES, MODES * SUB), 1)
    hit = (in_row // SUB) == (out_row % MODES)
    off = (in_row % SUB).astype(F32)
    first = out_row < MODES
    sel_s[...] = jnp.where(hit, jnp.where(first, 1.0, SUB - 1.0 - off), 0.0).astype(BF16)
    sel_b[...] = jnp.where(hit, jnp.where(first, 1.0, off + 1.0), 0.0).astype(BF16)
    out_row = iota((2 * SUB, SUB * MODES), 0)
    in_row = iota((2 * SUB, SUB * MODES), 1)
    pick[...] = jnp.where(in_row // HALF == out_row, 1.0, 0.0).astype(BF16)


def states(t, rate, u_ref, g_ref, ptab, btab, sel_s, sel_b, uf, gf, sub_s, sub_b, send_a):
    cols = columns(t)
    lam = rate[:, cols] * (1.0 / SEQ)
    step = jnp.exp(-lam * SUB)
    zero = jnp.zeros((MODES, TILE), F32)
    s, q, bn, tn, gr, gw = zero, zero, zero, zero, zero, zero
    decay = jnp.ones((MODES, TILE), F32)
    for k in range(NSUB):
        rows = slice(k * SUB, (k + 1) * SUB)
        su = dot(sel_s[...], spread(ptab[:, :, cols], u_ref[rows, cols]))
        sg = dot(sel_b[...], spread(btab[:, :, cols], g_ref[rows, cols]))
        s_k, m_k = su[:MODES], su[MODES:]
        b_k, t_k = sg[:MODES], sg[MODES:]
        sub_s[k, :, cols] = s_k
        sub_b[k, :, cols] = b_k
        gr = gr + b_k * s
        gw = gw + t_k * s + b_k * q
        q = step * (q + float(SUB) * s) + m_k
        s = step * s + s_k
        db = decay * b_k
        bn = bn + db
        tn = tn + decay * t_k + float(k * SUB) * db
        decay = decay * step
    halves = []
    for half in range(HALVES):
        acc = [jnp.zeros((8, LANES), F32) for _ in range(SUB)]
        for octet in range(NSUB // 8):
            us = [uf[half, pl.ds(octet * 8 * SUB + b, 8, stride=SUB), :] for b in range(SUB)]
            for b in range(SUB):
                gb = gf[half, pl.ds(octet * 8 * SUB + b, 8, stride=SUB), :]
                for lag in range(b + 1):
                    acc[lag] = acc[lag] + gb * us[b - lag]
        halves.append([jnp.sum(a, axis=0, keepdims=True) for a in acc])
    unit = jnp.exp(-lam)
    power = jnp.ones((MODES, TILE), F32)
    for lag in range(SUB):
        term = jnp.concatenate([h[lag] for h in halves], axis=1) * power
        gr = gr + term
        gw = gw + float(lag) * term
        power = power * unit
    for half in range(HALVES):
        part_cols = slice(half * LANES, (half + 1) * LANES)
        for x in range(SEGS):
            modes = slice(x * HALF, (x + 1) * HALF)
            parts = [part[modes, part_cols] for part in (s, q, bn, tn, gr, gw)]
            send_a[x * RUN + t * HALVES + half] = jnp.concatenate(parts, axis=0).astype(BF16)


def near_part(t, rate, res, u_ref, g_ref, wtab, vtab, htab, near_c, near_g):
    cols = columns(t)
    lam = rate[:, cols] * (1.0 / SEQ)
    unit = jnp.exp(-lam)
    power = res[:, cols]
    mid = power * jnp.exp(-lam * float(MID))
    powers = []
    for b in range(SUB):
        htab[b] = jnp.broadcast_to(jnp.sum(power, axis=0, keepdims=True), (SUB, TILE)).astype(BF16)
        powers.append(power - mid)
        power = power * unit
    powers.append(power - mid)
    for i in range(SUB // 2):
        for h in range(2):
            modes = slice(h * HALF, (h + 1) * HALF)
            pair = (powers[2 * i + 1][modes], powers[2 * i + 2][modes])
            wtab[h, i, :, cols] = jnp.concatenate(pair, axis=0).astype(BF16)
            pair = (powers[SUB - 1 - 2 * i][modes], powers[SUB - 2 - 2 * i][modes])
            vtab[h, i, :, cols] = jnp.concatenate(pair, axis=0).astype(BF16)
    out_row = iota((SUB, SUB * SUB), 0)
    in_row = iota((SUB, SUB * SUB), 1)
    lag, pos = in_row // SUB, in_row % SUB
    down = jnp.where(pos + lag == out_row, 1.0, 0.0).astype(BF16)
    up = jnp.where(pos - lag == out_row, 1.0, 0.0).astype(BF16)
    for k in range(NSUB):
        rows = slice(k * SUB, (k + 1) * SUB)
        near_c[rows, cols] = dot(down, spread(htab[...], u_ref[rows, cols]))
        near_g[rows, cols] = dot(up, spread(htab[...], g_ref[rows, cols]))


def far_part(t, rate, res, pick, k_in, v_in, go_in, wtab, vtab, sub_s, sub_b, near_c, near_g, recv_c, gq, gk, gv):
    cols = columns(t)
    lam = rate[:, cols] * (1.0 / SEQ)
    step = jnp.exp(-lam * SUB)
    mid = res[:, cols] * jnp.exp(-lam * float(MID))

    def incoming(n):
        rows = slice(n * HALF, (n + 1) * HALF)
        parts = [
            jnp.concatenate([recv_c[x * RUN + t * HALVES + h].astype(F32)[rows] for x in range(SEGS)], axis=0)
            for h in range(HALVES)
        ]
        return jnp.concatenate(parts, axis=1)

    def reach(tab, xs):
        sums = []
        bases = []
        for x in xs:
            bases.append(jnp.broadcast_to(jnp.sum(mid * x, axis=0, keepdims=True), (SUB, TILE)))
            low = jnp.concatenate([x[:HALF], x[:HALF]], axis=0).astype(BF16)
            high = jnp.concatenate([x[HALF:], x[HALF:]], axis=0).astype(BF16)
            sums.append((tab[0, :, :, cols] * low[None] + tab[1, :, :, cols] * high[None]).reshape(SUB * HALF, TILE))
        return dot(pick[...], jnp.concatenate(sums, axis=0)) + jnp.concatenate(bases, axis=0)

    x = incoming(0)
    for k in range(0, NSUB, 2):
        rows = slice(k * SUB, (k + 2) * SUB)
        after = step * x + sub_s[k, :, cols]
        conv = near_c[rows, cols] + reach(wtab, (x, after))
        gq[rows, cols] = (go_in[rows, cols].astype(F32) * conv).astype(BF16)
        x = step * after + sub_s[k + 1, :, cols]
    x = incoming(1)
    for k in reversed(range(0, NSUB, 2)):
        rows = slice(k * SUB, (k + 2) * SUB)
        before = step * x + sub_b[k + 1, :, cols]
        grad = near_g[rows, cols] + reach(vtab, (before, x))
        gk[rows, cols] = (v_in[rows, cols].astype(F32) * grad).astype(BF16)
        gv[rows, cols] = (k_in[rows, cols].astype(F32) * grad).astype(BF16)
        x = step * before + sub_b[k, :, cols]


def main_kernel(
    q_hbm, k_hbm, v_hbm, go_hbm, res_hbm, rate_hbm,
    gq, gk, gv, gres, grate,
    q_in, k_in, v_in, go_in, res, rate, u_ref, g_ref, uf, gf, ptab, btab, wtab, vtab, htab, sel_s, sel_b, pick,
    sub_s, sub_b, near_c, near_g,
    send_a, recv_a, pre_s, pre_b, send_m, recv_m, send_x, recv_x, send_c, recv_c, send_e, recv_e,
    in_sem, par_sem, sa, ra, sm, rm, sx, rx, sc, rc, se, re,
):
    me = lax.axis_index("ctx")
    seg = lax.div(me, DEPTH * RUN)
    z = lax.rem(lax.div(me, RUN), DEPTH)
    run = lax.rem(me, RUN)
    y = lax.div(run, 2)
    own = seg * RUN + run
    others = [lax.rem(own + d, GROUP) for d in (12, 4, 11, 5, 13, 3, 10, 6, 14, 2, 9, 7, 8, 15, 1)]
    layers = [lax.rem(z + d, DEPTH) for d in (4, 5, 3, 6, 2, 7, 1)]
    here, column = z * RUN, seg * (DEPTH * RUN) + run

    def member(j):
        return {"ctx": lax.div(j, RUN) * ((DEPTH - 1) * RUN) + here + j}

    def layer(p):
        return {"ctx": column + p * RUN}

    def gray(n):
        return n + lax.div(n, 2) - 2 * lax.div(n, 3)

    def tile_at(n):
        return lax.rem(y + gray(jnp.int32(n)), TILES)

    pairs = ((q_hbm, q_in), (k_hbm, k_in), (v_hbm, v_in), (go_hbm, go_in))

    def load(t, n):
        src, dst = pairs[n]
        return pltpu.make_async_copy(src.at[:, columns(t)], dst.at[:, columns(t)], in_sem.at[t, n])

    params = (
        pltpu.make_async_copy(rate_hbm, rate, par_sem.at[0]),
        pltpu.make_async_copy(res_hbm, res, par_sem.at[1]),
    )
    for cp in params:
        cp.start()
    barrier = pltpu.get_barrier_semaphore()
    for p in layers:
        pl.semaphore_signal(barrier, inc=1, device_id=layer(p), device_id_type=MESH)
    for j in others:
        pl.semaphore_signal(barrier, inc=1, device_id=member(j), device_id_type=MESH)

    for n in reversed(range(TILES)):
        for i in range(4):
            load(tile_at(n), i).start()

    def remote(src, dst, ssem, rsem, target):
        return pltpu.make_async_remote_copy(
            src_ref=src, dst_ref=dst, send_sem=ssem, recv_sem=rsem, device_id=target, device_id_type=MESH
        )

    def arrived(dst, count, rsem):
        part = dst.at[pl.ds(0, count)]
        remote(part, part, sa, rsem, member(others[0])).wait_recv()

    def departed(like, count, ssem):
        part = like.at[pl.ds(0, count)]
        remote(part, part, ssem, ra, member(others[0])).wait_send()

    selectors(sel_s, sel_b, pick)
    for cp in params:
        cp.wait()

    @pl.loop(0, TILES)
    def _(t):
        state_tables(t, rate, ptab, btab)

    def tile_states(t):
        cols = columns(t)
        for n in range(4):
            load(t, n).wait()
        u = (k_in[:, cols].astype(F32) * v_in[:, cols].astype(F32)).astype(BF16)
        g = (go_in[:, cols].astype(F32) * q_in[:, cols].astype(F32)).astype(BF16)
        u_ref[:, cols] = u
        g_ref[:, cols] = g
        for half in range(HALVES):
            part = slice(half * LANES, (half + 1) * LANES)
            uf[half] = u[:, part].astype(F32)
            gf[half] = g[:, part].astype(F32)
        states(t, rate, u_ref, g_ref, ptab, btab, sel_s, sel_b, uf, gf, sub_s, sub_b, send_a)

    def tile_owners(t):
        return [x * RUN + t * HALVES + half for x in (1 - seg, seg) for half in range(HALVES)]

    def tile_send(t):
        for j in tile_owners(t):

            @pl.when(j != own)
            def _():
                remote(send_a.at[j], recv_a.at[own], sa, ra, member(j)).start()

    @pl.loop(0, 2)
    def _(n):
        tile_states(tile_at(TILES - 1 - n))

    pl.semaphore_wait(barrier, GROUP + DEPTH - 2)
    tile_send(tile_at(3))
    tile_send(tile_at(2))

    @pl.loop(2, TILES)
    def _(n):
        tile_states(tile_at(TILES - 1 - n))
        tile_send(tile_at(TILES - 1 - n))

    recv_a[own] = send_a[own]

    def near(t):
        near_part(t, rate, res, u_ref, g_ref, wtab, vtab, htab, near_c, near_g)

    @pl.loop(0, 2)
    def _(t):
        near(t)

    block = pl.ds(pl.multiple_of(run * LANES, LANES), LANES)
    lam8 = rate[pl.ds(pl.multiple_of(seg * HALF, HALF), HALF), block] * (1.0 / SEQ)
    lam = jnp.concatenate([lam8, lam8], axis=0)
    dec = jnp.exp(-lam * float(ROWS))
    span = float(ROWS * RUN)
    dec_g = jnp.exp(-lam * span)
    ahead = jnp.exp(-lam8 * (span * z.astype(F32)))
    behind = jnp.exp(-lam8 * (span * (DEPTH - 1 - z).astype(F32)))
    decs = [jnp.ones((MODES, LANES), F32)]
    for w in range(1, RUN):
        decs.append(decs[-1] * dec)
    zero = jnp.zeros((MODES, LANES), F32)
    arrived(recv_a, GROUP - 1, ra)

    def combine(carry, part, decay, length):
        s, q, bn, tn, gr, gw, front, dist = carry
        s_j, m_j, b_j, t_j, gr_j, gw_j = part
        db = front * b_j
        return (
            decay * s + s_j,
            decay * (q + length * s) + m_j,
            bn + db,
            tn + front * t_j + dist * db,
            gr + gr_j + b_j * s,
            gw + gw_j + t_j * s + b_j * q,
            front * decay,
            dist + length,
        )

    ones = jnp.ones((MODES, LANES), F32)
    s, bn = zero, zero
    for w in range(RUN):
        pre_s[w] = s
        last = RUN - 1 - w
        pre_b[last] = bn
        s = dec * s + jnp.concatenate([recv_a[x * RUN + w].astype(F32)[0:HALF] for x in range(SEGS)], axis=0)
        near_b = [recv_a[x * RUN + last].astype(F32)[2 * HALF : 3 * HALF] for x in range(SEGS)]
        bn = dec * bn + jnp.concatenate(near_b, axis=0)
    send_m[...] = jnp.concatenate([s, bn], axis=0).astype(BF16)
    for p in layers:
        remote(send_m, recv_m.at[z], sm, rm, layer(p)).start()
    total = (zero, zero, zero, zero, zero, zero, ones, 0.0)
    for w in range(RUN):
        got = [recv_a[x * RUN + w].astype(F32) for x in range(SEGS)]
        part = [
            jnp.concatenate([rows[n * HALF : (n + 1) * HALF] for rows in got], axis=0) for n in range(6)
        ]
        total = combine(total, part, dec, float(ROWS))
    s, q, bn, tn, gr, gw = total[:6]
    early, late = slice(0, HALF), slice(HALF, MODES)
    send_x[...] = jnp.concatenate([q, tn, gr[early] + gr[late], gw[early] + gw[late]], axis=0).astype(BF16)

    for p in layers:
        remote(send_x, recv_x.at[z], sx, rx, layer(p)).start()
    recv_m[z] = send_m[...]
    recv_x[z] = send_x[...]

    @pl.loop(2, TILES)
    def _(t):
        near(t)

    arrived(recv_m, DEPTH - 1, rm)
    state, whole = zero, zero
    for p in range(DEPTH):
        s_p = recv_m[p, 0:MODES, :].astype(F32)
        state = jnp.where(p < z, dec_g * state + s_p, state)
        whole = dec_g * whole + s_p
    state = jnp.concatenate([state[:HALF], state[HALF:] + ahead * whole[:HALF]], axis=0)
    back, whole = zero, zero
    for p in reversed(range(DEPTH)):
        b_p = recv_m[p, MODES : 2 * MODES, :].astype(F32)
        back = jnp.where(p > z, dec_g * back + b_p, back)
        whole = dec_g * whole + b_p
    back = jnp.concatenate([back[:HALF] + behind * whole[HALF:], back[HALF:]], axis=0)

    for w in range(RUN):
        st = pre_s[w] + decs[w] * state
        bk = pre_b[w] + decs[RUN - 1 - w] * back
        for x in range(SEGS):
            rows = slice(x * HALF, (x + 1) * HALF)
            send_c[x * RUN + w] = jnp.concatenate([st[rows], bk[rows]], axis=0).astype(BF16)
    for j in reversed(others):
        remote(send_c.at[j], recv_c.at[own], sc, rc.at[own], member(j)).start()
    recv_c[own] = send_c[own]

    arrived(recv_x, DEPTH - 1, rx)
    total = (zero, zero, zero, zero, zero, zero, ones, 0.0)
    plain = jnp.zeros((MODES, LANES), F32)
    for p in range(DEPTH):
        states_p = recv_m[p].astype(F32)
        rest = recv_x[p].astype(F32)
        plain = plain + rest[2 * MODES : 3 * MODES]
        part = (states_p[:MODES], rest[:MODES], states_p[MODES:], rest[MODES : 2 * MODES], zero, zero)
        total = combine(total, part, dec_g, span)
    s, q, bn, tn, gr, gw = total[:6]
    gr_all = plain[early] + gr[early] + gr[late] + bn[late] * s[early]
    gw_all = plain[late] + gw[early] + gw[late] + tn[late] * s[early] + bn[late] * q[early]
    send_e[...] = jnp.concatenate([gr_all, gw_all], axis=0).astype(BF16)
    for j in others:
        remote(send_e, recv_e.at[own], se, re, member(j)).start()
    recv_e[own] = send_e[...]

    @pl.loop(0, TILES)
    def _(n):
        t = tile_at(n)
        for j in tile_owners(t):

            @pl.when(j != own)
            def _():
                remote(send_c.at[j], recv_c.at[j], sc, rc.at[j], member(j)).wait_recv()

        far_part(t, rate, res, pick, k_in, v_in, go_in, wtab, vtab, sub_s, sub_b, near_c, near_g, recv_c, gq, gk, gv)

    arrived(recv_e, GROUP - 1, re)
    scale = SEQ ** -0.5
    for w in range(RUN):
        cols = slice(w * LANES, (w + 1) * LANES)
        got = [recv_e[x * RUN + w].astype(F32) for x in range(SEGS)]
        gr, gw = [
            jnp.concatenate([rows[n * HALF : (n + 1) * HALF] for rows in got], axis=0) for n in range(2)
        ]
        gres[:, cols] = scale * gr
        grate[:, cols] = (-scale / SEQ) * res[:, cols] * gw
    departed(recv_a, GROUP - 1, sa)
    departed(recv_m, DEPTH - 1, sm)
    departed(recv_x, DEPTH - 1, sx)
    departed(recv_c, GROUP - 1, sc)
    departed(recv_e, GROUP - 1, se)


def store_kernel(*refs):
    srcs, dsts, sem = refs[:5], refs[5:10], refs[10]
    copies = [pltpu.make_async_copy(s, d, sem.at[n]) for n, (s, d) in enumerate(zip(srcs, dsts))]
    for cp in copies:
        cp.start()
    for cp in copies:
        cp.wait()


def local(query, key_in, value, grad_out, residue, rate):
    hbm = pl.BlockSpec(memory_space=pltpu.HBM)
    vmem = pl.BlockSpec(memory_space=pltpu.VMEM)
    big = jax.ShapeDtypeStruct((ROWS, CHANS), BF16)
    small = jax.ShapeDtypeStruct((MODES, CHANS), F32)
    dma = pltpu.SemaphoreType.DMA

    def buf(*shape, dtype=F32):
        return pltpu.VMEM(shape, dtype)

    held = [pltpu.VMEM((ROWS, CHANS), BF16)] * 3 + [pltpu.VMEM((MODES, CHANS), F32)] * 2
    args = [pltpu.with_memory_space_constraint(x, pltpu.HBM) for x in (query, key_in, value, grad_out, residue, rate)]
    results = pl.pallas_call(
        main_kernel,
        out_shape=held,
        in_specs=[hbm] * 6,
        out_specs=[vmem] * 5,
        scratch_shapes=[
            *[buf(ROWS, CHANS, dtype=BF16)] * 4,
            *[buf(MODES, CHANS)] * 2,
            *[buf(ROWS, CHANS, dtype=BF16)] * 2,
            *[buf(HALVES, ROWS, LANES)] * 2,
            *[buf(MODES, SUB, CHANS, dtype=BF16)] * 2,
            *[buf(SEGS, SUB // 2, 2 * HALF, CHANS, dtype=BF16)] * 2,
            buf(SUB, SUB, TILE, dtype=BF16),
            *[buf(2 * MODES, MODES * SUB, dtype=BF16)] * 3,
            *[buf(NSUB, MODES, CHANS)] * 2,
            *[buf(ROWS, CHANS)] * 2,
            *[buf(GROUP, 6 * HALF, LANES, dtype=BF16)] * 2,
            *[buf(RUN, MODES, LANES)] * 2,
            buf(2 * MODES, LANES, dtype=BF16), buf(DEPTH, 2 * MODES, LANES, dtype=BF16),
            buf(3 * MODES, LANES, dtype=BF16), buf(DEPTH, 3 * MODES, LANES, dtype=BF16),
            *[buf(GROUP, 2 * HALF, LANES, dtype=BF16)] * 2,
            buf(2 * HALF, LANES, dtype=BF16), buf(GROUP, 2 * HALF, LANES, dtype=BF16),
            dma((TILES, 4)), dma((2,)),
            dma, dma, dma, dma, dma, dma, dma, dma((GROUP,)), dma, dma,
        ],
        compiler_params=pltpu.CompilerParams(collective_id=0, has_side_effects=True, vmem_limit_bytes=VMEM_LIMIT),
        name="hyena",
    )(*args)

    return pl.pallas_call(
        store_kernel,
        out_shape=(big, big, big, small, small),
        in_specs=[vmem] * 5,
        out_specs=[hbm] * 5,
        scratch_shapes=[dma((5,))],
        compiler_params=pltpu.CompilerParams(vmem_limit_bytes=8 * 2**20),
        name="store",
    )(*[pltpu.with_memory_space_constraint(x, pltpu.VMEM) for x in results])


def solution(mesh):
    big, small = P("ctx", "tp"), P(None, "tp")
    return jax.shard_map(
        local, mesh=mesh, in_specs=(big, big, big, big, small, small),
        out_specs=(big, big, big, small, small), check_vma=False,
    )
```

```python
import jax
import jax.numpy as jnp
from jax import lax
from jax.experimental import pallas as pl
from jax.experimental.pallas import tpu as pltpu
from jax.sharding import PartitionSpec as P

SEQ = 32768
MODES = 16
ROWS = 256
CHANS = 1024
SUB = 16
NSUB = ROWS // SUB
MID = 8
LANES = 128
TILE = 256
TILES = CHANS // TILE
HALVES = TILE // LANES
RUN = 8
SEGS = 2
DEPTH = 8
GROUP = SEGS * RUN
HALF = MODES // SEGS
VMEM_LIMIT = 40 * 2**20
F32 = jnp.float32
BF16 = jnp.bfloat16
MESH = pl.DeviceIdType.MESH


def iota(shape, dim):
    return lax.broadcasted_iota(jnp.int32, shape, dim)


def dot(a, b):
    return jnp.dot(a, b, preferred_element_type=F32)


def columns(t):
    return pl.ds(pl.multiple_of(t * TILE, TILE), TILE)


def spread(tab, val):
    return (tab * val[None]).reshape(tab.shape[0] * tab.shape[1], TILE)


def state_tables(t, rate, ptab, btab):
    cols = columns(t)
    pos = iota((SUB, TILE), 0).astype(F32)
    lam = rate[:, cols] * (1.0 / SEQ)
    for m in range(MODES):
        row = lam[m : m + 1, :]
        ptab[m, :, cols] = jnp.exp(-row * (SUB - 1.0 - pos)).astype(BF16)
        btab[m, :, cols] = jnp.exp(-row * (pos + 1.0)).astype(BF16)


def selectors(sel_s, sel_b, pick):
    out_row = iota((2 * MODES, MODES * SUB), 0)
    in_row = iota((2 * MODES, MODES * SUB), 1)
    hit = (in_row // SUB) == (out_row % MODES)
    off = (in_row % SUB).astype(F32)
    first = out_row < MODES
    sel_s[...] = jnp.where(hit, jnp.where(first, 1.0, SUB - 1.0 - off), 0.0).astype(BF16)
    sel_b[...] = jnp.where(hit, jnp.where(first, 1.0, off + 1.0), 0.0).astype(BF16)
    out_row = iota((2 * SUB, SUB * MODES), 0)
    in_row = iota((2 * SUB, SUB * MODES), 1)
    pick[...] = jnp.where(in_row // HALF == out_row, 1.0, 0.0).astype(BF16)


def states(t, rate, u_ref, g_ref, ptab, btab, sel_s, sel_b, uf, gf, sub_s, sub_b, send_a):
    cols = columns(t)
    lam = rate[:, cols] * (1.0 / SEQ)
    step = jnp.exp(-lam * SUB)
    zero = jnp.zeros((MODES, TILE), F32)
    s, q, bn, tn, gr, gw = zero, zero, zero, zero, zero, zero
    decay = jnp.ones((MODES, TILE), F32)
    for k in range(NSUB):
        rows = slice(k * SUB, (k + 1) * SUB)
        su = dot(sel_s[...], spread(ptab[:, :, cols], u_ref[rows, cols]))
        sg = dot(sel_b[...], spread(btab[:, :, cols], g_ref[rows, cols]))
        s_k, m_k = su[:MODES], su[MODES:]
        b_k, t_k = sg[:MODES], sg[MODES:]
        sub_s[k, :, cols] = s_k
        sub_b[k, :, cols] = b_k
        gr = gr + b_k * s
        gw = gw + t_k * s + b_k * q
        q = step * (q + float(SUB) * s) + m_k
        s = step * s + s_k
        db = decay * b_k
        bn = bn + db
        tn = tn + decay * t_k + float(k * SUB) * db
        decay = decay * step
    halves = []
    for half in range(HALVES):
        acc = [jnp.zeros((8, LANES), F32) for _ in range(SUB)]
        for octet in range(NSUB // 8):
            us = [uf[half, pl.ds(octet * 8 * SUB + b, 8, stride=SUB), :] for b in range(SUB)]
            for b in range(SUB):
                gb = gf[half, pl.ds(octet * 8 * SUB + b, 8, stride=SUB), :]
                for lag in range(b + 1):
                    acc[lag] = acc[lag] + gb * us[b - lag]
        halves.append([jnp.sum(a, axis=0, keepdims=True) for a in acc])
    unit = jnp.exp(-lam)
    power = jnp.ones((MODES, TILE), F32)
    for lag in range(SUB):
        term = jnp.concatenate([h[lag] for h in halves], axis=1) * power
        gr = gr + term
        gw = gw + float(lag) * term
        power = power * unit
    for half in range(HALVES):
        part_cols = slice(half * LANES, (half + 1) * LANES)
        for x in range(SEGS):
            modes = slice(x * HALF, (x + 1) * HALF)
            parts = [part[modes, part_cols] for part in (s, q, bn, tn, gr, gw)]
            send_a[x * RUN + t * HALVES + half] = jnp.concatenate(parts, axis=0).astype(BF16)


def near_part(t, rate, res, u_ref, g_ref, wtab, vtab, htab, near_c, near_g):
    cols = columns(t)
    lam = rate[:, cols] * (1.0 / SEQ)
    unit = jnp.exp(-lam)
    power = res[:, cols]
    mid = power * jnp.exp(-lam * float(MID))
    powers = []
    for b in range(SUB):
        htab[b] = jnp.broadcast_to(jnp.sum(power, axis=0, keepdims=True), (SUB, TILE)).astype(BF16)
        powers.append(power - mid)
        power = power * unit
    powers.append(power - mid)
    for i in range(SUB // 2):
        for h in range(2):
            modes = slice(h * HALF, (h + 1) * HALF)
            pair = (powers[2 * i + 1][modes], powers[2 * i + 2][modes])
            wtab[h, i, :, cols] = jnp.concatenate(pair, axis=0).astype(BF16)
            pair = (powers[SUB - 1 - 2 * i][modes], powers[SUB - 2 - 2 * i][modes])
            vtab[h, i, :, cols] = jnp.concatenate(pair, axis=0).astype(BF16)
    out_row = iota((SUB, SUB * SUB), 0)
    in_row = iota((SUB, SUB * SUB), 1)
    lag, pos = in_row // SUB, in_row % SUB
    down = jnp.where(pos + lag == out_row, 1.0, 0.0).astype(BF16)
    up = jnp.where(pos - lag == out_row, 1.0, 0.0).astype(BF16)
    for k in range(NSUB):
        rows = slice(k * SUB, (k + 1) * SUB)
        near_c[rows, cols] = dot(down, spread(htab[...], u_ref[rows, cols]))
        near_g[rows, cols] = dot(up, spread(htab[...], g_ref[rows, cols]))


def far_part(t, rate, res, pick, k_in, v_in, go_in, wtab, vtab, sub_s, sub_b, near_c, near_g, recv_c, gq, gk, gv):
    cols = columns(t)
    lam = rate[:, cols] * (1.0 / SEQ)
    step = jnp.exp(-lam * SUB)
    mid = res[:, cols] * jnp.exp(-lam * float(MID))

    def incoming(n):
        rows = slice(n * HALF, (n + 1) * HALF)
        parts = [
            jnp.concatenate([recv_c[x * RUN + t * HALVES + h].astype(F32)[rows] for x in range(SEGS)], axis=0)
            for h in range(HALVES)
        ]
        return jnp.concatenate(parts, axis=1)

    def reach(tab, xs):
        sums = []
        bases = []
        for x in xs:
            bases.append(jnp.broadcast_to(jnp.sum(mid * x, axis=0, keepdims=True), (SUB, TILE)))
            low = jnp.concatenate([x[:HALF], x[:HALF]], axis=0).astype(BF16)
            high = jnp.concatenate([x[HALF:], x[HALF:]], axis=0).astype(BF16)
            sums.append((tab[0, :, :, cols] * low[None] + tab[1, :, :, cols] * high[None]).reshape(SUB * HALF, TILE))
        return dot(pick[...], jnp.concatenate(sums, axis=0)) + jnp.concatenate(bases, axis=0)

    x = incoming(0)
    for k in range(0, NSUB, 2):
        rows = slice(k * SUB, (k + 2) * SUB)
        after = step * x + sub_s[k, :, cols]
        conv = near_c[rows, cols] + reach(wtab, (x, after))
        gq[rows, cols] = (go_in[rows, cols].astype(F32) * conv).astype(BF16)
        x = step * after + sub_s[k + 1, :, cols]
    x = incoming(1)
    for k in reversed(range(0, NSUB, 2)):
        rows = slice(k * SUB, (k + 2) * SUB)
        before = step * x + sub_b[k + 1, :, cols]
        grad = near_g[rows, cols] + reach(vtab, (before, x))
        gk[rows, cols] = (v_in[rows, cols].astype(F32) * grad).astype(BF16)
        gv[rows, cols] = (k_in[rows, cols].astype(F32) * grad).astype(BF16)
        x = step * before + sub_b[k, :, cols]


def main_kernel(
    q_hbm, k_hbm, v_hbm, go_hbm, res_hbm, rate_hbm,
    gq, gk, gv, gres, grate,
    q_in, k_in, v_in, go_in, res, rate, u_ref, g_ref, uf, gf, ptab, btab, wtab, vtab, htab, sel_s, sel_b, pick,
    sub_s, sub_b, near_c, near_g,
    send_a, recv_a, pre_s, pre_b, send_m, recv_m, send_x, recv_x, send_c, recv_c, send_e, recv_e,
    in_sem, par_sem, sa, ra, sm, rm, sx, rx, sc, rc, se, re,
):
    me = lax.axis_index("ctx")
    seg = lax.div(me, DEPTH * RUN)
    z = lax.rem(lax.div(me, RUN), DEPTH)
    run = lax.rem(me, RUN)
    y = lax.div(run, 2)
    own = seg * RUN + run
    others = [lax.rem(own + d, GROUP) for d in (12, 4, 11, 5, 13, 3, 10, 6, 14, 2, 9, 7, 8, 15, 1)]
    layers = [lax.rem(z + d, DEPTH) for d in (4, 5, 3, 6, 2, 7, 1)]
    here, column = z * RUN, seg * (DEPTH * RUN) + run

    def member(j):
        return {"ctx": lax.div(j, RUN) * ((DEPTH - 1) * RUN) + here + j}

    def layer(p):
        return {"ctx": column + p * RUN}

    def gray(n):
        return n + lax.div(n, 2) - 2 * lax.div(n, 3)

    def tile_at(n):
        return lax.rem(y + gray(jnp.int32(n)), TILES)

    pairs = ((q_hbm, q_in), (k_hbm, k_in), (v_hbm, v_in), (go_hbm, go_in))

    def load(t, n):
        src, dst = pairs[n]
        return pltpu.make_async_copy(src.at[:, columns(t)], dst.at[:, columns(t)], in_sem.at[t, n])

    params = (
        pltpu.make_async_copy(rate_hbm, rate, par_sem.at[0]),
        pltpu.make_async_copy(res_hbm, res, par_sem.at[1]),
    )
    for cp in params:
        cp.start()
    barrier = pltpu.get_barrier_semaphore()
    for p in layers:
        pl.semaphore_signal(barrier, inc=1, device_id=layer(p), device_id_type=MESH)
    for j in others:
        pl.semaphore_signal(barrier, inc=1, device_id=member(j), device_id_type=MESH)

    for n in reversed(range(TILES)):
        for i in range(4):
            load(tile_at(n), i).start()

    def remote(src, dst, ssem, rsem, target):
        return pltpu.make_async_remote_copy(
            src_ref=src, dst_ref=dst, send_sem=ssem, recv_sem=rsem, device_id=target, device_id_type=MESH
        )

    def arrived(dst, count, rsem):
        part = dst.at[pl.ds(0, count)]
        remote(part, part, sa, rsem, member(others[0])).wait_recv()

    def departed(like, count, ssem):
        part = like.at[pl.ds(0, count)]
        remote(part, part, ssem, ra, member(others[0])).wait_send()

    selectors(sel_s, sel_b, pick)
    for cp in params:
        cp.wait()

    @pl.loop(0, TILES)
    def _(t):
        state_tables(t, rate, ptab, btab)

    def tile_states(t):
        cols = columns(t)
        for n in range(4):
            load(t, n).wait()
        u = (k_in[:, cols].astype(F32) * v_in[:, cols].astype(F32)).astype(BF16)
        g = (go_in[:, cols].astype(F32) * q_in[:, cols].astype(F32)).astype(BF16)
        u_ref[:, cols] = u
        g_ref[:, cols] = g
        for half in range(HALVES):
            part = slice(half * LANES, (half + 1) * LANES)
            uf[half] = u[:, part].astype(F32)
            gf[half] = g[:, part].astype(F32)
        states(t, rate, u_ref, g_ref, ptab, btab, sel_s, sel_b, uf, gf, sub_s, sub_b, send_a)

    def tile_owners(t):
        return [x * RUN + t * HALVES + half for x in (1 - seg, seg) for half in range(HALVES)]

    def tile_send(t):
        for j in tile_owners(t):

            @pl.when(j != own)
            def _():
                remote(send_a.at[j], recv_a.at[own], sa, ra, member(j)).start()

    @pl.loop(0, 2)
    def _(n):
        tile_states(tile_at(TILES - 1 - n))

    pl.semaphore_wait(barrier, GROUP + DEPTH - 2)
    tile_send(tile_at(3))
    tile_send(tile_at(2))

    @pl.loop(2, TILES)
    def _(n):
        tile_states(tile_at(TILES - 1 - n))
        tile_send(tile_at(TILES - 1 - n))

    recv_a[own] = send_a[own]

    def near(t):
        near_part(t, rate, res, u_ref, g_ref, wtab, vtab, htab, near_c, near_g)

    @pl.loop(0, 2)
    def _(t):
        near(t)

    block = pl.ds(pl.multiple_of(run * LANES, LANES), LANES)
    lam8 = rate[pl.ds(pl.multiple_of(seg * HALF, HALF), HALF), block] * (1.0 / SEQ)
    lam = jnp.concatenate([lam8, lam8], axis=0)
    dec = jnp.exp(-lam * float(ROWS))
    span = float(ROWS * RUN)
    dec_g = jnp.exp(-lam * span)
    ahead = jnp.exp(-lam8 * (span * z.astype(F32)))
    behind = jnp.exp(-lam8 * (span * (DEPTH - 1 - z).astype(F32)))
    decs = [jnp.ones((MODES, LANES), F32)]
    for w in range(1, RUN):
        decs.append(decs[-1] * dec)
    zero = jnp.zeros((MODES, LANES), F32)
    arrived(recv_a, GROUP - 1, ra)

    def combine(carry, part, decay, length):
        s, q, bn, tn, gr, gw, front, dist = carry
        s_j, m_j, b_j, t_j, gr_j, gw_j = part
        db = front * b_j
        return (
            decay * s + s_j,
            decay * (q + length * s) + m_j,
            bn + db,
            tn + front * t_j + dist * db,
            gr + gr_j + b_j * s,
            gw + gw_j + t_j * s + b_j * q,
            front * decay,
            dist + length,
        )

    ones = jnp.ones((MODES, LANES), F32)
    s, bn = zero, zero
    for w in range(RUN):
        pre_s[w] = s
        last = RUN - 1 - w
        pre_b[last] = bn
        s = dec * s + jnp.concatenate([recv_a[x * RUN + w].astype(F32)[0:HALF] for x in range(SEGS)], axis=0)
        near_b = [recv_a[x * RUN + last].astype(F32)[2 * HALF : 3 * HALF] for x in range(SEGS)]
        bn = dec * bn + jnp.concatenate(near_b, axis=0)
    send_m[...] = jnp.concatenate([s, bn], axis=0).astype(BF16)
    for p in layers:
        remote(send_m, recv_m.at[z], sm, rm, layer(p)).start()
    total = (zero, zero, zero, zero, zero, zero, ones, 0.0)
    for w in range(RUN):
        got = [recv_a[x * RUN + w].astype(F32) for x in range(SEGS)]
        part = [
            jnp.concatenate([rows[n * HALF : (n + 1) * HALF] for rows in got], axis=0) for n in range(6)
        ]
        total = combine(total, part, dec, float(ROWS))
    s, q, bn, tn, gr, gw = total[:6]
    early, late = slice(0, HALF), slice(HALF, MODES)
    send_x[...] = jnp.concatenate([q, tn, gr[early] + gr[late], gw[early] + gw[late]], axis=0).astype(BF16)

    for p in layers:
        remote(send_x, recv_x.at[z], sx, rx, layer(p)).start()
    recv_m[z] = send_m[...]
    recv_x[z] = send_x[...]

    @pl.loop(2, TILES)
    def _(t):
        near(t)

    arrived(recv_m, DEPTH - 1, rm)
    state, whole = zero, zero
    for p in range(DEPTH):
        s_p = recv_m[p, 0:MODES, :].astype(F32)
        state = jnp.where(p < z, dec_g * state + s_p, state)
        whole = dec_g * whole + s_p
    state = jnp.concatenate([state[:HALF], state[HALF:] + ahead * whole[:HALF]], axis=0)
    back, whole = zero, zero
    for p in reversed(range(DEPTH)):
        b_p = recv_m[p, MODES : 2 * MODES, :].astype(F32)
        back = jnp.where(p > z, dec_g * back + b_p, back)
        whole = dec_g * whole + b_p
    back = jnp.concatenate([back[:HALF] + behind * whole[HALF:], back[HALF:]], axis=0)

    for w in range(RUN):
        st = pre_s[w] + decs[w] * state
        bk = pre_b[w] + decs[RUN - 1 - w] * back
        for x in range(SEGS):
            rows = slice(x * HALF, (x + 1) * HALF)
            send_c[x * RUN + w] = jnp.concatenate([st[rows], bk[rows]], axis=0).astype(BF16)
    for j in others:
        remote(send_c.at[j], recv_c.at[own], sc, rc.at[own], member(j)).start()
    recv_c[own] = send_c[own]

    arrived(recv_x, DEPTH - 1, rx)
    total = (zero, zero, zero, zero, zero, zero, ones, 0.0)
    plain = jnp.zeros((MODES, LANES), F32)
    for p in range(DEPTH):
        states_p = recv_m[p].astype(F32)
        rest = recv_x[p].astype(F32)
        plain = plain + rest[2 * MODES : 3 * MODES]
        part = (states_p[:MODES], rest[:MODES], states_p[MODES:], rest[MODES : 2 * MODES], zero, zero)
        total = combine(total, part, dec_g, span)
    s, q, bn, tn, gr, gw = total[:6]
    gr_all = plain[early] + gr[early] + gr[late] + bn[late] * s[early]
    gw_all = plain[late] + gw[early] + gw[late] + tn[late] * s[early] + bn[late] * q[early]
    send_e[...] = jnp.concatenate([gr_all, gw_all], axis=0).astype(BF16)
    for j in others:
        remote(send_e, recv_e.at[own], se, re, member(j)).start()
    recv_e[own] = send_e[...]

    @pl.loop(0, TILES)
    def _(n):
        t = tile_at(n)
        for j in tile_owners(t):

            @pl.when(j != own)
            def _():
                remote(send_c.at[j], recv_c.at[j], sc, rc.at[j], member(j)).wait_recv()

        far_part(t, rate, res, pick, k_in, v_in, go_in, wtab, vtab, sub_s, sub_b, near_c, near_g, recv_c, gq, gk, gv)

    arrived(recv_e, GROUP - 1, re)
    scale = SEQ ** -0.5
    for w in range(RUN):
        cols = slice(w * LANES, (w + 1) * LANES)
        got = [recv_e[x * RUN + w].astype(F32) for x in range(SEGS)]
        gr, gw = [
            jnp.concatenate([rows[n * HALF : (n + 1) * HALF] for rows in got], axis=0) for n in range(2)
        ]
        gres[:, cols] = scale * gr
        grate[:, cols] = (-scale / SEQ) * res[:, cols] * gw
    departed(recv_a, GROUP - 1, sa)
    departed(recv_m, DEPTH - 1, sm)
    departed(recv_x, DEPTH - 1, sx)
    departed(recv_c, GROUP - 1, sc)
    departed(recv_e, GROUP - 1, se)


def store_kernel(*refs):
    srcs, dsts, sem = refs[:5], refs[5:10], refs[10]
    copies = [pltpu.make_async_copy(s, d, sem.at[n]) for n, (s, d) in enumerate(zip(srcs, dsts))]
    for cp in copies:
        cp.start()
    for cp in copies:
        cp.wait()


def local(query, key_in, value, grad_out, residue, rate):
    hbm = pl.BlockSpec(memory_space=pltpu.HBM)
    vmem = pl.BlockSpec(memory_space=pltpu.VMEM)
    big = jax.ShapeDtypeStruct((ROWS, CHANS), BF16)
    small = jax.ShapeDtypeStruct((MODES, CHANS), F32)
    dma = pltpu.SemaphoreType.DMA

    def buf(*shape, dtype=F32):
        return pltpu.VMEM(shape, dtype)

    held = [pltpu.VMEM((ROWS, CHANS), BF16)] * 3 + [pltpu.VMEM((MODES, CHANS), F32)] * 2
    args = [pltpu.with_memory_space_constraint(x, pltpu.HBM) for x in (query, key_in, value, grad_out, residue, rate)]
    results = pl.pallas_call(
        main_kernel,
        out_shape=held,
        in_specs=[hbm] * 6,
        out_specs=[vmem] * 5,
        scratch_shapes=[
            *[buf(ROWS, CHANS, dtype=BF16)] * 4,
            *[buf(MODES, CHANS)] * 2,
            *[buf(ROWS, CHANS, dtype=BF16)] * 2,
            *[buf(HALVES, ROWS, LANES)] * 2,
            *[buf(MODES, SUB, CHANS, dtype=BF16)] * 2,
            *[buf(SEGS, SUB // 2, 2 * HALF, CHANS, dtype=BF16)] * 2,
            buf(SUB, SUB, TILE, dtype=BF16),
            *[buf(2 * MODES, MODES * SUB, dtype=BF16)] * 3,
            *[buf(NSUB, MODES, CHANS)] * 2,
            *[buf(ROWS, CHANS)] * 2,
            *[buf(GROUP, 6 * HALF, LANES, dtype=BF16)] * 2,
            *[buf(RUN, MODES, LANES)] * 2,
            buf(2 * MODES, LANES, dtype=BF16), buf(DEPTH, 2 * MODES, LANES, dtype=BF16),
            buf(3 * MODES, LANES, dtype=BF16), buf(DEPTH, 3 * MODES, LANES, dtype=BF16),
            *[buf(GROUP, 2 * HALF, LANES, dtype=BF16)] * 2,
            buf(2 * HALF, LANES, dtype=BF16), buf(GROUP, 2 * HALF, LANES, dtype=BF16),
            dma((TILES, 4)), dma((2,)),
            dma, dma, dma, dma, dma, dma, dma, dma((GROUP,)), dma, dma,
        ],
        compiler_params=pltpu.CompilerParams(collective_id=0, has_side_effects=True, vmem_limit_bytes=VMEM_LIMIT),
        name="hyena",
    )(*args)

    return pl.pallas_call(
        store_kernel,
        out_shape=(big, big, big, small, small),
        in_specs=[vmem] * 5,
        out_specs=[hbm] * 5,
        scratch_shapes=[dma((5,))],
        compiler_params=pltpu.CompilerParams(vmem_limit_bytes=8 * 2**20),
        name="store",
    )(*[pltpu.with_memory_space_constraint(x, pltpu.VMEM) for x in results])


def solution(mesh):
    big, small = P("ctx", "tp"), P(None, "tp")
    return jax.shard_map(
        local, mesh=mesh, in_specs=(big, big, big, big, small, small),
        out_specs=(big, big, big, small, small), check_vma=False,
    )
```
